32 devices in a mesh: dp: 4 (over y, core), row: 2 (over x), col: 4 (over z).
Axes of the slice: x: 2, y: 2, z: 4, core: 2. Of those that a mesh axis runs over, the one named last changes fastest.
Arguments:
- tokens: bfloat16 [16384, 2048], P(('dp', 'col'), 'row'), may hold values from -6 to 6
- cotangent: bfloat16 [16384, 2048], P(('dp', 'col'), 'row')
- prefix: int32 [8], P('dp'), may hold values from 204 to 1024
- query_weight: float32 [2048, 2048], P('row', 'col'), may hold values from -0.5 to 0.5
- key_projection: float32 [2048, 512], P('row'), may hold values from -0.5 to 0.5
- value_projection: float32 [2048, 512], P('row'), may hold values from -0.125 to 0.125
- out_weight: float32 [2048, 2048], P('col', 'row'), may hold values from -1.5 to 1.5
- gate_weight: float32 [2048, 8192], P('row', 'col'), may hold values from -0.125 to 0.125
- up_weight: float32 [2048, 8192], P('row', 'col'), may hold values from -0.125 to 0.125
- down_weight: float32 [8192, 2048], P('col', 'row'), may hold values from -0.375 to 0.375
- norm_gains: float32 [2, 2048], P(None, 'row')
- query_moment: float32 [2048, 2048], P('row', 'col'), may hold values from -0.0005128985 to 0.0005128985
- key_first_moment: float32 [2048, 512], P('row'), may hold values from -0.0005128985 to 0.0005128985
- value_first_moment: float32 [2048, 512], P('row'), may hold values from -0.0005128985 to 0.0005128985
- out_moment: float32 [2048, 2048], P('col', 'row'), may hold values from -0.00012822462 to 0.00012822462
- gate_moment: float32 [2048, 8192], P('row', 'col'), may hold values from -0.0005128985 to 0.0005128985
- up_moment: float32 [2048, 8192], P('row', 'col'), may hold values from -0.0005128985 to 0.0005128985
- down_moment: float32 [8192, 2048], P('col', 'row'), may hold values from -0.00017951446 to 0.00017951446
- gains_moment: float32 [2, 2048], P(None, 'row'), may hold values from -0.0005128985 to 0.0005128985
- query_square: float32 [2048, 2048], P('row', 'col'), may hold values from 1.6441554e-08 to 6.5766216e-08
- key_second_moment: float32 [2048, 512], P('row'), may hold values from 1.6441554e-08 to 6.5766216e-08
- value_second_moment: float32 [2048, 512], P('row'), may hold values from 1.6441554e-08 to 6.5766216e-08
- out_square: float32 [2048, 2048], P('col', 'row'), may hold values from 4.932466e-10 to 1.9729864e-09
- gate_square: float32 [2048, 8192], P('row', 'col'), may hold values from 1.6441554e-08 to 6.5766216e-08
- up_square: float32 [2048, 8192], P('row', 'col'), may hold values from 1.6441554e-08 to 6.5766216e-08
- down_square: float32 [8192, 2048], P('col', 'row'), may hold values from 9.864932e-10 to 3.945973e-09
- gains_square: float32 [2, 2048], P(None, 'row'), may hold values from 1.6441554e-08 to 6.5766216e-08
Outputs:
- layer_out: bfloat16 [16384, 2048], P(('dp', 'col'), 'row')
- input_grad: bfloat16 [16384, 2048], P(('dp', 'col'), 'row')
- query_grad: float32 [2048, 2048], P('row', 'col')
- key_grad: float32 [2048, 512], P('row')
- value_grad: float32 [2048, 512], P('row')
- out_grad: float32 [2048, 2048], P('col', 'row')
- gate_grad: float32 [2048, 8192], P('row', 'col')
- up_grad: float32 [2048, 8192], P('row', 'col')
- down_grad: float32 [8192, 2048], P('col', 'row')
- gains_grad: float32 [2, 2048], P(None, 'row')
- query_next: float32 [2048, 2048], P('row', 'col')
- key_next: float32 [2048, 512], P('row')
- value_next: float32 [2048, 512], P('row')
- out_next: float32 [2048, 2048], P('col', 'row')
- gate_next: float32 [2048, 8192], P('row', 'col')
- up_next: float32 [2048, 8192], P('row', 'col')
- down_next: float32 [8192, 2048], P('col', 'row')
- gains_next: float32 [2, 2048], P(None, 'row')
- query_variance: float32 [2048, 2048], P('row', 'col')
- key_variance: float32 [2048, 512], P('row')
- value_variance: float32 [2048, 512], P('row')
- out_variance: float32 [2048, 2048], P('col', 'row')
- gate_variance: float32 [2048, 8192], P('row', 'col')
- up_variance: float32 [2048, 8192], P('row', 'col')
- down_variance: float32 [8192, 2048], P('col', 'row')
- gains_variance: float32 [2, 2048], P(None, 'row')
- grad_norm: float32 [], replicated
The draws below stay inside these ranges and needn't reach their ends.
Inputs may be any that keep to these rules, and one draw needn't show every extreme that they name: prefix[s] leading tokens of sequence s are visible to every token of that sequence.
All inputs are finite; a program needn't handle non-finite values.
Results may differ from the reference program's by a relative error of at most 0.025.
The reference program's roundings to bfloat16 on the way count: a program that leaves them out, or rounds other values in their place, can miss the bound.
Values may be sent and summed in bfloat16 or wider, within the bound.
No kernel may reach another device: no remote copies, remote signals or barrier semaphores. Data moves between devices by JAX's collectives and lax.ppermute only.
A program may use at most 576 MiB of HBM per device.

```python
import math
import jax
import jax.numpy as jnp
from jax import lax

MODEL_WIDTH = 2048
QUERY_HEADS = 32
KEY_VALUE_HEADS = 8
HEAD_SIZE = 64
FF = 8192
SEQUENCE_LENGTH = 2048
STEP = 5
SEQS = 8
TOKENS = 16384
PARAMETER_COUNT = 60821504


def draw_cotangent(key, part):
    key = jax.random.fold_in(key, 11)
    rows = jnp.arange(TOKENS, dtype=jnp.float32)[:, None] / TOKENS
    cols = jnp.arange(MODEL_WIDTH, dtype=jnp.float32)[None, :] / MODEL_WIDTH
    base = jnp.clip(jax.random.normal(key, (TOKENS, MODEL_WIDTH), jnp.float32), -5.0, 5.0)
    return (base * (0.6 + 1.2 * rows) * (0.6 + 1.2 * cols)).astype(jnp.bfloat16)


def draw_norm_gains(key, part):
    key = jax.random.fold_in(key, 23)
    cols = jnp.arange(MODEL_WIDTH, dtype=jnp.float32)[None, :] / MODEL_WIDTH
    noise = 1.0 + 0.05 * jnp.clip(jax.random.normal(key, (2, MODEL_WIDTH), jnp.float32), -3.0, 3.0)
    return noise * (0.6 + 1.2 * cols)


def touch_ends(values, rng, least, high):
    place = [jax.random.randint(jax.random.fold_in(rng, axis), (), 0, length) for axis, length in enumerate(values.shape)]
    main_axis = values.shape.index(max(values.shape))
    beside = place[:main_axis] + [(place[main_axis] + 1) % values.shape[main_axis]] + place[main_axis + 1:]
    return values.at[tuple(place)].set(least).at[tuple(beside)].set(high)


def level_of(stream_key, shape, split, low, largest):
    gain = 1.0
    for axis_at, shards_of in split:
        steps = jax.random.uniform(jax.random.fold_in(jax.random.fold_in(stream_key, 6), axis_at), (shards_of,), jnp.float32, low / len(split), largest / len(split))
        gain = gain * jnp.repeat(jnp.exp(steps), shape[axis_at] // shards_of).reshape((-1,) + (1,) * (len(shape) - 1 - axis_at))
    return gain


def scatter_about(key, shape, spread, limit, pieces=(), kind=jnp.bfloat16):
    entries = jax.random.normal(key, shape, jnp.float32) * spread
    if len(pieces) > 0:
        entries = level_of(key, shape, pieces, -0.22, 0.18) * entries
    return jnp.clip(entries, min=-limit, max=limit).astype(kind)


def setup_inputs(seed: int = 0) -> dict:
    seeds = jax.random.split(jax.random.key(seed), 28)
    return {
        "tokens": scatter_about(seeds[0], (TOKENS, MODEL_WIDTH), 1.0, 6.0, ((0, 16), (1, 2))),
        "cotangent": draw_cotangent(jax.random.fold_in(seeds[27], 71), 0),
        "prefix": touch_ends(jax.random.randint(seeds[2], (SEQS,), SEQUENCE_LENGTH // 10, SEQUENCE_LENGTH // 2 + 1), jax.random.fold_in(seeds[2], 1), SEQUENCE_LENGTH // 10, (SEQUENCE_LENGTH // 2 + 1) - 1).astype(jnp.int32),
        "query_weight": scatter_about(seeds[3], (MODEL_WIDTH, QUERY_HEADS * HEAD_SIZE), (MODEL_WIDTH // 16) ** -0.5, 0.5, ((0, 2), (1, 4)), jnp.float32),
        "key_projection": scatter_about(seeds[4], (MODEL_WIDTH, KEY_VALUE_HEADS * HEAD_SIZE), (MODEL_WIDTH // 16) ** -0.5, 0.5, ((0, 2),), jnp.float32),
        "value_projection": scatter_about(seeds[5], (MODEL_WIDTH, KEY_VALUE_HEADS * HEAD_SIZE), MODEL_WIDTH ** -0.5, 0.125, ((0, 2),), jnp.float32),
        "out_weight": scatter_about(seeds[6], (QUERY_HEADS * HEAD_SIZE, MODEL_WIDTH), (QUERY_HEADS * HEAD_SIZE // 128) ** -0.5, 1.5, ((0, 4), (1, 2)), jnp.float32),
        "gate_weight": scatter_about(seeds[7], (MODEL_WIDTH, FF), MODEL_WIDTH ** -0.5, 0.125, ((0, 2), (1, 4)), jnp.float32),
        "up_weight": scatter_about(seeds[8], (MODEL_WIDTH, FF), MODEL_WIDTH ** -0.5, 0.125, ((0, 2), (1, 4)), jnp.float32),
        "down_weight": scatter_about(seeds[9], (FF, MODEL_WIDTH), (FF // 32) ** -0.5, 0.375, ((0, 4), (1, 2)), jnp.float32),
        "norm_gains": draw_norm_gains(jax.random.fold_in(seeds[27], 71), 0),
        "query_moment": scatter_about(seeds[11], (MODEL_WIDTH, QUERY_HEADS * HEAD_SIZE), (PARAMETER_COUNT ** -0.5), 0.0005128985, ((0, 2), (1, 4)), jnp.float32),
        "key_first_moment": scatter_about(seeds[12], (MODEL_WIDTH, KEY_VALUE_HEADS * HEAD_SIZE), (PARAMETER_COUNT ** -0.5), 0.0005128985, ((0, 2),), jnp.float32),
        "value_first_moment": scatter_about(seeds[13], (MODEL_WIDTH, KEY_VALUE_HEADS * HEAD_SIZE), (PARAMETER_COUNT ** -0.5), 0.0005128985, ((0, 2),), jnp.float32),
        "out_moment": scatter_about(seeds[14], (QUERY_HEADS * HEAD_SIZE, MODEL_WIDTH), (0.25 * PARAMETER_COUNT ** -0.5), 0.00012822462, ((0, 4), (1, 2)), jnp.float32),
        "gate_moment": scatter_about(seeds[15], (MODEL_WIDTH, FF), (PARAMETER_COUNT ** -0.5), 0.0005128985, ((0, 2), (1, 4)), jnp.float32),
        "up_moment": scatter_about(seeds[16], (MODEL_WIDTH, FF), (PARAMETER_COUNT ** -0.5), 0.0005128985, ((0, 2), (1, 4)), jnp.float32),
        "down_moment": scatter_about(seeds[17], (FF, MODEL_WIDTH), (0.35 * PARAMETER_COUNT ** -0.5), 0.00017951446, ((0, 4), (1, 2)), jnp.float32),
        "gains_moment": scatter_about(seeds[18], (2, MODEL_WIDTH), (PARAMETER_COUNT ** -0.5), 0.0005128985, ((1, 2),), jnp.float32),
        "query_square": jnp.clip(jnp.exp(math.log(6.576621558451734e-08) - 1.3862944 * jax.random.uniform(seeds[19], (MODEL_WIDTH, QUERY_HEADS * HEAD_SIZE), jnp.float32) ** level_of(seeds[19], (MODEL_WIDTH, QUERY_HEADS * HEAD_SIZE), ((0, 2), (1, 4)), -0.2, 0.2)), 1.6441553896129335e-08, 6.576621558451734e-08),
        "key_second_moment": jnp.clip(jnp.exp(math.log(6.576621558451734e-08) - 1.3862944 * jax.random.uniform(seeds[20], (MODEL_WIDTH, KEY_VALUE_HEADS * HEAD_SIZE), jnp.float32) ** level_of(seeds[20], (MODEL_WIDTH, KEY_VALUE_HEADS * HEAD_SIZE), ((0, 2),), -0.2, 0.2)), 1.6441553896129335e-08, 6.576621558451734e-08),
        "value_second_moment": jnp.clip(jnp.exp(math.log(6.576621558451734e-08) - 1.3862944 * jax.random.uniform(seeds[21], (MODEL_WIDTH, KEY_VALUE_HEADS * HEAD_SIZE), jnp.float32) ** level_of(seeds[21], (MODEL_WIDTH, KEY_VALUE_HEADS * HEAD_SIZE), ((0, 2),), -0.2, 0.2)), 1.6441553896129335e-08, 6.576621558451734e-08),
        "out_square": jnp.clip(jnp.exp(math.log(1.9729864408901676e-09) - 1.3862944 * jax.random.uniform(seeds[22], (QUERY_HEADS * HEAD_SIZE, MODEL_WIDTH), jnp.float32) ** level_of(seeds[22], (QUERY_HEADS * HEAD_SIZE, MODEL_WIDTH), ((0, 4), (1, 2)), -0.2, 0.2)), 4.932466102225419e-10, 1.9729864408901676e-09),
        "gate_square": jnp.clip(jnp.exp(math.log(6.576621558451734e-08) - 1.3862944 * jax.random.uniform(seeds[23], (MODEL_WIDTH, FF), jnp.float32) ** level_of(seeds[23], (MODEL_WIDTH, FF), ((0, 2), (1, 4)), -0.2, 0.2)), 1.6441553896129335e-08, 6.576621558451734e-08),
        "up_square": jnp.clip(jnp.exp(math.log(6.576621558451734e-08) - 1.3862944 * jax.random.uniform(seeds[24], (MODEL_WIDTH, FF), jnp.float32) ** level_of(seeds[24], (MODEL_WIDTH, FF), ((0, 2), (1, 4)), -0.2, 0.2)), 1.6441553896129335e-08, 6.576621558451734e-08),
        "down_square": jnp.clip(jnp.exp(math.log(3.945972881780335e-09) - 1.3862944 * jax.random.uniform(seeds[25], (FF, MODEL_WIDTH), jnp.float32) ** level_of(seeds[25], (FF, MODEL_WIDTH), ((0, 4), (1, 2)), -0.2, 0.2)), 9.864932204450838e-10, 3.945972881780335e-09),
        "gains_square": jnp.clip(jnp.exp(math.log(6.576621558451734e-08) - 1.3862944 * jax.random.uniform(seeds[26], (2, MODEL_WIDTH), jnp.float32) ** level_of(seeds[26], (2, MODEL_WIDTH), ((1, 2),), -0.2, 0.2)), 1.6441553896129335e-08, 6.576621558451734e-08),
    }


EPS_NORM = 1e-05
RESID = 0.22
ATTN_SCALE = 1.0 / 64.0
THETA = 10000000.0
LEARN = 0.1
GAINS_LEARN = 0.5
BETA_ONE = 0.5
BETA_TWO = 0.5
ADAM_EPS = 1e-08
DECAY = 0.1
CLIP = 1.0

@jax.custom_vjp
def low(v):
    return lax.optimization_barrier(v.astype(jnp.bfloat16)).astype(jnp.float32)

@jax.custom_vjp
def low_back(v):
    return v

def low_keep(v):
    return (low(v), None)

def low_pass(kept, grad):
    return (grad,)

def back_keep(v):
    return (v, None)

def back_low(kept, grad):
    return (low(grad),)
low.defvjp(low_keep, low_pass)
low_back.defvjp(back_keep, back_low)

def matrix_multiply(left_side, right_side):
    return jnp.dot(left_side, right_side, precision=lax.Precision.HIGHEST, preferred_element_type=jnp.float32)

def rope_tables(length):
    half_width = HEAD_SIZE // 2
    frequency = THETA ** (-(jnp.arange(half_width, dtype=jnp.float32) * 2.0 / HEAD_SIZE))
    angles = jnp.arange(length, dtype=jnp.float32)[:, None] * frequency[None, :]
    angles = jnp.concatenate([angles, angles], axis=1)
    return (jnp.cos(angles), jnp.sin(angles))

def rotate(values):
    half_width = values.shape[-1] // 2
    return jnp.concatenate([-values[..., half_width:], values[..., :half_width]], axis=-1)

def rope(values, cosine_table, sine_table):
    return values * cosine_table[:, None, :] + rotate(values) * sine_table[:, None, :]

def rms_norm(values, gain_row):
    mean_square = lax.optimization_barrier(jnp.mean(values * values, axis=-1, keepdims=True))
    return low(values * lax.rsqrt(mean_square + EPS_NORM) * gain_row)

def attend_block(query_block, heads_of_keys, heads_of_values, positions, prefix_length):
    scores = low_back(jnp.einsum('qhgd,khd->hgqk', query_block, heads_of_keys, precision=lax.Precision.HIGHEST))
    key_place = jnp.arange(SEQUENCE_LENGTH)
    visible = (key_place[None, :] <= positions[:, None]) | (key_place[None, :] < prefix_length)
    scores = jnp.where(visible, scores, -1e+30)
    row_max = lax.optimization_barrier(jnp.max(scores, axis=-1, keepdims=True))
    exponent = jnp.exp(scores - row_max)
    probability = exponent / lax.optimization_barrier(jnp.sum(exponent, axis=-1, keepdims=True))
    return jnp.einsum('hgqk,khd->qhgd', low(probability), heads_of_values, precision=lax.Precision.HIGHEST)

def layer_sequence(inputs, weights, cosine_table, sine_table):
    values_in, prefix_length = inputs
    query_w, key_matrix, value_matrix, out_w, gate_w, up_w, down_w, gain_one, gain_two = weights
    group_width = QUERY_HEADS // KEY_VALUE_HEADS
    rows_per_block = min(512, SEQUENCE_LENGTH)
    hidden_first = rms_norm(values_in, gain_one)
    heads_of_queries = low_back(matrix_multiply(hidden_first, query_w)).reshape(SEQUENCE_LENGTH, QUERY_HEADS, HEAD_SIZE)
    heads_of_keys = low_back(matrix_multiply(hidden_first, key_matrix)).reshape(SEQUENCE_LENGTH, KEY_VALUE_HEADS, HEAD_SIZE)
    heads_of_values = low(low_back(matrix_multiply(hidden_first, value_matrix))).reshape(SEQUENCE_LENGTH, KEY_VALUE_HEADS, HEAD_SIZE)
    heads_of_queries = low(rope(heads_of_queries, cosine_table, sine_table) * ATTN_SCALE)
    heads_of_queries = heads_of_queries.reshape(SEQUENCE_LENGTH // rows_per_block, rows_per_block, KEY_VALUE_HEADS, group_width, HEAD_SIZE)
    heads_of_keys = low(rope(heads_of_keys, cosine_table, sine_table))
    positions = jnp.arange(SEQUENCE_LENGTH).reshape(SEQUENCE_LENGTH // rows_per_block, rows_per_block)
    attend = jax.checkpoint(lambda block_inputs: attend_block(block_inputs[0], heads_of_keys, heads_of_values, block_inputs[1], prefix_length))
    head_out = lax.map(attend, (heads_of_queries, positions))
    head_out = low(low_back(head_out.reshape(SEQUENCE_LENGTH, QUERY_HEADS * HEAD_SIZE)))
    attended = low_back(matrix_multiply(head_out, out_w))
    residual_mid = values_in + RESID * attended
    h_two = rms_norm(residual_mid, gain_two)
    gate_value = low_back(matrix_multiply(h_two, gate_w))
    up_value = low_back(matrix_multiply(h_two, up_w))
    hidden = low(jax.nn.silu(gate_value) * up_value)
    return residual_mid + RESID * low_back(matrix_multiply(hidden, down_w))

def adam(weight, gradient, moment_one, moment_two, decay_rate, learn_rate):
    moment_new = BETA_ONE * moment_one + (1.0 - BETA_ONE) * gradient
    square_new = BETA_TWO * moment_two + (1.0 - BETA_TWO) * gradient * gradient
    moment_hat = moment_new / (1.0 - BETA_ONE ** STEP)
    square_hat = square_new / (1.0 - BETA_TWO ** STEP)
    return (weight - learn_rate * (moment_hat / (jnp.sqrt(square_hat) + ADAM_EPS) + decay_rate * weight), square_new)

def reference(tokens, cotangent, prefix, query_weight, key_projection, value_projection, out_weight, gate_weight, up_weight, down_weight, norm_gains, query_moment, key_first_moment, value_first_moment, out_moment, gate_moment, up_moment, down_moment, gains_moment, query_square, key_second_moment, value_second_moment, out_square, gate_square, up_square, down_square, gains_square):
    cosine_table, sine_table = rope_tables(SEQUENCE_LENGTH)
    masters = (query_weight, key_projection, value_projection, out_weight, gate_weight, up_weight, down_weight)
    moments = (query_moment, key_first_moment, value_first_moment, out_moment, gate_moment, up_moment, down_moment)
    squares = (query_square, key_second_moment, value_second_moment, out_square, gate_square, up_square, down_square)

    def forward(inputs, weights, gains_all):
        rounded = tuple((low(weight) for weight in weights)) + (gains_all[0], gains_all[1])
        shaped = inputs.reshape(SEQS, SEQUENCE_LENGTH, MODEL_WIDTH)
        one_sequence = jax.checkpoint(lambda seq_inputs: layer_sequence(seq_inputs, rounded, cosine_table, sine_table))
        return lax.map(one_sequence, (shaped, prefix)).reshape(TOKENS, MODEL_WIDTH)
    output, pullback = jax.vjp(forward, tokens.astype(jnp.float32), masters, norm_gains)
    input_grad, weight_grads, gains_raw = pullback(cotangent.astype(jnp.float32))
    total_sum = jnp.sum(gains_raw * gains_raw)
    for gradient in weight_grads:
        total_sum = total_sum + jnp.sum(gradient * gradient)
    grad_norm = jnp.sqrt(total_sum)
    factor = jnp.minimum(1.0, CLIP / grad_norm)
    clipped = []
    nexts = []
    variances = []
    for position in range(7):
        gradient = weight_grads[position] * factor
        weight_next, variance = adam(masters[position], gradient, moments[position], squares[position], DECAY, LEARN)
        clipped.append(gradient)
        nexts.append(weight_next)
        variances.append(variance)
    gains_grad = gains_raw * factor
    gains_next, gains_variance = adam(norm_gains, gains_grad, gains_moment, gains_square, 0.0, GAINS_LEARN)
    return (output.astype(jnp.bfloat16), input_grad.astype(jnp.bfloat16), clipped[0], clipped[1], clipped[2], clipped[3], clipped[4], clipped[5], clipped[6], gains_grad, nexts[0], nexts[1], nexts[2], nexts[3], nexts[4], nexts[5], nexts[6], gains_next, variances[0], variances[1], variances[2], variances[3], variances[4], variances[5], variances[6], gains_variance, grad_norm)
```

```python
import functools

import jax
import jax.numpy as jnp
from jax import lax
from jax.experimental import pallas as pl
from jax.experimental.pallas import tpu as pltpu
from jax.sharding import PartitionSpec as P

MODEL_WIDTH = 2048
QUERY_HEADS = 32
KEY_VALUE_HEADS = 8
HEAD_SIZE = 64
SEQUENCE_LENGTH = 2048
STEP = 5


EPS_NORM = 1e-05
RESID = 0.22
ATTN_SCALE = 1.0 / 64.0
THETA = 10000000.0
LEARN = 0.1
GAINS_LEARN = 0.5
BETA_ONE = 0.5
BETA_TWO = 0.5
ADAM_EPS = 1e-08
DECAY = 0.1
CLIP = 1.0


def matrix_multiply(left_side, right_side):
    return jnp.dot(left_side, right_side, preferred_element_type=jnp.float32)


def left_product(left_side, right_side):
    return lax.dot_general(
        left_side, right_side, (((0,), (0,)), ((), ())), preferred_element_type=jnp.float32
    )


def right_product(left_side, right_side):
    return lax.dot_general(
        left_side, right_side, (((1,), (1,)), ((), ())), preferred_element_type=jnp.float32
    )


def width_total(values):
    return lax.psum(values, "row")


def gather_tokens(values):
    return lax.all_gather(values, "col", axis=0, tiled=True)


def sum_tokens(term, tok_rows):
    return lax.psum_scatter(
        term(jnp.int32(0), lax.axis_size("col") * tok_rows).astype(jnp.bfloat16),
        "col",
        scatter_dimension=0,
        tiled=True,
    ).astype(jnp.float32)


def fetch_weights(first, second, third, fourth, fifth):
    return (
        lax.all_gather(first, "row", axis=0, tiled=True),
        lax.all_gather(second, "row", axis=0, tiled=True),
        lax.all_gather(third, "row", axis=0, tiled=True),
        lax.all_gather(fourth, "row", axis=1, tiled=True),
        lax.all_gather(fifth, "row", axis=1, tiled=True),
    )


def enter_rows(values):
    return lax.all_to_all(values, "row", split_axis=0, concat_axis=1, tiled=True)


def leave_rows(values):
    return lax.all_to_all(
        values.astype(jnp.bfloat16), "row", split_axis=1, concat_axis=0, tiled=True
    ).astype(values.dtype)


def reduce_rows(first, second, third, fourth, fifth):
    return (
        lax.psum_scatter(first.astype(jnp.bfloat16), "row", scatter_dimension=0, tiled=True).astype(
            jnp.float32
        ),
        lax.psum_scatter(
            second.astype(jnp.bfloat16), "row", scatter_dimension=0, tiled=True
        ).astype(jnp.float32),
        lax.psum_scatter(third.astype(jnp.bfloat16), "row", scatter_dimension=1, tiled=True).astype(
            jnp.float32
        ),
        lax.psum_scatter(
            fourth.astype(jnp.bfloat16), "row", scatter_dimension=0, tiled=True
        ).astype(jnp.float32),
        lax.psum_scatter(fifth.astype(jnp.bfloat16), "row", scatter_dimension=1, tiled=True).astype(
            jnp.float32
        ),
    )


def rope_tables(length):
    half_width = HEAD_SIZE // 2
    frequency = THETA ** (-(jnp.arange(half_width, dtype=jnp.float32) * 2.0 / HEAD_SIZE))
    angles = jnp.arange(length, dtype=jnp.float32)[:, None] * frequency[None, :]
    angles = jnp.concatenate([angles, angles], axis=1)
    return (jnp.cos(angles), jnp.sin(angles))


def rotate(values):
    half_width = values.shape[-1] // 2
    return jnp.concatenate([-values[..., half_width:], values[..., :half_width]], axis=-1)


def rope(values, cosine_table, sine_table):
    return values * cosine_table[:, None, :] + rotate(values) * sine_table[:, None, :]


def rope_back(gradient, cosine_table, sine_table):
    return gradient * cosine_table[:, None, :] - rotate(gradient * sine_table[:, None, :])


def rms_forward(values, gain_row):
    squares = width_total(jnp.sum(values * values, axis=1))
    factor = lax.rsqrt(squares[:, None] / MODEL_WIDTH + EPS_NORM)
    normed = values * factor
    return ((normed * gain_row).astype(jnp.bfloat16), normed, factor)


def rms_backward(grad_normed, normed, factor, gain_row):
    weighted = grad_normed * gain_row
    inner_sum = width_total(jnp.sum(weighted * normed, axis=1))
    grad_input = factor * (weighted - normed * (inner_sum[:, None] / MODEL_WIDTH))
    return (grad_input, jnp.sum(grad_normed * normed, axis=0))


def attend_sequence(
    heads_of_queries, heads_of_keys, heads_of_values, prefix_length, rows_per_block
):
    length = heads_of_keys.shape[0]
    key_place = jnp.arange(length)

    def one_block(inputs):
        query_block, positions = inputs
        scores = jnp.einsum(
            "qhgd,khd->hgqk", query_block, heads_of_keys, preferred_element_type=jnp.float32
        )
        visible = (key_place[None, :] <= positions[:, None]) | (key_place[None, :] < prefix_length)
        scores = jnp.where(visible, scores, -1e30)
        row_max = jnp.max(scores, axis=-1, keepdims=True)
        exponent = jnp.exp(scores - row_max)
        total_sum = jnp.sum(exponent, axis=-1, keepdims=True)
        probability = (exponent / total_sum).astype(jnp.bfloat16)
        result = jnp.einsum(
            "hgqk,khd->qhgd", probability, heads_of_values, preferred_element_type=jnp.float32
        )
        return (result, row_max[..., 0] + jnp.log(total_sum[..., 0]))

    block_count = length // rows_per_block
    shaped = heads_of_queries.reshape((block_count, rows_per_block) + heads_of_queries.shape[1:])
    positions = jnp.arange(length).reshape(block_count, rows_per_block)
    result, logsum = lax.map(one_block, (shaped, positions))
    return (result.reshape(heads_of_queries.shape), logsum)


def attend_back(
    heads_of_queries,
    heads_of_keys,
    heads_of_values,
    prefix_length,
    logsum,
    grad_heads,
    rows_per_block,
):
    length = heads_of_keys.shape[0]
    key_place = jnp.arange(length)
    block_count = length // rows_per_block

    def one_block(carried, inputs):
        query_block, grad_block, logsum_block, positions = inputs
        scores = jnp.einsum(
            "qhgd,khd->hgqk", query_block, heads_of_keys, preferred_element_type=jnp.float32
        )
        visible = (key_place[None, :] <= positions[:, None]) | (key_place[None, :] < prefix_length)
        scores = jnp.where(visible, scores, -1e30)
        probability = jnp.exp(scores - logsum_block[..., None])
        grad_prob = jnp.einsum(
            "qhgd,khd->hgqk", grad_block, heads_of_values, preferred_element_type=jnp.float32
        )
        delta_sum = jnp.sum(probability * grad_prob, axis=-1, keepdims=True)
        grad_scores = (probability * (grad_prob - delta_sum)).astype(jnp.bfloat16)
        grad_query = jnp.einsum(
            "hgqk,khd->qhgd", grad_scores, heads_of_keys, preferred_element_type=jnp.float32
        )
        grad_keys = jnp.einsum(
            "hgqk,qhgd->khd", grad_scores, query_block, preferred_element_type=jnp.float32
        )
        grad_values = jnp.einsum(
            "hgqk,qhgd->khd",
            probability.astype(jnp.bfloat16),
            grad_block,
            preferred_element_type=jnp.float32,
        )
        return ((carried[0] + grad_keys, carried[1] + grad_values), grad_query)

    block_shape = (block_count, rows_per_block) + heads_of_queries.shape[1:]
    initial = (
        jnp.zeros(heads_of_keys.shape, jnp.float32),
        jnp.zeros(heads_of_values.shape, jnp.float32),
    )
    positions = jnp.arange(length).reshape(block_count, rows_per_block)
    inputs = (
        heads_of_queries.reshape(block_shape),
        grad_heads.reshape(block_shape),
        logsum,
        positions,
    )
    (grad_keys, grad_values), grad_query = lax.scan(one_block, initial, inputs)
    return (grad_query.reshape(heads_of_queries.shape), grad_keys, grad_values)


def adam(weight, gradient, moment_one, moment_two, decay_rate, learn_rate):
    moment_new = BETA_ONE * moment_one + (1.0 - BETA_ONE) * gradient
    square_new = BETA_TWO * moment_two + (1.0 - BETA_TWO) * gradient * gradient
    moment_hat = moment_new / (1.0 - BETA_ONE**STEP)
    square_hat = square_new / (1.0 - BETA_TWO**STEP)
    return (
        weight
        - learn_rate * (moment_hat / (jnp.sqrt(square_hat) + ADAM_EPS) + decay_rate * weight),
        square_new,
    )


def shards(
    tokens,
    cotangent,
    prefix,
    query_weight,
    key_projection,
    value_projection,
    out_weight,
    gate_weight,
    up_weight,
    down_weight,
    norm_gains,
    query_moment,
    key_first_moment,
    value_first_moment,
    out_moment,
    gate_moment,
    up_moment,
    down_moment,
    gains_moment,
    query_square,
    key_second_moment,
    value_second_moment,
    out_square,
    gate_square,
    up_square,
    down_square,
    gains_square,
):
    tok_rows = tokens.shape[0]
    query_cols = query_weight.shape[1]
    kv_all = key_projection.shape[1]
    ffn_cols = gate_weight.shape[1]
    row_size = lax.axis_size("row")
    col_size = lax.axis_size("col")
    row_index = lax.axis_index("row")
    col_index = lax.axis_index("col")
    tok_count = tok_rows * col_size
    seq_count = prefix.shape[0]
    group_width = QUERY_HEADS // KEY_VALUE_HEADS
    rows_per_block = min(512, SEQUENCE_LENGTH)
    col_heads = query_cols // HEAD_SIZE
    frame_used = max(1, col_heads // group_width)
    frame_start = col_index * col_heads // group_width
    frame_width = frame_used * HEAD_SIZE
    key_here = lax.dynamic_slice_in_dim(key_projection, frame_start * HEAD_SIZE, frame_width, 1)
    value_here = lax.dynamic_slice_in_dim(value_projection, frame_start * HEAD_SIZE, frame_width, 1)
    query_mat = query_weight.astype(jnp.bfloat16)
    kv_mat = (
        jnp.stack([key_here, value_here], axis=1)
        .astype(jnp.bfloat16)
        .reshape(key_here.shape[0], 2 * frame_width)
    )
    out_mat = out_weight.astype(jnp.bfloat16)
    ffn_mat = (
        jnp.stack([gate_weight, up_weight], axis=1)
        .astype(jnp.bfloat16)
        .reshape(gate_weight.shape[0], 2 * ffn_cols)
    )
    down_mat = down_weight.astype(jnp.bfloat16)
    gain_one = norm_gains[0]
    gain_two = norm_gains[1]
    query_use, kv_use, ffn_use, out_use, down_use = fetch_weights(
        query_mat, kv_mat, ffn_mat, out_mat, down_mat
    )
    use_rows = tok_count // row_size
    seq_use = seq_count // row_size
    prefix_use = lax.dynamic_slice_in_dim(prefix, row_index * seq_use, seq_use, 0)
    kv_used = max(1, col_heads // group_width)
    group_here = col_heads // kv_used
    cosine_one, sine_one = rope_tables(SEQUENCE_LENGTH)
    cosine_table = jnp.tile(cosine_one, (seq_use, 1))
    sine_table = jnp.tile(sine_one, (seq_use, 1))

    def spread(values):
        return enter_rows(values)

    def to_tokens(product_fn):
        whole = leave_rows(product_fn(0, use_rows))

        def term(start_row, rows_here):
            return whole

        return sum_tokens(term, tok_rows)

    input_float = tokens.astype(jnp.float32)
    hidden_first, normed_one, factor_one = rms_forward(input_float, gain_one)
    h_one_use = spread(gather_tokens(hidden_first))
    query_sum = matrix_multiply(h_one_use, query_use)
    kv_frame = matrix_multiply(h_one_use, kv_use).reshape(use_rows, 2, frame_width)
    query_round = (
        rope(query_sum.reshape(use_rows, col_heads, HEAD_SIZE), cosine_table, sine_table)
        * ATTN_SCALE
    ).astype(jnp.bfloat16)
    key_round = rope(
        kv_frame[:, 0].reshape(use_rows, kv_used, HEAD_SIZE), cosine_table, sine_table
    ).astype(jnp.bfloat16)
    value_round = kv_frame[:, 1].reshape(use_rows, kv_used, HEAD_SIZE).astype(jnp.bfloat16)
    query_seq = query_round.reshape(seq_use, SEQUENCE_LENGTH, kv_used, group_here, HEAD_SIZE)
    key_seq = key_round.reshape(seq_use, SEQUENCE_LENGTH, kv_used, HEAD_SIZE)
    value_seq = value_round.reshape(seq_use, SEQUENCE_LENGTH, kv_used, HEAD_SIZE)

    def forward_sequence(inputs):
        return attend_sequence(inputs[0], inputs[1], inputs[2], inputs[3], rows_per_block)

    attended, logsum = lax.map(forward_sequence, (query_seq, key_seq, value_seq, prefix_use))
    head_round = attended.reshape(use_rows, col_heads * HEAD_SIZE).astype(jnp.bfloat16)

    def out_term(start_row, rows_here):
        return matrix_multiply(head_round, out_use)

    residual_mid = input_float + RESID * to_tokens(out_term)
    h_two, normed_two, factor_two = rms_forward(residual_mid, gain_two)
    h_two_use = spread(gather_tokens(h_two))
    ffn_part = matrix_multiply(h_two_use, ffn_use).reshape(use_rows, 2, ffn_cols)
    gate_value = ffn_part[:, 0]
    up_value = ffn_part[:, 1]
    hidden = (jax.nn.silu(gate_value) * up_value).astype(jnp.bfloat16)

    def down_term(start_row, rows_here):
        return matrix_multiply(hidden, down_use)

    layer_out = (residual_mid + RESID * to_tokens(down_term)).astype(jnp.bfloat16)
    grad_output = cotangent.astype(jnp.float32)
    grad_mlp = (RESID * grad_output).astype(jnp.bfloat16)
    grad_mlp_use = spread(gather_tokens(grad_mlp))
    down_local = left_product(hidden, grad_mlp_use)
    hidden_part = right_product(grad_mlp_use, down_use)
    sigmoid_gate = jax.nn.sigmoid(gate_value)
    grad_gate = hidden_part * up_value * sigmoid_gate * (1.0 + gate_value * (1.0 - sigmoid_gate))
    grad_up = hidden_part * (gate_value * sigmoid_gate)
    grad_pair = jnp.stack([grad_gate, grad_up], axis=1).astype(jnp.bfloat16)
    pair_flat = grad_pair.reshape(use_rows, 2 * ffn_cols)
    ffn_local = left_product(h_two_use, pair_flat).reshape(-1, 2, ffn_cols)

    def ffn_back_term(start_row, rows_here):
        return right_product(pair_flat, ffn_use)

    grad_mid_part, gain_two_part = rms_backward(
        to_tokens(ffn_back_term), normed_two, factor_two, gain_two
    )
    grad_mid = grad_output + grad_mid_part
    grad_attended = (RESID * grad_mid).astype(jnp.bfloat16)
    grad_attended_use = spread(gather_tokens(grad_attended))
    out_local = left_product(head_round, grad_attended_use)
    head_part = right_product(grad_attended_use, out_use)
    head_grad = head_part
    head_grad = head_grad.astype(jnp.bfloat16).reshape(
        seq_use, SEQUENCE_LENGTH, kv_used, group_here, HEAD_SIZE
    )

    def backward_sequence(inputs):
        return attend_back(
            inputs[0], inputs[1], inputs[2], inputs[3], inputs[4], inputs[5], rows_per_block
        )

    query_back, key_back, value_back = lax.map(
        backward_sequence, (query_seq, key_seq, value_seq, prefix_use, logsum, head_grad)
    )
    query_grad_heads = rope_back(
        query_back.reshape(use_rows, col_heads, HEAD_SIZE) * ATTN_SCALE, cosine_table, sine_table
    )
    query_grad_round = query_grad_heads.reshape(use_rows, col_heads * HEAD_SIZE).astype(
        jnp.bfloat16
    )
    key_grad_heads = rope_back(
        key_back.reshape(use_rows, kv_used, HEAD_SIZE), cosine_table, sine_table
    )
    kv_grad_used = jnp.stack(
        [
            key_grad_heads.reshape(use_rows, kv_used * HEAD_SIZE),
            value_back.reshape(use_rows, kv_used * HEAD_SIZE),
        ],
        axis=1,
    )
    kv_grad = kv_grad_used.astype(jnp.bfloat16)
    kv_flat = kv_grad.reshape(use_rows, 2 * frame_width)
    query_local = left_product(h_one_use, query_grad_round)
    kv_frame_local = left_product(h_one_use, kv_flat).reshape(-1, 2, frame_width)
    kv_local = lax.dynamic_update_slice_in_dim(
        jnp.zeros((kv_frame_local.shape[0], 2, kv_all), jnp.float32),
        kv_frame_local,
        frame_start * HEAD_SIZE,
        2,
    )

    def input_term(start_row, rows_here):
        return right_product(query_grad_round, query_use) + right_product(kv_flat, kv_use)

    grad_in_part, gain_one_part = rms_backward(
        to_tokens(input_term), normed_one, factor_one, gain_one
    )
    input_grad = (grad_mid + grad_in_part).astype(jnp.bfloat16)
    local_grads = reduce_rows(query_local, kv_local, out_local, ffn_local, down_local)
    summed = (
        lax.psum(local_grads[0].astype(jnp.bfloat16), "dp").astype(jnp.float32),
        lax.psum(local_grads[2].astype(jnp.bfloat16), "dp").astype(jnp.float32),
        lax.psum(local_grads[3].astype(jnp.bfloat16), "dp").astype(jnp.float32),
        lax.psum(local_grads[4].astype(jnp.bfloat16), "dp").astype(jnp.float32),
    )
    kv_summed, gains_total = lax.psum(
        (local_grads[1], jnp.stack([gain_one_part, gain_two_part])), ("dp", "col")
    )
    raw_grads = (
        summed[0],
        kv_summed[:, 0],
        kv_summed[:, 1],
        summed[1],
        summed[2][:, 0],
        summed[2][:, 1],
        summed[3],
    )
    masters = (
        query_weight,
        key_projection,
        value_projection,
        out_weight,
        gate_weight,
        up_weight,
        down_weight,
    )
    moments = (
        query_moment,
        key_first_moment,
        value_first_moment,
        out_moment,
        gate_moment,
        up_moment,
        down_moment,
    )
    squares = (
        query_square,
        key_second_moment,
        value_second_moment,
        out_square,
        gate_square,
        up_square,
        down_square,
    )
    copied_sum = jnp.sum(gains_total * gains_total) + jnp.sum(kv_summed * kv_summed)
    square_local = jnp.where(col_index == 0, copied_sum, 0.0)
    for position in (0, 3, 4, 5, 6):
        square_local = square_local + jnp.sum(raw_grads[position] * raw_grads[position])
    total_sum = lax.psum(square_local, ("row", "col"))
    grad_norm = jnp.sqrt(total_sum)
    factor = jnp.minimum(1.0, CLIP / grad_norm)
    clipped = []
    nexts = []
    variances = []
    for position in range(7):
        gradient = raw_grads[position] * factor
        weight_next, variance = adam(
            masters[position], gradient, moments[position], squares[position], DECAY, LEARN
        )
        clipped.append(gradient)
        nexts.append(weight_next)
        variances.append(variance)
    gains_grad = gains_total * factor
    gains_next, gains_variance = adam(
        norm_gains, gains_grad, gains_moment, gains_square, 0.0, GAINS_LEARN
    )
    return (
        layer_out,
        input_grad,
        clipped[0],
        clipped[1],
        clipped[2],
        clipped[3],
        clipped[4],
        clipped[5],
        clipped[6],
        gains_grad,
        nexts[0],
        nexts[1],
        nexts[2],
        nexts[3],
        nexts[4],
        nexts[5],
        nexts[6],
        gains_next,
        variances[0],
        variances[1],
        variances[2],
        variances[3],
        variances[4],
        variances[5],
        variances[6],
        gains_variance,
        grad_norm,
    )


LOW = jnp.bfloat16
WIDE = jnp.float32
CHUNK = 512
LANES = 128
MASKED = -1e30
VMEM_BYTES = 48 * 1024 * 1024


def swaps_fit(mesh):
    return dict(mesh.shape) == {"dp": 4, "row": 2, "col": 4}


def swap(values, axis, bit):
    size = lax.axis_size(axis)
    return lax.ppermute(values, axis, [(place, place ^ bit) for place in range(size)])


def swap_core(values):
    return swap(values, "dp", 1)


def swap_y(values):
    return swap(values, "dp", 2)


def swap_x(values):
    return swap(values, "row", 1)


def swap_near(values):
    return swap(values, "col", 1)


def swap_far(values):
    return swap(values, "col", 2)


def swap_corner(values):
    cols = lax.axis_size("col")
    pairs = [
        (row * cols + col, (row ^ 1) * cols + (col ^ 1))
        for row in range(lax.axis_size("row"))
        for col in range(cols)
    ]
    return lax.ppermute(values, ("row", "col"), pairs)


def fold(kept, sent, move):
    return kept + move(sent.astype(LOW)).astype(WIDE)


def in_order(place, own, other, axis):
    return jnp.concatenate(
        [jnp.where(place == 0, own, other), jnp.where(place == 0, other, own)], axis=axis
    )


def cut(values, start, size, axis):
    return lax.dynamic_slice_in_dim(values, start, size, axis)


def partner_lanes(values):
    lane = lax.broadcasted_iota(jnp.int32, values.shape, 1)
    half = HEAD_SIZE // 2
    ahead = pltpu.roll(values, values.shape[1] - half, 1)
    behind = pltpu.roll(values, half, 1)
    return jnp.where(lane % HEAD_SIZE < half, ahead, behind)


def first_lanes(shape):
    return lax.broadcasted_iota(jnp.int32, shape, 1) < HEAD_SIZE


def dot_nt(left_side, right_side):
    return lax.dot_general(
        left_side, right_side, (((1,), (1,)), ((), ())), preferred_element_type=WIDE
    )


def dot_tn(left_side, right_side):
    return lax.dot_general(
        left_side, right_side, (((0,), (0,)), ((), ())), preferred_element_type=WIDE
    )


def project_kernel(normed_ref, weight_ref, cosine_ref, sine_ref, out_ref):
    product = jnp.dot(normed_ref[0], weight_ref[...], preferred_element_type=WIDE)
    cosine = cosine_ref[0]
    sine = sine_ref[0]
    for tile in range(3):
        part = product[:, tile * LANES : (tile + 1) * LANES]
        turned = part * cosine + partner_lanes(part) * sine
        if tile < 2:
            turned = turned * ATTN_SCALE
        else:
            turned = jnp.where(first_lanes(part.shape), turned, part)
        out_ref[0, 0, :, tile * LANES : (tile + 1) * LANES] = turned.astype(LOW)


def project(normed_pair, weights, cosine, sine):
    groups = 4
    wide = 3 * LANES
    return pl.pallas_call(
        project_kernel,
        grid=(2, groups),
        in_specs=[
            pl.BlockSpec((1, CHUNK, MODEL_WIDTH), lambda i, j: (i, 0, 0)),
            pl.BlockSpec((MODEL_WIDTH, wide), lambda i, j: (0, j)),
            pl.BlockSpec((1, CHUNK, LANES), lambda i, j: (0, 0, 0)),
            pl.BlockSpec((1, CHUNK, LANES), lambda i, j: (0, 0, 0)),
        ],
        out_specs=pl.BlockSpec((1, 1, CHUNK, wide), lambda i, j: (j, i, 0, 0)),
        out_shape=jax.ShapeDtypeStruct((groups, 2, CHUNK, wide), LOW),
        compiler_params=pltpu.CompilerParams(vmem_limit_bytes=VMEM_BYTES),
        cost_estimate=pl.CostEstimate(
            flops=2 * 2 * CHUNK * MODEL_WIDTH * groups * wide,
            bytes_accessed=4 * MODEL_WIDTH * (2 * CHUNK + groups * wide),
            transcendentals=0,
        ),
    )(normed_pair, weights, cosine, sine)


def split_heads(tiles, lanes_from):
    heads = []
    for head in range(4):
        tile = tiles[:, (head // 2) * LANES : (head // 2 + 1) * LANES].astype(WIDE)
        if (head % 2) * HEAD_SIZE != lanes_from:
            tile = pltpu.roll(tile, HEAD_SIZE, 1)
        low = first_lanes(tile.shape)
        heads.append(jnp.where(low if lanes_from == 0 else ~low, tile, 0.0).astype(LOW))
    return heads


def join_heads(heads, lanes_from):
    tiles = []
    for pair in range(2):
        even, odd = heads[2 * pair], heads[2 * pair + 1]
        if lanes_from == 0:
            odd = pltpu.roll(odd, HEAD_SIZE, 1)
        else:
            even = pltpu.roll(even, HEAD_SIZE, 1)
        tiles.append(jnp.where(first_lanes(even.shape), even, odd))
    return tiles


def visible_chunks(chunk, prefix):
    whole = jnp.maximum(chunk, prefix // CHUNK)
    some = jnp.maximum(chunk + 1, (prefix + CHUNK - 1) // CHUNK)
    return whole, some


def attend_kernel(place_ref, prefix_ref, q_ref, kv_ref, o_ref, lse_ref, heads, top, total, acc):
    sequence = pl.program_id(0)
    place = place_ref[0]
    prefix = prefix_ref[sequence]
    chunk = pl.program_id(1) ^ place
    for head, tile in enumerate(split_heads(q_ref[0, 0], 0)):
        heads[head] = tile
        top[head] = jnp.full((CHUNK, LANES), MASKED, WIDE)
        total[head] = jnp.zeros((CHUNK, LANES), WIDE)
        acc[head] = jnp.zeros((CHUNK, LANES), WIDE)

    def step(masked, other, carry):
        kv = kv_ref[other ^ place, 0]
        if masked:
            row = lax.broadcasted_iota(jnp.int32, (CHUNK, CHUNK), 0) + chunk * CHUNK
            key = lax.broadcasted_iota(jnp.int32, (CHUNK, CHUNK), 1) + other * CHUNK
            visible = key <= jnp.maximum(row, prefix - 1)
        for head in range(4):
            scores = dot_nt(heads[head], kv)
            if masked:
                scores = jnp.where(visible, scores, MASKED)
            old = top[head]
            new = jnp.maximum(old, jnp.max(scores, axis=1, keepdims=True))
            exponent = jnp.exp(scores - new[:, :1])
            shrink = jnp.exp(old - new)
            top[head] = new
            total[head] = total[head] * shrink + jnp.sum(exponent, axis=1, keepdims=True)
            acc[head] = acc[head] * shrink + jnp.dot(
                exponent.astype(LOW), kv, preferred_element_type=WIDE
            )
        return carry

    whole, some = visible_chunks(chunk, prefix)
    lax.fori_loop(0, whole, functools.partial(step, False), 0)
    lax.fori_loop(whole, some, functools.partial(step, True), 0)
    lane = lax.broadcasted_iota(jnp.int32, (CHUNK, LANES), 1)
    logs = jnp.zeros((CHUNK, LANES), WIDE)
    results = []
    for head in range(4):
        results.append(acc[head] / total[head])
        logs = jnp.where(lane == head, top[head] + jnp.log(total[head]), logs)
    lse_ref[0, 0] = jnp.transpose(logs)[:8]
    for pair, tile in enumerate(join_heads(results, HEAD_SIZE)):
        o_ref[0, 0, :, pair * LANES : (pair + 1) * LANES] = tile.astype(LOW)


def attend(place, prefixes, packed):
    units = 2 * 4 * 10
    return pl.pallas_call(
        attend_kernel,
        grid_spec=pltpu.PrefetchScalarGridSpec(
            num_scalar_prefetch=2,
            grid=(2, 4),
            in_specs=[
                pl.BlockSpec((1, 1, CHUNK, 2 * LANES), lambda i, j, *_: (j, i, 0, 0)),
                pl.BlockSpec((4, 1, CHUNK, LANES), lambda i, j, *_: (0, i, 0, 2)),
            ],
            out_specs=[
                pl.BlockSpec((1, 1, CHUNK, 2 * LANES), lambda i, j, *_: (j, i, 0, 0)),
                pl.BlockSpec((1, 1, 8, CHUNK), lambda i, j, *_: (j, i, 0, 0)),
            ],
            scratch_shapes=[
                pltpu.VMEM((4, CHUNK, LANES), LOW),
                pltpu.VMEM((4, CHUNK, LANES), WIDE),
                pltpu.VMEM((4, CHUNK, LANES), WIDE),
                pltpu.VMEM((4, CHUNK, LANES), WIDE),
            ],
        ),
        out_shape=[
            jax.ShapeDtypeStruct((4, 2, CHUNK, 2 * LANES), LOW),
            jax.ShapeDtypeStruct((4, 2, 8, CHUNK), WIDE),
        ],
        compiler_params=pltpu.CompilerParams(vmem_limit_bytes=VMEM_BYTES),
        cost_estimate=pl.CostEstimate(
            flops=units * 4 * CHUNK * CHUNK * 256 * 2 * 2,
            bytes_accessed=8 * 1024 * 1024,
            transcendentals=units * 4 * CHUNK * CHUNK,
        ),
    )(place, prefixes, packed, packed)


def attend_back_kernel(
    place_ref,
    prefix_ref,
    q_ref,
    kv_ref,
    o_ref,
    do_ref,
    lse_ref,
    cosine_ref,
    sine_ref,
    out_ref,
    heads,
    grads,
    deltas,
    q_acc,
    kv_acc,
):
    sequence = pl.program_id(0)
    slot = pl.program_id(1)
    place = place_ref[0]
    prefix = prefix_ref[sequence]
    chunk = slot ^ place

    @pl.when(slot == 0)
    def _():
        kv_acc[...] = jnp.zeros_like(kv_acc)

    ones = jnp.ones((8, LANES), WIDE)
    out_heads = split_heads(o_ref[0, 0], HEAD_SIZE)
    grad_heads = split_heads(do_ref[0, 0], HEAD_SIZE)
    for head, tile in enumerate(split_heads(q_ref[0, 0], 0)):
        heads[head] = tile
        grads[head] = grad_heads[head]
        product = out_heads[head].astype(WIDE) * grad_heads[head].astype(WIDE)
        deltas[head] = lax.dot_general(
            ones,
            product,
            (((1,), (1,)), ((), ())),
            precision=lax.Precision.HIGHEST,
            preferred_element_type=WIDE,
        )
        q_acc[head] = jnp.zeros((CHUNK, LANES), WIDE)

    def step(masked, other, carry):
        other_slot = other ^ place
        kv = kv_ref[other_slot, 0]
        if masked:
            key = lax.broadcasted_iota(jnp.int32, (CHUNK, CHUNK), 0) + other * CHUNK
            row = lax.broadcasted_iota(jnp.int32, (CHUNK, CHUNK), 1) + chunk * CHUNK
            visible = key <= jnp.maximum(row, prefix - 1)
        for head in range(4):
            scores = dot_nt(kv, heads[head])
            if masked:
                scores = jnp.where(visible, scores, MASKED)
            probability = jnp.exp(scores - lse_ref[0, 0, head : head + 1])
            grad_prob = dot_nt(kv, grads[head])
            grad_scores = (probability * (grad_prob - deltas[head][:1])).astype(LOW)
            kv_acc[other_slot] += jnp.dot(
                grad_scores, heads[head], preferred_element_type=WIDE
            ) + jnp.dot(probability.astype(LOW), grads[head], preferred_element_type=WIDE)
            q_acc[head] += dot_tn(grad_scores, kv)
        return carry

    whole, some = visible_chunks(chunk, prefix)
    lax.fori_loop(0, whole, functools.partial(step, False), 0)
    lax.fori_loop(whole, some, functools.partial(step, True), 0)
    cosine = cosine_ref[slot]
    sine = sine_ref[slot]
    for pair, tile in enumerate(join_heads([q_acc[head] for head in range(4)], 0)):
        tile = tile * ATTN_SCALE
        turned = tile * cosine + partner_lanes(tile * sine)
        out_ref[slot, 0, :, pair * LANES : (pair + 1) * LANES] = turned.astype(LOW)

    @pl.when(slot == 3)
    def _():
        for other in range(4):
            tile = kv_acc[other]
            turned = tile * cosine_ref[other] + partner_lanes(tile * sine_ref[other])
            turned = jnp.where(first_lanes(tile.shape), turned, tile)
            out_ref[other, 0, :, 2 * LANES :] = turned.astype(LOW)


def attend_grad(place, prefixes, packed, attended, grad_attended, logsum, cosine, sine):
    units = 2 * 4 * 10
    return pl.pallas_call(
        attend_back_kernel,
        grid_spec=pltpu.PrefetchScalarGridSpec(
            num_scalar_prefetch=2,
            grid=(2, 4),
            in_specs=[
                pl.BlockSpec((1, 1, CHUNK, 2 * LANES), lambda i, j, *_: (j, i, 0, 0)),
                pl.BlockSpec((4, 1, CHUNK, LANES), lambda i, j, *_: (0, i, 0, 2)),
                pl.BlockSpec((1, 1, CHUNK, 2 * LANES), lambda i, j, *_: (j, i, 0, 0)),
                pl.BlockSpec((1, 1, CHUNK, 2 * LANES), lambda i, j, *_: (j, i, 0, 0)),
                pl.BlockSpec((1, 1, 8, CHUNK), lambda i, j, *_: (j, i, 0, 0)),
                pl.BlockSpec((4, CHUNK, LANES), lambda i, j, *_: (0, 0, 0)),
                pl.BlockSpec((4, CHUNK, LANES), lambda i, j, *_: (0, 0, 0)),
            ],
            out_specs=pl.BlockSpec((4, 1, CHUNK, 3 * LANES), lambda i, j, *_: (0, i, 0, 0)),
            scratch_shapes=[
                pltpu.VMEM((4, CHUNK, LANES), LOW),
                pltpu.VMEM((4, CHUNK, LANES), LOW),
                pltpu.VMEM((4, 8, CHUNK), WIDE),
                pltpu.VMEM((4, CHUNK, LANES), WIDE),
                pltpu.VMEM((4, CHUNK, LANES), WIDE),
            ],
        ),
        out_shape=jax.ShapeDtypeStruct((4, 2, CHUNK, 3 * LANES), LOW),
        compiler_params=pltpu.CompilerParams(vmem_limit_bytes=VMEM_BYTES),
        cost_estimate=pl.CostEstimate(
            flops=units * 4 * CHUNK * CHUNK * 256 * 2 * 5,
            bytes_accessed=16 * 1024 * 1024,
            transcendentals=units * 4 * CHUNK * CHUNK,
        ),
    )(place, prefixes, packed, packed, attended, grad_attended, logsum, cosine, sine)


def dp_spot(dp):
    return dp.reshape(1)


def step_kernel(spot_ref, factor_ref, grad_ref, weight_ref, moment_ref, square_ref, *outs):
    gradient = grad_ref[0].astype(WIDE) * factor_ref[0, 0]
    following, variance = adam(
        weight_ref[...], gradient, moment_ref[...], square_ref[...], DECAY, LEARN
    )
    outs[0][...] = gradient
    outs[1][...] = following
    outs[2][...] = variance


def step_weight(spot, factor, pieces, axis, weight, moment, square):
    count, rows, columns = pieces.shape
    block_rows = min(rows, (1 << 17) // columns)
    parts = rows // block_rows

    def piece_at(block, part, spot_ref):
        code = spot_ref[0]
        return (block ^ ((code % 2) * 2 + code // 2), part, 0)

    def weight_at(block, part, spot_ref):
        return (part, block) if axis == 1 else (block * parts + part, 0)

    spec = pl.BlockSpec((block_rows, columns), weight_at)
    return pl.pallas_call(
        step_kernel,
        grid_spec=pltpu.PrefetchScalarGridSpec(
            num_scalar_prefetch=1,
            grid=(count, parts),
            in_specs=[
                pl.BlockSpec(memory_space=pltpu.SMEM),
                pl.BlockSpec((1, block_rows, columns), piece_at),
                spec,
                spec,
                spec,
            ],
            out_specs=[spec] * 3,
        ),
        out_shape=[jax.ShapeDtypeStruct(weight.shape, WIDE)] * 3,
        compiler_params=pltpu.CompilerParams(vmem_limit_bytes=VMEM_BYTES),
        cost_estimate=pl.CostEstimate(
            flops=12 * weight.size, bytes_accessed=26 * weight.size, transcendentals=weight.size
        ),
    )(spot, factor, pieces, weight, moment, square)


def step_pair_kernel(spot_ref, factor_ref, grad_ref, *refs):
    core, start = spot_ref[0], spot_ref[1]
    factor = factor_ref[0, 0]
    for group in range(4):
        turned = group ^ start
        slot = turned // 2 + (turned % 2) * 2
        first = grad_ref[core * 4 + slot].astype(WIDE) * factor
        second = grad_ref[(1 - core) * 4 + slot].astype(WIDE) * factor
        low = first_lanes(first.shape)
        lanes = pl.ds(group * LANES, LANES)
        key_grad = jnp.where(low, first, pltpu.roll(second, HEAD_SIZE, 1))
        value_grad = jnp.where(low, pltpu.roll(first, HEAD_SIZE, 1), second)
        for gradient, at in ((key_grad, 0), (value_grad, 1)):
            weight_ref, moment_ref, square_ref = refs[3 * at : 3 * at + 3]
            following, variance = adam(
                weight_ref[:, lanes],
                gradient,
                moment_ref[:, lanes],
                square_ref[:, lanes],
                DECAY,
                LEARN,
            )
            outs = refs[6 + 3 * at : 9 + 3 * at]
            outs[0][:, lanes] = gradient
            outs[1][:, lanes] = following
            outs[2][:, lanes] = variance


def step_pair(spot, factor, pieces, key, value):
    rows, columns = key[0].shape
    block_rows = 128
    spec = pl.BlockSpec((block_rows, columns), lambda i, *_: (i, 0))
    outs = pl.pallas_call(
        step_pair_kernel,
        grid_spec=pltpu.PrefetchScalarGridSpec(
            num_scalar_prefetch=1,
            grid=(rows // block_rows,),
            in_specs=[
                pl.BlockSpec(memory_space=pltpu.SMEM),
                pl.BlockSpec((8, block_rows, LANES), lambda i, *_: (0, i, 0)),
            ]
            + [spec] * 6,
            out_specs=[spec] * 6,
        ),
        out_shape=[jax.ShapeDtypeStruct((rows, columns), WIDE)] * 6,
        compiler_params=pltpu.CompilerParams(vmem_limit_bytes=VMEM_BYTES),
        cost_estimate=pl.CostEstimate(
            flops=24 * rows * columns,
            bytes_accessed=52 * rows * columns,
            transcendentals=2 * rows * columns,
        ),
    )(spot, factor, pieces, *key, *value)
    return outs[:3], outs[3:]


def slot_tables(place):
    half = HEAD_SIZE // 2
    frequency = THETA ** (-(jnp.arange(half, dtype=WIDE) * 2.0 / HEAD_SIZE))
    chunk = jnp.arange(4, dtype=jnp.int32) ^ place
    position = (chunk[:, None] * CHUNK + jnp.arange(CHUNK)[None, :]).astype(WIDE)
    angles = position[:, :, None] * frequency[None, None, :]
    cosine, sine = jnp.cos(angles), jnp.sin(angles)
    return (
        jnp.concatenate([cosine] * 4, axis=2),
        jnp.concatenate([-sine, sine, -sine, sine], axis=2),
    )


def exchange(pieces):
    return [
        pieces[0],
        swap_x(pieces[1]),
        swap_near(pieces[2]),
        swap_corner(pieces[3]),
    ]


def rows_norm(values):
    factor = lax.rsqrt(
        jnp.sum(values * values, axis=1, keepdims=True) / MODEL_WIDTH + EPS_NORM
    )
    return values * factor, factor


def rows_norm_back(gradient, normed, factor, gain_row):
    weighted = gradient * gain_row
    inner = jnp.sum(weighted * normed, axis=1, keepdims=True) / MODEL_WIDTH
    return factor * (weighted - normed * inner), jnp.sum(gradient * normed, axis=0)


def swapped_shards(
    tokens,
    cotangent,
    prefix,
    query_weight,
    key_projection,
    value_projection,
    out_weight,
    gate_weight,
    up_weight,
    down_weight,
    norm_gains,
    query_moment,
    key_first_moment,
    value_first_moment,
    out_moment,
    gate_moment,
    up_moment,
    down_moment,
    gains_moment,
    query_square,
    key_second_moment,
    value_second_moment,
    out_square,
    gate_square,
    up_square,
    down_square,
    gains_square,
):
    row = lax.axis_index("row")
    col = lax.axis_index("col")
    dp = lax.axis_index("dp")
    core = dp % 2
    side = dp // 2
    near = col % 2
    far = col // 2
    place = near * 2 + row
    half_rows = tokens.shape[0] // 2
    half_width = tokens.shape[1]

    owner = [col ^ (2 * row), col ^ (2 - 2 * row), col ^ (1 + 2 * row), col ^ (3 - 2 * row)]

    def by_owner(block, axis):
        other = swap_far(block)
        first = jnp.where(row == 0, block, other)
        second = jnp.where(row == 0, other, block)
        pair = jnp.stack([first, second])
        return jnp.concatenate([pair, swap_near(pair)])

    swapped = [1, 0, 3, 2]

    def reorder(blocks):
        return jnp.stack([blocks[place_at] for place_at in swapped])

    q_cut = cut(query_weight, core * 2 * LANES + side * LANES, LANES, 1).astype(LOW)
    q_blocks = by_owner(q_cut, 1)
    q_own = jnp.stack([q_blocks, swap_y(q_blocks)], axis=1)
    q_whole = jnp.concatenate(
        [q_own, swap_x(reorder(q_own))], axis=2
    )

    def heads_of(matrix):
        return jnp.stack(
            [cut(matrix, (at * 2 + core) * HEAD_SIZE, HEAD_SIZE, 1) for at in owner]
        ).astype(LOW)

    kv_own = jnp.concatenate([heads_of(key_projection), heads_of(value_projection)], axis=2)
    kv_whole = jnp.concatenate([kv_own, swap_x(reorder(kv_own))], axis=1)
    in_weights = jnp.stack([q_whole[:, 0], q_whole[:, 1], kv_whole], axis=1)
    in_weights = in_weights.transpose(2, 0, 1, 3).reshape(MODEL_WIDTH, 4 * 3 * LANES)

    o_cut = cut(out_weight, core * 2 * LANES + side * LANES, LANES, 0).astype(LOW)
    o_blocks = by_owner(o_cut, 0)
    o_rows = jnp.concatenate([o_blocks, swap_x(reorder(o_blocks))], axis=2)
    out_weights = jnp.stack([o_rows, swap_y(o_rows)], axis=1).reshape(
        4 * 2 * LANES, MODEL_WIDTH
    )

    units = gate_weight.shape[1] // 2

    def hidden_cut(matrix, axis):
        return cut(matrix, core * units + side * (units // 2), units // 2, axis).astype(LOW)

    def widen(matrix, unit_axis, x_first):
        block = hidden_cut(matrix, unit_axis)
        block = jnp.concatenate([block, swap_far(block)], axis=unit_axis)
        if x_first:
            block = jnp.concatenate([block, swap_x(block)], axis=1 - unit_axis)
            return jnp.concatenate([block, swap_y(block)], axis=unit_axis)
        block = jnp.concatenate([block, swap_y(block)], axis=unit_axis)
        return jnp.concatenate([block, swap_x(block)], axis=1 - unit_axis)

    gate_whole = widen(gate_weight, 1, True)
    up_whole = widen(up_weight, 1, False)
    down_whole = widen(down_weight, 0, True)

    def enter(values):
        own = cut(values, row * half_rows, half_rows, 0)
        sent = cut(values, (1 - row) * half_rows, half_rows, 0)
        return jnp.concatenate([own, swap_x(sent)], axis=1)

    def leave(values):
        back = swap_x(values[:, half_width:])
        return in_order(row, values[:, :half_width], back, 0)

    def pair_core(values):
        return jnp.concatenate([values, swap_core(values)], axis=0)

    def gather_four(values):
        both = jnp.concatenate([values, swap_near(values)], axis=0)
        return jnp.concatenate([both, swap_core(both)], axis=0)

    def sum_four(part):
        count = part.shape[0] // 4
        part = fold(part[: 2 * count], part[2 * count :], swap_core)
        return fold(part[:count], part[count:], swap_near)

    gains = jnp.concatenate([norm_gains, swap_x(norm_gains)], axis=1)
    prefixes = jnp.stack([prefix[far], swap_core(prefix)[far]])
    place_array = place.reshape(1)
    cosine, sine = slot_tables(place)

    x = enter(tokens).astype(WIDE)
    normed_one, factor_one = rows_norm(x)
    h_one = pair_core((normed_one * gains[0]).astype(LOW))
    projected = project(h_one.reshape(2, CHUNK, MODEL_WIDTH), in_weights, cosine, sine)
    packed = jnp.stack(exchange([projected[slot] for slot in range(4)]))
    attended, logsum = attend(place_array, prefixes, packed)
    back = exchange([attended[slot] for slot in range(4)])
    o_tokens = jnp.concatenate(back, axis=2).reshape(2 * CHUNK, 4 * 2 * LANES)
    out_part = matrix_multiply(o_tokens, out_weights)
    residual = x + RESID * fold(out_part[:half_rows], out_part[half_rows:], swap_core)

    normed_two, factor_two = rows_norm(residual)
    h_two = gather_four((normed_two * gains[1]).astype(LOW))
    gate_value = matrix_multiply(h_two, gate_whole)
    up_value = matrix_multiply(h_two, up_whole)
    hidden = (jax.nn.silu(gate_value) * up_value).astype(LOW)
    down_part = sum_four(matrix_multiply(hidden, down_whole))
    layer_out = leave((residual + RESID * down_part).astype(LOW))

    grad_output = enter(cotangent).astype(WIDE)
    grad_mlp = gather_four((RESID * grad_output).astype(LOW))
    down_local = left_product(hidden, grad_mlp)
    hidden_part = right_product(grad_mlp, down_whole)
    sigmoid_gate = jax.nn.sigmoid(gate_value)
    grad_gate = (
        hidden_part * up_value * sigmoid_gate * (1.0 + gate_value * (1.0 - sigmoid_gate))
    ).astype(LOW)
    grad_up = (hidden_part * (gate_value * sigmoid_gate)).astype(LOW)
    h_two_part = right_product(grad_gate, gate_whole) + right_product(grad_up, up_whole)
    gate_local = left_product(h_two, grad_gate)
    up_local = left_product(h_two, grad_up)
    grad_mid_part, gain_two_part = rows_norm_back(
        sum_four(h_two_part), normed_two, factor_two, gains[1]
    )
    grad_mid = grad_output + grad_mid_part

    grad_attended = pair_core((RESID * grad_mid).astype(LOW))
    head_grad = right_product(grad_attended, out_weights).astype(LOW)
    head_grad = head_grad.reshape(2, CHUNK, 4, 2 * LANES)
    out_local = left_product(o_tokens, grad_attended)
    head_pieces = jnp.stack(exchange([head_grad[:, :, slot] for slot in range(4)]))
    packed_grad = attend_grad(
        place_array, prefixes, packed, attended, head_pieces, logsum, cosine, sine
    )
    pieces = exchange([packed_grad[slot] for slot in range(4)])
    in_grads = jnp.concatenate(pieces, axis=2).reshape(2 * CHUNK, 4 * 3 * LANES)
    in_local = left_product(h_one, in_grads)
    h_one_part = right_product(in_grads, in_weights)
    grad_in_part, gain_one_part = rows_norm_back(
        fold(h_one_part[:half_rows], h_one_part[half_rows:], swap_core),
        normed_one,
        factor_one,
        gains[0],
    )
    input_grad = leave((grad_mid + grad_in_part).astype(LOW))

    def halve_hidden(part, unit_axis, x_first):
        def half(values, axis, which):
            size = values.shape[axis] // 2
            return lax.slice_in_dim(values, which * size, (which + 1) * size, axis=axis)

        steps = [(swap_x, 1 - unit_axis), (swap_y, unit_axis)]
        if not x_first:
            steps = steps[::-1]
        for move, axis in steps + [(swap_far, unit_axis)]:
            part = fold(half(part, axis, 0), half(part, axis, 1), move)
        return part.astype(LOW)

    def spread(piece):
        pair = jnp.stack([piece, swap_y(piece)])
        return jnp.concatenate([pair, swap_core(pair)])

    gate_piece = halve_hidden(gate_local, 1, False)
    up_piece = halve_hidden(up_local, 1, True)
    down_piece = halve_hidden(down_local, 0, True)

    wide = 3 * LANES

    def columns(values, order, size):
        return jnp.concatenate([values[:, at * size : (at + 1) * size] for at in order], axis=1)

    in_part = fold(
        in_local[:half_width], columns(in_local[half_width:], swapped, wide), swap_x
    )
    in_part = fold(in_part[:, : 2 * wide], in_part[:, 2 * wide :], swap_near)
    in_part = fold(
        jnp.where(row == 0, in_part[:, :wide], in_part[:, wide:]),
        jnp.where(row == 0, in_part[:, wide:], in_part[:, :wide]),
        swap_far,
    ).astype(LOW)
    from_side = swap_y(in_part[:, LANES:])
    query_piece = (
        in_part[:, :LANES].astype(WIDE) + from_side[:, :LANES].astype(WIDE)
    ).astype(LOW)
    kv_piece = (
        in_part[:, 2 * LANES :].astype(WIDE) + from_side[:, LANES:].astype(WIDE)
    ).astype(LOW)

    def out_rows(values):
        size = 2 * LANES
        return jnp.concatenate([values[at * size : (at + 1) * size] for at in swapped])

    out_part = fold(out_local[:, :half_width], out_rows(out_local[:, half_width:]), swap_x)
    out_part = fold(out_part[: 4 * LANES], out_part[4 * LANES :], swap_near)
    out_part = fold(
        jnp.where(row == 0, out_part[: 2 * LANES], out_part[2 * LANES :]),
        jnp.where(row == 0, out_part[2 * LANES :], out_part[: 2 * LANES]),
        swap_far,
    )
    out_piece = fold(out_part[:LANES], out_part[LANES:], swap_y).astype(LOW)

    kv_pieces = jnp.stack([kv_piece, swap_far(kv_piece)])
    kv_pieces = jnp.concatenate([kv_pieces, swap_near(kv_pieces)])
    kv_pieces = jnp.concatenate([kv_pieces, swap_core(kv_pieces)])

    gain_parts = jnp.stack([gain_one_part, gain_two_part])
    gain_parts = gain_parts[:, :half_width] + swap_x(gain_parts[:, half_width:])
    gains_total = lax.psum(gain_parts, ("dp", "col"))

    def squares_of(values):
        values = values.astype(WIDE)
        return jnp.sum(values * values)

    square_local = jnp.where((col == 0) & (dp == 0), squares_of(gains_total), 0.0)
    square_local = square_local + jnp.where(side == 0, squares_of(kv_piece), 0.0)
    for piece in (query_piece, out_piece, gate_piece, up_piece, down_piece):
        square_local = square_local + squares_of(piece)
    grad_norm = jnp.sqrt(lax.psum(square_local, ("dp", "row", "col")))
    factor = jnp.minimum(1.0, CLIP / grad_norm)
    factor_cell = factor.reshape(1, 1)
    spot = dp_spot(dp)

    def step(piece, axis, weight, moment, square):
        return step_weight(spot, factor_cell, spread(piece), axis, weight, moment, square)

    query_out = step(query_piece, 1, query_weight, query_moment, query_square)
    out_out = step(out_piece, 0, out_weight, out_moment, out_square)
    gate_out = step(gate_piece, 1, gate_weight, gate_moment, gate_square)
    up_out = step(up_piece, 1, up_weight, up_moment, up_square)
    down_out = step(down_piece, 0, down_weight, down_moment, down_square)
    kv_spot = jnp.stack([core, col])
    key_out, value_out = step_pair(
        kv_spot,
        factor_cell,
        kv_pieces,
        (key_projection, key_first_moment, key_second_moment),
        (value_projection, value_first_moment, value_second_moment),
    )
    results = (query_out, key_out, value_out, out_out, gate_out, up_out, down_out)
    clipped, nexts, variances = zip(*results)
    gains_grad = gains_total * factor
    gains_next, gains_variance = adam(
        norm_gains, gains_grad, gains_moment, gains_square, 0.0, GAINS_LEARN
    )
    return (
        layer_out,
        input_grad,
        *clipped,
        gains_grad,
        *nexts,
        gains_next,
        *variances,
        gains_variance,
        grad_norm,
    )


def solution(mesh):
    placed = (
        P(("dp", "col"), "row"),
        P(("dp", "col"), "row"),
        P("dp"),
        P("row", "col"),
        P("row", None),
        P("row", None),
        P("col", "row"),
        P("row", "col"),
        P("row", "col"),
        P("col", "row"),
        P(None, "row"),
        P("row", "col"),
        P("row", None),
        P("row", None),
        P("col", "row"),
        P("row", "col"),
        P("row", "col"),
        P("col", "row"),
        P(None, "row"),
        P("row", "col"),
        P("row", None),
        P("row", None),
        P("col", "row"),
        P("row", "col"),
        P("row", "col"),
        P("col", "row"),
        P(None, "row"),
    )
    return jax.shard_map(
        swapped_shards if swaps_fit(mesh) else shards,
        mesh=mesh,
        in_specs=placed,
        out_specs=(
            P(("dp", "col"), "row"),
            P(("dp", "col"), "row"),
            P("row", "col"),
            P("row", None),
            P("row", None),
            P("col", "row"),
            P("row", "col"),
            P("row", "col"),
            P("col", "row"),
            P(None, "row"),
            P("row", "col"),
            P("row", None),
            P("row", None),
            P("col", "row"),
            P("row", "col"),
            P("row", "col"),
            P("col", "row"),
            P(None, "row"),
            P("row", "col"),
            P("row", None),
            P("row", None),
            P("col", "row"),
            P("row", "col"),
            P("row", "col"),
            P("col", "row"),
            P(None, "row"),
            P(),
        ),
        check_vma=False,
    )
```

```python
import functools

import jax
import jax.numpy as jnp
from jax import lax
from jax.experimental import pallas as pl
from jax.experimental.pallas import tpu as pltpu
from jax.sharding import PartitionSpec as P

MODEL_WIDTH = 2048
QUERY_HEADS = 32
KEY_VALUE_HEADS = 8
HEAD_SIZE = 64
SEQUENCE_LENGTH = 2048
STEP = 5


EPS_NORM = 1e-05
RESID = 0.22
ATTN_SCALE = 1.0 / 64.0
THETA = 10000000.0
LEARN = 0.1
GAINS_LEARN = 0.5
BETA_ONE = 0.5
BETA_TWO = 0.5
ADAM_EPS = 1e-08
DECAY = 0.1
CLIP = 1.0


def matrix_multiply(left_side, right_side):
    return jnp.dot(left_side, right_side, preferred_element_type=jnp.float32)


def left_product(left_side, right_side):
    return lax.dot_general(
        left_side, right_side, (((0,), (0,)), ((), ())), preferred_element_type=jnp.float32
    )


def right_product(left_side, right_side):
    return lax.dot_general(
        left_side, right_side, (((1,), (1,)), ((), ())), preferred_element_type=jnp.float32
    )


def width_total(values):
    return lax.psum(values, "row")


def gather_tokens(values):
    return lax.all_gather(values, "col", axis=0, tiled=True)


def sum_tokens(term, tok_rows):
    return lax.psum_scatter(
        term(jnp.int32(0), lax.axis_size("col") * tok_rows).astype(jnp.bfloat16),
        "col",
        scatter_dimension=0,
        tiled=True,
    ).astype(jnp.float32)


def fetch_weights(first, second, third, fourth, fifth):
    return (
        lax.all_gather(first, "row", axis=0, tiled=True),
        lax.all_gather(second, "row", axis=0, tiled=True),
        lax.all_gather(third, "row", axis=0, tiled=True),
        lax.all_gather(fourth, "row", axis=1, tiled=True),
        lax.all_gather(fifth, "row", axis=1, tiled=True),
    )


def enter_rows(values):
    return lax.all_to_all(values, "row", split_axis=0, concat_axis=1, tiled=True)


def leave_rows(values):
    return lax.all_to_all(
        values.astype(jnp.bfloat16), "row", split_axis=1, concat_axis=0, tiled=True
    ).astype(values.dtype)


def reduce_rows(first, second, third, fourth, fifth):
    return (
        lax.psum_scatter(first.astype(jnp.bfloat16), "row", scatter_dimension=0, tiled=True).astype(
            jnp.float32
        ),
        lax.psum_scatter(
            second.astype(jnp.bfloat16), "row", scatter_dimension=0, tiled=True
        ).astype(jnp.float32),
        lax.psum_scatter(third.astype(jnp.bfloat16), "row", scatter_dimension=1, tiled=True).astype(
            jnp.float32
        ),
        lax.psum_scatter(
            fourth.astype(jnp.bfloat16), "row", scatter_dimension=0, tiled=True
        ).astype(jnp.float32),
        lax.psum_scatter(fifth.astype(jnp.bfloat16), "row", scatter_dimension=1, tiled=True).astype(
            jnp.float32
        ),
    )


def rope_tables(length):
    half_width = HEAD_SIZE // 2
    frequency = THETA ** (-(jnp.arange(half_width, dtype=jnp.float32) * 2.0 / HEAD_SIZE))
    angles = jnp.arange(length, dtype=jnp.float32)[:, None] * frequency[None, :]
    angles = jnp.concatenate([angles, angles], axis=1)
    return (jnp.cos(angles), jnp.sin(angles))


def rotate(values):
    half_width = values.shape[-1] // 2
    return jnp.concatenate([-values[..., half_width:], values[..., :half_width]], axis=-1)


def rope(values, cosine_table, sine_table):
    return values * cosine_table[:, None, :] + rotate(values) * sine_table[:, None, :]


def rope_back(gradient, cosine_table, sine_table):
    return gradient * cosine_table[:, None, :] - rotate(gradient * sine_table[:, None, :])


def rms_forward(values, gain_row):
    squares = width_total(jnp.sum(values * values, axis=1))
    factor = lax.rsqrt(squares[:, None] / MODEL_WIDTH + EPS_NORM)
    normed = values * factor
    return ((normed * gain_row).astype(jnp.bfloat16), normed, factor)


def rms_backward(grad_normed, normed, factor, gain_row):
    weighted = grad_normed * gain_row
    inner_sum = width_total(jnp.sum(weighted * normed, axis=1))
    grad_input = factor * (weighted - normed * (inner_sum[:, None] / MODEL_WIDTH))
    return (grad_input, jnp.sum(grad_normed * normed, axis=0))


def attend_sequence(
    heads_of_queries, heads_of_keys, heads_of_values, prefix_length, rows_per_block
):
    length = heads_of_keys.shape[0]
    key_place = jnp.arange(length)

    def one_block(inputs):
        query_block, positions = inputs
        scores = jnp.einsum(
            "qhgd,khd->hgqk", query_block, heads_of_keys, preferred_element_type=jnp.float32
        )
        visible = (key_place[None, :] <= positions[:, None]) | (key_place[None, :] < prefix_length)
        scores = jnp.where(visible, scores, -1e30)
        row_max = jnp.max(scores, axis=-1, keepdims=True)
        exponent = jnp.exp(scores - row_max)
        total_sum = jnp.sum(exponent, axis=-1, keepdims=True)
        probability = (exponent / total_sum).astype(jnp.bfloat16)
        result = jnp.einsum(
            "hgqk,khd->qhgd", probability, heads_of_values, preferred_element_type=jnp.float32
        )
        return (result, row_max[..., 0] + jnp.log(total_sum[..., 0]))

    block_count = length // rows_per_block
    shaped = heads_of_queries.reshape((block_count, rows_per_block) + heads_of_queries.shape[1:])
    positions = jnp.arange(length).reshape(block_count, rows_per_block)
    result, logsum = lax.map(one_block, (shaped, positions))
    return (result.reshape(heads_of_queries.shape), logsum)


def attend_back(
    heads_of_queries,
    heads_of_keys,
    heads_of_values,
    prefix_length,
    logsum,
    grad_heads,
    rows_per_block,
):
    length = heads_of_keys.shape[0]
    key_place = jnp.arange(length)
    block_count = length // rows_per_block

    def one_block(carried, inputs):
        query_block, grad_block, logsum_block, positions = inputs
        scores = jnp.einsum(
            "qhgd,khd->hgqk", query_block, heads_of_keys, preferred_element_type=jnp.float32
        )
        visible = (key_place[None, :] <= positions[:, None]) | (key_place[None, :] < prefix_length)
        scores = jnp.where(visible, scores, -1e30)
        probability = jnp.exp(scores - logsum_block[..., None])
        grad_prob = jnp.einsum(
            "qhgd,khd->hgqk", grad_block, heads_of_values, preferred_element_type=jnp.float32
        )
        delta_sum = jnp.sum(probability * grad_prob, axis=-1, keepdims=True)
        grad_scores = (probability * (grad_prob - delta_sum)).astype(jnp.bfloat16)
        grad_query = jnp.einsum(
            "hgqk,khd->qhgd", grad_scores, heads_of_keys, preferred_element_type=jnp.float32
        )
        grad_keys = jnp.einsum(
            "hgqk,qhgd->khd", grad_scores, query_block, preferred_element_type=jnp.float32
        )
        grad_values = jnp.einsum(
            "hgqk,qhgd->khd",
            probability.astype(jnp.bfloat16),
            grad_block,
            preferred_element_type=jnp.float32,
        )
        return ((carried[0] + grad_keys, carried[1] + grad_values), grad_query)

    block_shape = (block_count, rows_per_block) + heads_of_queries.shape[1:]
    initial = (
        jnp.zeros(heads_of_keys.shape, jnp.float32),
        jnp.zeros(heads_of_values.shape, jnp.float32),
    )
    positions = jnp.arange(length).reshape(block_count, rows_per_block)
    inputs = (
        heads_of_queries.reshape(block_shape),
        grad_heads.reshape(block_shape),
        logsum,
        positions,
    )
    (grad_keys, grad_values), grad_query = lax.scan(one_block, initial, inputs)
    return (grad_query.reshape(heads_of_queries.shape), grad_keys, grad_values)


def adam(weight, gradient, moment_one, moment_two, decay_rate, learn_rate):
    moment_new = BETA_ONE * moment_one + (1.0 - BETA_ONE) * gradient
    square_new = BETA_TWO * moment_two + (1.0 - BETA_TWO) * gradient * gradient
    moment_hat = moment_new / (1.0 - BETA_ONE**STEP)
    square_hat = square_new / (1.0 - BETA_TWO**STEP)
    return (
        weight
        - learn_rate * (moment_hat / (jnp.sqrt(square_hat) + ADAM_EPS) + decay_rate * weight),
        square_new,
    )


def shards(
    tokens,
    cotangent,
    prefix,
    query_weight,
    key_projection,
    value_projection,
    out_weight,
    gate_weight,
    up_weight,
    down_weight,
    norm_gains,
    query_moment,
    key_first_moment,
    value_first_moment,
    out_moment,
    gate_moment,
    up_moment,
    down_moment,
    gains_moment,
    query_square,
    key_second_moment,
    value_second_moment,
    out_square,
    gate_square,
    up_square,
    down_square,
    gains_square,
):
    tok_rows = tokens.shape[0]
    query_cols = query_weight.shape[1]
    kv_all = key_projection.shape[1]
    ffn_cols = gate_weight.shape[1]
    row_size = lax.axis_size("row")
    col_size = lax.axis_size("col")
    row_index = lax.axis_index("row")
    col_index = lax.axis_index("col")
    tok_count = tok_rows * col_size
    seq_count = prefix.shape[0]
    group_width = QUERY_HEADS // KEY_VALUE_HEADS
    rows_per_block = min(512, SEQUENCE_LENGTH)
    col_heads = query_cols // HEAD_SIZE
    frame_used = max(1, col_heads // group_width)
    frame_start = col_index * col_heads // group_width
    frame_width = frame_used * HEAD_SIZE
    key_here = lax.dynamic_slice_in_dim(key_projection, frame_start * HEAD_SIZE, frame_width, 1)
    value_here = lax.dynamic_slice_in_dim(value_projection, frame_start * HEAD_SIZE, frame_width, 1)
    query_mat = query_weight.astype(jnp.bfloat16)
    kv_mat = (
        jnp.stack([key_here, value_here], axis=1)
        .astype(jnp.bfloat16)
        .reshape(key_here.shape[0], 2 * frame_width)
    )
    out_mat = out_weight.astype(jnp.bfloat16)
    ffn_mat = (
        jnp.stack([gate_weight, up_weight], axis=1)
        .astype(jnp.bfloat16)
        .reshape(gate_weight.shape[0], 2 * ffn_cols)
    )
    down_mat = down_weight.astype(jnp.bfloat16)
    gain_one = norm_gains[0]
    gain_two = norm_gains[1]
    query_use, kv_use, ffn_use, out_use, down_use = fetch_weights(
        query_mat, kv_mat, ffn_mat, out_mat, down_mat
    )
    use_rows = tok_count // row_size
    seq_use = seq_count // row_size
    prefix_use = lax.dynamic_slice_in_dim(prefix, row_index * seq_use, seq_use, 0)
    kv_used = max(1, col_heads // group_width)
    group_here = col_heads // kv_used
    cosine_one, sine_one = rope_tables(SEQUENCE_LENGTH)
    cosine_table = jnp.tile(cosine_one, (seq_use, 1))
    sine_table = jnp.tile(sine_one, (seq_use, 1))

    def spread(values):
        return enter_rows(values)

    def to_tokens(product_fn):
        whole = leave_rows(product_fn(0, use_rows))

        def term(start_row, rows_here):
            return whole

        return sum_tokens(term, tok_rows)

    input_float = tokens.astype(jnp.float32)
    hidden_first, normed_one, factor_one = rms_forward(input_float, gain_one)
    h_one_use = spread(gather_tokens(hidden_first))
    query_sum = matrix_multiply(h_one_use, query_use)
    kv_frame = matrix_multiply(h_one_use, kv_use).reshape(use_rows, 2, frame_width)
    query_round = (
        rope(query_sum.reshape(use_rows, col_heads, HEAD_SIZE), cosine_table, sine_table)
        * ATTN_SCALE
    ).astype(jnp.bfloat16)
    key_round = rope(
        kv_frame[:, 0].reshape(use_rows, kv_used, HEAD_SIZE), cosine_table, sine_table
    ).astype(jnp.bfloat16)
    value_round = kv_frame[:, 1].reshape(use_rows, kv_used, HEAD_SIZE).astype(jnp.bfloat16)
    query_seq = query_round.reshape(seq_use, SEQUENCE_LENGTH, kv_used, group_here, HEAD_SIZE)
    key_seq = key_round.reshape(seq_use, SEQUENCE_LENGTH, kv_used, HEAD_SIZE)
    value_seq = value_round.reshape(seq_use, SEQUENCE_LENGTH, kv_used, HEAD_SIZE)

    def forward_sequence(inputs):
        return attend_sequence(inputs[0], inputs[1], inputs[2], inputs[3], rows_per_block)

    attended, logsum = lax.map(forward_sequence, (query_seq, key_seq, value_seq, prefix_use))
    head_round = attended.reshape(use_rows, col_heads * HEAD_SIZE).astype(jnp.bfloat16)

    def out_term(start_row, rows_here):
        return matrix_multiply(head_round, out_use)

    residual_mid = input_float + RESID * to_tokens(out_term)
    h_two, normed_two, factor_two = rms_forward(residual_mid, gain_two)
    h_two_use = spread(gather_tokens(h_two))
    ffn_part = matrix_multiply(h_two_use, ffn_use).reshape(use_rows, 2, ffn_cols)
    gate_value = ffn_part[:, 0]
    up_value = ffn_part[:, 1]
    hidden = (jax.nn.silu(gate_value) * up_value).astype(jnp.bfloat16)

    def down_term(start_row, rows_here):
        return matrix_multiply(hidden, down_use)

    layer_out = (residual_mid + RESID * to_tokens(down_term)).astype(jnp.bfloat16)
    grad_output = cotangent.astype(jnp.float32)
    grad_mlp = (RESID * grad_output).astype(jnp.bfloat16)
    grad_mlp_use = spread(gather_tokens(grad_mlp))
    down_local = left_product(hidden, grad_mlp_use)
    hidden_part = right_product(grad_mlp_use, down_use)
    sigmoid_gate = jax.nn.sigmoid(gate_value)
    grad_gate = hidden_part * up_value * sigmoid_gate * (1.0 + gate_value * (1.0 - sigmoid_gate))
    grad_up = hidden_part * (gate_value * sigmoid_gate)
    grad_pair = jnp.stack([grad_gate, grad_up], axis=1).astype(jnp.bfloat16)
    pair_flat = grad_pair.reshape(use_rows, 2 * ffn_cols)
    ffn_local = left_product(h_two_use, pair_flat).reshape(-1, 2, ffn_cols)

    def ffn_back_term(start_row, rows_here):
        return right_product(pair_flat, ffn_use)

    grad_mid_part, gain_two_part = rms_backward(
        to_tokens(ffn_back_term), normed_two, factor_two, gain_two
    )
    grad_mid = grad_output + grad_mid_part
    grad_attended = (RESID * grad_mid).astype(jnp.bfloat16)
    grad_attended_use = spread(gather_tokens(grad_attended))
    out_local = left_product(head_round, grad_attended_use)
    head_part = right_product(grad_attended_use, out_use)
    head_grad = head_part
    head_grad = head_grad.astype(jnp.bfloat16).reshape(
        seq_use, SEQUENCE_LENGTH, kv_used, group_here, HEAD_SIZE
    )

    def backward_sequence(inputs):
        return attend_back(
            inputs[0], inputs[1], inputs[2], inputs[3], inputs[4], inputs[5], rows_per_block
        )

    query_back, key_back, value_back = lax.map(
        backward_sequence, (query_seq, key_seq, value_seq, prefix_use, logsum, head_grad)
    )
    query_grad_heads = rope_back(
        query_back.reshape(use_rows, col_heads, HEAD_SIZE) * ATTN_SCALE, cosine_table, sine_table
    )
    query_grad_round = query_grad_heads.reshape(use_rows, col_heads * HEAD_SIZE).astype(
        jnp.bfloat16
    )
    key_grad_heads = rope_back(
        key_back.reshape(use_rows, kv_used, HEAD_SIZE), cosine_table, sine_table
    )
    kv_grad_used = jnp.stack(
        [
            key_grad_heads.reshape(use_rows, kv_used * HEAD_SIZE),
            value_back.reshape(use_rows, kv_used * HEAD_SIZE),
        ],
        axis=1,
    )
    kv_grad = kv_grad_used.astype(jnp.bfloat16)
    kv_flat = kv_grad.reshape(use_rows, 2 * frame_width)
    query_local = left_product(h_one_use, query_grad_round)
    kv_frame_local = left_product(h_one_use, kv_flat).reshape(-1, 2, frame_width)
    kv_local = lax.dynamic_update_slice_in_dim(
        jnp.zeros((kv_frame_local.shape[0], 2, kv_all), jnp.float32),
        kv_frame_local,
        frame_start * HEAD_SIZE,
        2,
    )

    def input_term(start_row, rows_here):
        return right_product(query_grad_round, query_use) + right_product(kv_flat, kv_use)

    grad_in_part, gain_one_part = rms_backward(
        to_tokens(input_term), normed_one, factor_one, gain_one
    )
    input_grad = (grad_mid + grad_in_part).astype(jnp.bfloat16)
    local_grads = reduce_rows(query_local, kv_local, out_local, ffn_local, down_local)
    summed = (
        lax.psum(local_grads[0].astype(jnp.bfloat16), "dp").astype(jnp.float32),
        lax.psum(local_grads[2].astype(jnp.bfloat16), "dp").astype(jnp.float32),
        lax.psum(local_grads[3].astype(jnp.bfloat16), "dp").astype(jnp.float32),
        lax.psum(local_grads[4].astype(jnp.bfloat16), "dp").astype(jnp.float32),
    )
    kv_summed, gains_total = lax.psum(
        (local_grads[1], jnp.stack([gain_one_part, gain_two_part])), ("dp", "col")
    )
    raw_grads = (
        summed[0],
        kv_summed[:, 0],
        kv_summed[:, 1],
        summed[1],
        summed[2][:, 0],
        summed[2][:, 1],
        summed[3],
    )
    masters = (
        query_weight,
        key_projection,
        value_projection,
        out_weight,
        gate_weight,
        up_weight,
        down_weight,
    )
    moments = (
        query_moment,
        key_first_moment,
        value_first_moment,
        out_moment,
        gate_moment,
        up_moment,
        down_moment,
    )
    squares = (
        query_square,
        key_second_moment,
        value_second_moment,
        out_square,
        gate_square,
        up_square,
        down_square,
    )
    copied_sum = jnp.sum(gains_total * gains_total) + jnp.sum(kv_summed * kv_summed)
    square_local = jnp.where(col_index == 0, copied_sum, 0.0)
    for position in (0, 3, 4, 5, 6):
        square_local = square_local + jnp.sum(raw_grads[position] * raw_grads[position])
    total_sum = lax.psum(square_local, ("row", "col"))
    grad_norm = jnp.sqrt(total_sum)
    factor = jnp.minimum(1.0, CLIP / grad_norm)
    clipped = []
    nexts = []
    variances = []
    for position in range(7):
        gradient = raw_grads[position] * factor
        weight_next, variance = adam(
            masters[position], gradient, moments[position], squares[position], DECAY, LEARN
        )
        clipped.append(gradient)
        nexts.append(weight_next)
        variances.append(variance)
    gains_grad = gains_total * factor
    gains_next, gains_variance = adam(
        norm_gains, gains_grad, gains_moment, gains_square, 0.0, GAINS_LEARN
    )
    return (
        layer_out,
        input_grad,
        clipped[0],
        clipped[1],
        clipped[2],
        clipped[3],
        clipped[4],
        clipped[5],
        clipped[6],
        gains_grad,
        nexts[0],
        nexts[1],
        nexts[2],
        nexts[3],
        nexts[4],
        nexts[5],
        nexts[6],
        gains_next,
        variances[0],
        variances[1],
        variances[2],
        variances[3],
        variances[4],
        variances[5],
        variances[6],
        gains_variance,
        grad_norm,
    )


LOW = jnp.bfloat16
WIDE = jnp.float32
CHUNK = 512
LANES = 128
MASKED = -1e30
VMEM_BYTES = 48 * 1024 * 1024


def swaps_fit(mesh):
    return dict(mesh.shape) == {"dp": 4, "row": 2, "col": 4}


def swap(values, axis, bit):
    size = lax.axis_size(axis)
    return lax.ppermute(values, axis, [(place, place ^ bit) for place in range(size)])


def swap_core(values):
    return swap(values, "dp", 1)


def swap_y(values):
    return swap(values, "dp", 2)


def swap_x(values):
    return swap(values, "row", 1)


def swap_near(values):
    return swap(values, "col", 1)


def swap_far(values):
    return swap(values, "col", 2)


def swap_corner(values):
    cols = lax.axis_size("col")
    pairs = [
        (row * cols + col, (row ^ 1) * cols + (col ^ 1))
        for row in range(lax.axis_size("row"))
        for col in range(cols)
    ]
    return lax.ppermute(values, ("row", "col"), pairs)


def after(value, *others):
    return lax.optimization_barrier((value,) + others)[0]


def fold(kept, sent, move):
    return kept + move(sent.astype(LOW)).astype(WIDE)


def in_order(place, own, other, axis):
    return jnp.concatenate(
        [jnp.where(place == 0, own, other), jnp.where(place == 0, other, own)], axis=axis
    )


def cut(values, start, size, axis):
    return lax.dynamic_slice_in_dim(values, start, size, axis)


def partner_lanes(values):
    lane = lax.broadcasted_iota(jnp.int32, values.shape, 1)
    half = HEAD_SIZE // 2
    ahead = pltpu.roll(values, values.shape[1] - half, 1)
    behind = pltpu.roll(values, half, 1)
    return jnp.where(lane % HEAD_SIZE < half, ahead, behind)


def first_lanes(shape):
    return lax.broadcasted_iota(jnp.int32, shape, 1) < HEAD_SIZE


def dot_nt(left_side, right_side):
    return lax.dot_general(
        left_side, right_side, (((1,), (1,)), ((), ())), preferred_element_type=WIDE
    )


def dot_tn(left_side, right_side):
    return lax.dot_general(
        left_side, right_side, (((0,), (0,)), ((), ())), preferred_element_type=WIDE
    )


WIDE_BLOCK = 512
COST_SHARE = 1


def one_buffer(shape, index_map):
    return pl.BlockSpec(shape, index_map, pipeline_mode=pl.Buffered(1))


def cost(flops, read, written):
    return pl.CostEstimate(
        flops=int(flops * COST_SHARE),
        bytes_accessed=int(2 * (read + written) * COST_SHARE),
        transcendentals=0,
    )


def mm(left_side, right_side):
    return jnp.dot(left_side, right_side, preferred_element_type=WIDE)


def both(refs, axis):
    return jnp.concatenate([ref[...] for ref in refs], axis=axis)


def flat(*blocks):
    return [array for block in blocks for array in block]


def both_of(refs, which, axis):
    return jnp.concatenate([ref[which] for ref in refs], axis=axis)


def hidden_kernel(normed_ref, *refs):
    hidden_ref, gate_ref, up_ref = refs[4:]
    half = normed_ref.shape[1] // 2
    left, right = normed_ref[:, :half], normed_ref[:, half:]
    gate = mm(left, both_of(refs[0:2], 0, 1)) + mm(right, both_of(refs[2:4], 0, 1))
    up = mm(left, both_of(refs[0:2], 1, 1)) + mm(right, both_of(refs[2:4], 1, 1))
    hidden_ref[...] = (gate * jax.nn.sigmoid(gate) * up).astype(LOW)
    gate_ref[...] = gate.astype(LOW)
    up_ref[...] = up.astype(LOW)


def hidden_units(normed, pairs):
    tokens, width = normed.shape
    weights = flat(*pairs)
    units = 2 * weights[0].shape[2]
    block = WIDE_BLOCK
    weight = one_buffer(weights[0].shape, lambda i: (0, 0, 0))
    out = pl.BlockSpec((block, units), lambda i: (i, 0))
    return pl.pallas_call(
        hidden_kernel,
        grid=(tokens // block,),
        in_specs=[pl.BlockSpec((block, width), lambda i: (i, 0))] + [weight] * 4,
        out_specs=[out] * 3,
        out_shape=[jax.ShapeDtypeStruct((tokens, units), LOW)] * 3,
        compiler_params=pltpu.CompilerParams(vmem_limit_bytes=VMEM_BYTES),
        cost_estimate=cost(
            4 * tokens * width * units, tokens * width + 2 * width * units, 3 * tokens * units
        ),
    )(normed, *weights)


def down_kernel(h0, h1, *refs):
    weights, outs = refs[:8], refs[8:]
    half = weights[0].shape[1]
    for at, out_ref in enumerate(outs):

        @pl.when(pl.program_id(0) == at)
        def _(out_ref=out_ref):
            for side in range(2):
                total = mm(h0[...], both(weights[2 * side : 2 * side + 2], 0))
                total = total + mm(h1[...], both(weights[4 + 2 * side : 6 + 2 * side], 0))
                out_ref[:, side * half : (side + 1) * half] = total.astype(LOW)


def down_units(hidden, down):
    tokens, units = hidden[0].shape
    weights = flat(*down[0], *down[1])
    half = weights[0].shape[1]
    block = WIDE_BLOCK
    weight = one_buffer(weights[0].shape, lambda i: (0, 0))
    left = pl.BlockSpec((block, units), lambda i: (i, 0))
    return pl.pallas_call(
        down_kernel,
        grid=(tokens // block,),
        in_specs=[left] * 2 + [weight] * 8,
        out_specs=[one_buffer((block, 2 * half), lambda i: (0, 0))] * (tokens // block),
        out_shape=[jax.ShapeDtypeStruct((block, 2 * half), LOW)] * (tokens // block),
        compiler_params=pltpu.CompilerParams(vmem_limit_bytes=VMEM_BYTES),
        cost_estimate=cost(
            8 * tokens * units * half, 2 * tokens * units + 4 * units * half, 2 * tokens * half
        ),
    )(*hidden, *weights)


def hidden_back_kernel(grad_ref, d0, d1, d2, d3, gate_ref, up_ref, grad_gate_ref, grad_up_ref):
    half = d0.shape[1]
    part = dot_nt(grad_ref[:, :half], both((d0, d1), 0))
    part = part + dot_nt(grad_ref[:, half:], both((d2, d3), 0))
    gate = gate_ref[...].astype(WIDE)
    up = up_ref[...].astype(WIDE)
    sigmoid = jax.nn.sigmoid(gate)
    grad_gate_ref[...] = (part * up * sigmoid * (1.0 + gate * (1.0 - sigmoid))).astype(LOW)
    grad_up_ref[...] = (part * (gate * sigmoid)).astype(LOW)


def hidden_back(grads, down, gate, up):
    tokens, width = grads.shape
    weights = flat(*down)
    units = 2 * weights[0].shape[0]
    block = WIDE_BLOCK
    weight = one_buffer(weights[0].shape, lambda i: (0, 0))
    row = pl.BlockSpec((block, units), lambda i: (i, 0))
    return pl.pallas_call(
        hidden_back_kernel,
        grid=(tokens // block,),
        in_specs=[pl.BlockSpec((block, width), lambda i: (i, 0))] + [weight] * 4 + [row] * 2,
        out_specs=[row] * 2,
        out_shape=[jax.ShapeDtypeStruct((tokens, units), LOW)] * 2,
        compiler_params=pltpu.CompilerParams(vmem_limit_bytes=VMEM_BYTES),
        cost_estimate=cost(
            2 * tokens * width * units,
            tokens * width + width * units + 2 * tokens * units,
            2 * tokens * units,
        ),
    )(grads, *weights, gate, up)


def normed_back_kernel(a0, a1, b0, b1, *refs):
    weights, outs = refs[:8], refs[8:]
    half = weights[0].shape[1]
    for at, out_ref in enumerate(outs):

        @pl.when(pl.program_id(0) == at)
        def _(out_ref=out_ref):
            for side in range(2):
                total = jnp.zeros((a0.shape[0], half), WIDE)
                for which, lefts in enumerate(((a0, b0), (a1, b1))):
                    start = 4 * which + 2 * side
                    for kind, left in enumerate(lefts):
                        right = both_of(weights[start : start + 2], kind, 1)
                        total = total + dot_nt(left[...], right)
                out_ref[:, side * half : (side + 1) * half] = total.astype(LOW)


def normed_back(grad_gate, grad_up, pairs):
    tokens, units = grad_gate[0].shape
    weights = flat(*pairs[0], *pairs[1])
    half = weights[0].shape[1]
    block = WIDE_BLOCK
    weight = one_buffer(weights[0].shape, lambda i: (0, 0, 0))
    left = pl.BlockSpec((block, units), lambda i: (i, 0))
    return pl.pallas_call(
        normed_back_kernel,
        grid=(tokens // block,),
        in_specs=[left] * 4 + [weight] * 8,
        out_specs=[one_buffer((block, 2 * half), lambda i: (0, 0))] * (tokens // block),
        out_shape=[jax.ShapeDtypeStruct((block, 2 * half), LOW)] * (tokens // block),
        compiler_params=pltpu.CompilerParams(vmem_limit_bytes=VMEM_BYTES),
        cost_estimate=cost(
            16 * tokens * units * half, 4 * tokens * units + 8 * units * half, 2 * tokens * half
        ),
    )(*grad_gate, *grad_up, *weights)


def weight_grad(lefts, place, rights, columns):
    count, tokens, parts = len(rights), lefts[0].shape[0], len(lefts)
    span = rights[0][0].shape[1]
    block = WIDE_BLOCK

    def kernel(*refs):
        left_refs, out_ref = refs[:parts], refs[-1]
        for at in range(count):
            right_refs = refs[parts * (at + 1) : parts * (at + 2)]
            total = dot_tn(left_refs[0][...], right_refs[0][...])
            for left_ref, right_ref in zip(left_refs[1:], right_refs[1:]):
                total = total + dot_tn(left_ref[...], right_ref[...])
            out_ref[:, at * span : (at + 1) * span] = total.astype(LOW)

    start = place * columns // block
    return pl.pallas_call(
        kernel,
        grid=(columns // block,),
        in_specs=[pl.BlockSpec((tokens, block), lambda i: (0, i + start))] * parts
        + [one_buffer((tokens, span), lambda i: (0, 0))] * (count * parts),
        out_specs=pl.BlockSpec((block, count * span), lambda i: (i, 0)),
        out_shape=jax.ShapeDtypeStruct((columns, count * span), LOW),
        compiler_params=pltpu.CompilerParams(vmem_limit_bytes=VMEM_BYTES),
        cost_estimate=cost(
            2 * count * parts * tokens * columns * span,
            parts * tokens * (columns + count * span),
            count * columns * span,
        ),
    )(*lefts, *[value for right in rights for value in right])


def project_kernel(
    normed_ref, own_ref, kv_ref, first_ref, second_ref, kv_other_ref, cosine_ref, sine_ref, out_ref
):
    half = own_ref.shape[1]
    near_rows = jnp.concatenate([own_ref[0], kv_ref[0]], axis=1)
    other_rows = jnp.concatenate([first_ref[0], second_ref[0], kv_other_ref[0]], axis=1)
    product = mm(normed_ref[0, :, :half], near_rows) + mm(normed_ref[0, :, half:], other_rows)
    cosine = cosine_ref[0]
    sine = sine_ref[0]
    for tile in range(3):
        part = product[:, tile * LANES : (tile + 1) * LANES]
        turned = part * cosine + partner_lanes(part) * sine
        if tile < 2:
            turned = turned * ATTN_SCALE
        else:
            turned = jnp.where(first_lanes(part.shape), turned, part)
        out_ref[0, 0, :, tile * LANES : (tile + 1) * LANES] = turned.astype(LOW)


def piece_specs(pieces):
    return [pl.BlockSpec((1,) + piece.shape[1:], lambda j, i: (j, 0, 0)) for piece in pieces]


def project(normed, pieces, cosine, sine):
    groups = 4
    wide = 3 * LANES
    table = pl.BlockSpec((1, CHUNK, LANES), lambda j, i: (0, 0, 0))
    return pl.pallas_call(
        project_kernel,
        grid=(groups, 2),
        in_specs=[pl.BlockSpec((1, CHUNK, MODEL_WIDTH), lambda j, i: (i, 0, 0))]
        + piece_specs(pieces)
        + [table, table],
        out_specs=pl.BlockSpec((1, 1, CHUNK, wide), lambda j, i: (j, i, 0, 0)),
        out_shape=jax.ShapeDtypeStruct((groups, 2, CHUNK, wide), LOW),
        compiler_params=pltpu.CompilerParams(vmem_limit_bytes=VMEM_BYTES),
        cost_estimate=cost(
            2 * CHUNK * MODEL_WIDTH * groups * wide, MODEL_WIDTH * (CHUNK + groups * wide), 0
        ),
    )(normed, *pieces, cosine, sine)


def project_back_kernel(
    grad_ref, own_ref, kv_ref, first_ref, second_ref, kv_other_ref, out_ref, acc
):
    group, tokens = pl.program_id(0), pl.program_id(1)
    half = own_ref.shape[1]

    @pl.when(group == 0)
    def _():
        acc[tokens] = jnp.zeros(acc.shape[1:], WIDE)

    near_rows = jnp.concatenate([own_ref[0], kv_ref[0]], axis=1)
    other_rows = jnp.concatenate([first_ref[0], second_ref[0], kv_other_ref[0]], axis=1)
    acc[tokens, :, :half] += dot_nt(grad_ref[0], near_rows)
    acc[tokens, :, half:] += dot_nt(grad_ref[0], other_rows)

    @pl.when(group == pl.num_programs(0) - 1)
    def _():
        out_ref[tokens] = acc[tokens].astype(LOW)


def project_back(grads, pieces):
    groups = 4
    wide = 3 * LANES
    return pl.pallas_call(
        project_back_kernel,
        grid=(groups, 2),
        in_specs=[pl.BlockSpec((1, CHUNK, wide), lambda j, i: (i, 0, j))] + piece_specs(pieces),
        out_specs=pl.BlockSpec((2, CHUNK, MODEL_WIDTH), lambda j, i: (0, 0, 0)),
        out_shape=jax.ShapeDtypeStruct((2, CHUNK, MODEL_WIDTH), LOW),
        scratch_shapes=[pltpu.VMEM((2, CHUNK, MODEL_WIDTH), WIDE)],
        compiler_params=pltpu.CompilerParams(vmem_limit_bytes=VMEM_BYTES),
        cost_estimate=cost(
            2 * CHUNK * MODEL_WIDTH * groups * wide, MODEL_WIDTH * (CHUNK + groups * wide), 0
        ),
    )(grads, *pieces)


def split_heads(tiles, lanes_from):
    heads = []
    for head in range(4):
        tile = tiles[:, (head // 2) * LANES : (head // 2 + 1) * LANES].astype(WIDE)
        if (head % 2) * HEAD_SIZE != lanes_from:
            tile = pltpu.roll(tile, HEAD_SIZE, 1)
        low = first_lanes(tile.shape)
        heads.append(jnp.where(low if lanes_from == 0 else ~low, tile, 0.0).astype(LOW))
    return heads


def join_heads(heads, lanes_from):
    tiles = []
    for pair in range(2):
        even, odd = heads[2 * pair], heads[2 * pair + 1]
        if lanes_from == 0:
            odd = pltpu.roll(odd, HEAD_SIZE, 1)
        else:
            even = pltpu.roll(even, HEAD_SIZE, 1)
        tiles.append(jnp.where(first_lanes(even.shape), even, odd))
    return tiles


def visible_chunks(chunk, prefix):
    whole = jnp.maximum(chunk, prefix // CHUNK)
    some = jnp.maximum(chunk + 1, (prefix + CHUNK - 1) // CHUNK)
    return whole, some


def attend_kernel(place_ref, q_ref, kv_ref, *rest):
    o_ref, lse_ref, heads, top, total, acc = rest[-6:]
    place = place_ref[0]
    prefix = place_ref[1 + pl.program_id(0)]
    chunk = pl.program_id(1) ^ place
    for head, tile in enumerate(split_heads(q_ref[0, 0], 0)):
        heads[head] = tile
        top[head] = jnp.full((CHUNK, LANES), MASKED, WIDE)
        total[head] = jnp.zeros((CHUNK, LANES), WIDE)
        acc[head] = jnp.zeros((CHUNK, LANES), WIDE)

    def step(masked, other, carry):
        kv = kv_ref[other ^ place, 0]
        if masked:
            row = lax.broadcasted_iota(jnp.int32, (CHUNK, CHUNK), 0) + chunk * CHUNK
            key = lax.broadcasted_iota(jnp.int32, (CHUNK, CHUNK), 1) + other * CHUNK
            visible = key <= jnp.maximum(row, prefix - 1)
        for head in range(4):
            scores = dot_nt(heads[head], kv)
            if masked:
                scores = jnp.where(visible, scores, MASKED)
            old = top[head]
            new = jnp.maximum(old, jnp.max(scores, axis=1, keepdims=True))
            exponent = jnp.exp(scores - new[:, :1])
            shrink = jnp.exp(old - new)
            top[head] = new
            total[head] = total[head] * shrink + jnp.sum(exponent, axis=1, keepdims=True)
            acc[head] = acc[head] * shrink + jnp.dot(
                exponent.astype(LOW), kv, preferred_element_type=WIDE
            )
        return carry

    whole, some = visible_chunks(chunk, prefix)
    lax.fori_loop(0, whole, functools.partial(step, False), 0)
    lax.fori_loop(whole, some, functools.partial(step, True), 0)
    lane = lax.broadcasted_iota(jnp.int32, (CHUNK, LANES), 1)
    logs = jnp.zeros((CHUNK, LANES), WIDE)
    results = []
    for head in range(4):
        results.append(acc[head] / total[head])
        logs = jnp.where(lane == head, top[head] + jnp.log(total[head]), logs)
    lse_ref[0, 0] = jnp.transpose(logs)[:8]
    for pair, tile in enumerate(join_heads(results, HEAD_SIZE)):
        o_ref[0, 0, :, pair * LANES : (pair + 1) * LANES] = tile.astype(LOW)


def attend(spot, packed, holds=()):
    units = 2 * 4 * 10
    return pl.pallas_call(
        attend_kernel,
        grid_spec=pltpu.PrefetchScalarGridSpec(
            num_scalar_prefetch=1,
            grid=(2, 4),
            in_specs=[
                pl.BlockSpec((1, 1, CHUNK, 2 * LANES), lambda i, j, *_: (j, i, 0, 0)),
                pl.BlockSpec((4, 1, CHUNK, LANES), lambda i, j, *_: (0, i, 0, 2)),
            ]
            + [pl.BlockSpec(memory_space=pl.ANY)] * len(holds),
            out_specs=[
                pl.BlockSpec((1, 1, CHUNK, 2 * LANES), lambda i, j, *_: (j, i, 0, 0)),
                pl.BlockSpec((1, 1, 8, CHUNK), lambda i, j, *_: (j, i, 0, 0)),
            ],
            scratch_shapes=[
                pltpu.VMEM((4, CHUNK, LANES), LOW),
                pltpu.VMEM((4, CHUNK, LANES), WIDE),
                pltpu.VMEM((4, CHUNK, LANES), WIDE),
                pltpu.VMEM((4, CHUNK, LANES), WIDE),
            ],
        ),
        out_shape=[
            jax.ShapeDtypeStruct((4, 2, CHUNK, 2 * LANES), LOW),
            jax.ShapeDtypeStruct((4, 2, 8, CHUNK), WIDE),
        ],
        compiler_params=pltpu.CompilerParams(vmem_limit_bytes=VMEM_BYTES),
        cost_estimate=pl.CostEstimate(
            flops=int(units * 4 * CHUNK * CHUNK * 256 * 2 * 2 * COST_SHARE),
            bytes_accessed=1024 * 1024,
            transcendentals=0,
        ),
    )(spot, packed, packed, *holds)


def attend_back_kernel(
    sequence, place_ref, q_ref, kv_ref, o_ref, do_ref, lse_ref, cosine_ref, sine_ref, *rest
):
    out_ref, heads, grads, deltas, q_acc, kv_acc = rest[-6:]
    slot = pl.program_id(0)
    place = place_ref[0]
    prefix = place_ref[1 + sequence]
    chunk = slot ^ place

    @pl.when(slot == 0)
    def _():
        kv_acc[...] = jnp.zeros_like(kv_acc)

    ones = jnp.ones((8, LANES), WIDE)
    out_heads = split_heads(o_ref[0, 0], HEAD_SIZE)
    grad_heads = split_heads(do_ref[0, 0], HEAD_SIZE)
    for head, tile in enumerate(split_heads(q_ref[0, 0], 0)):
        heads[head] = tile
        grads[head] = grad_heads[head]
        product = out_heads[head].astype(WIDE) * grad_heads[head].astype(WIDE)
        deltas[head] = lax.dot_general(
            ones,
            product,
            (((1,), (1,)), ((), ())),
            precision=lax.Precision.HIGHEST,
            preferred_element_type=WIDE,
        )
        q_acc[head] = jnp.zeros((CHUNK, LANES), WIDE)

    def step(masked, other, carry):
        other_slot = other ^ place
        kv = kv_ref[other_slot, 0]
        if masked:
            key = lax.broadcasted_iota(jnp.int32, (CHUNK, CHUNK), 0) + other * CHUNK
            row = lax.broadcasted_iota(jnp.int32, (CHUNK, CHUNK), 1) + chunk * CHUNK
            visible = key <= jnp.maximum(row, prefix - 1)
        for head in range(4):
            scores = dot_nt(kv, heads[head])
            if masked:
                scores = jnp.where(visible, scores, MASKED)
            probability = jnp.exp(scores - lse_ref[0, 0, head : head + 1])
            grad_prob = dot_nt(kv, grads[head])
            grad_scores = (probability * (grad_prob - deltas[head][:1])).astype(LOW)
            kv_acc[other_slot] += jnp.dot(
                grad_scores, heads[head], preferred_element_type=WIDE
            ) + jnp.dot(probability.astype(LOW), grads[head], preferred_element_type=WIDE)
            q_acc[head] += dot_tn(grad_scores, kv)
        return carry

    whole, some = visible_chunks(chunk, prefix)
    lax.fori_loop(0, whole, functools.partial(step, False), 0)
    lax.fori_loop(whole, some, functools.partial(step, True), 0)
    cosine = cosine_ref[slot]
    sine = sine_ref[slot]
    for pair, tile in enumerate(join_heads([q_acc[head] for head in range(4)], 0)):
        tile = tile * ATTN_SCALE
        turned = tile * cosine + partner_lanes(tile * sine)
        out_ref[slot, :, pair * LANES : (pair + 1) * LANES] = turned.astype(LOW)

    @pl.when(slot == 3)
    def _():
        for other in range(4):
            tile = kv_acc[other]
            turned = tile * cosine_ref[other] + partner_lanes(tile * sine_ref[other])
            turned = jnp.where(first_lanes(tile.shape), turned, tile)
            out_ref[other, :, 2 * LANES :] = turned.astype(LOW)


def attend_grad(sequence, spot, packed, attended, grad_attended, logsum, cosine, sine, holds=()):
    units = 4 * 10
    tile = pl.BlockSpec((1, 1, CHUNK, 2 * LANES), lambda j, *_: (j, sequence, 0, 0))
    table = pl.BlockSpec((4, CHUNK, LANES), lambda j, *_: (0, 0, 0))
    return pl.pallas_call(
        functools.partial(attend_back_kernel, sequence),
        grid_spec=pltpu.PrefetchScalarGridSpec(
            num_scalar_prefetch=1,
            grid=(4,),
            in_specs=[
                tile,
                pl.BlockSpec((4, 1, CHUNK, LANES), lambda j, *_: (0, sequence, 0, 2)),
                tile,
                tile,
                pl.BlockSpec((1, 1, 8, CHUNK), lambda j, *_: (j, sequence, 0, 0)),
                table,
                table,
            ]
            + [pl.BlockSpec(memory_space=pl.ANY)] * len(holds),
            out_specs=pl.BlockSpec((4, CHUNK, 3 * LANES), lambda j, *_: (0, 0, 0)),
            scratch_shapes=[
                pltpu.VMEM((4, CHUNK, LANES), LOW),
                pltpu.VMEM((4, CHUNK, LANES), LOW),
                pltpu.VMEM((4, 8, CHUNK), WIDE),
                pltpu.VMEM((4, CHUNK, LANES), WIDE),
                pltpu.VMEM((4, CHUNK, LANES), WIDE),
            ],
        ),
        out_shape=jax.ShapeDtypeStruct((4, CHUNK, 3 * LANES), LOW),
        compiler_params=pltpu.CompilerParams(vmem_limit_bytes=VMEM_BYTES),
        cost_estimate=pl.CostEstimate(
            flops=int(units * 4 * CHUNK * CHUNK * 256 * 2 * 5 * COST_SHARE),
            bytes_accessed=1024 * 1024,
            transcendentals=0,
        ),
    )(spot, packed, packed, attended, grad_attended, logsum, cosine, sine, *holds)


def dp_spot(dp):
    return dp.reshape(1)


def step_kernel(spot_ref, factor_ref, grad_ref, weight_ref, moment_ref, square_ref, *outs):
    gradient = grad_ref[0].astype(WIDE) * factor_ref[0, 0]
    following, variance = adam(
        weight_ref[...], gradient, moment_ref[...], square_ref[...], DECAY, LEARN
    )
    outs[0][...] = gradient
    outs[1][...] = following
    outs[2][...] = variance


def step_weight(spot, factor, pieces, axis, weight, moment, square):
    count, rows, columns = pieces.shape
    block_rows = min(rows, (1 << 19) // columns)
    parts = rows // block_rows

    def piece_at(block, part, spot_ref):
        code = spot_ref[0]
        return (block ^ ((code % 2) * 2 + code // 2), part, 0)

    def weight_at(block, part, spot_ref):
        return (part, block) if axis == 1 else (block * parts + part, 0)

    spec = pl.BlockSpec((block_rows, columns), weight_at)
    return pl.pallas_call(
        step_kernel,
        grid_spec=pltpu.PrefetchScalarGridSpec(
            num_scalar_prefetch=1,
            grid=(count, parts),
            in_specs=[
                pl.BlockSpec(memory_space=pltpu.SMEM),
                pl.BlockSpec((1, block_rows, columns), piece_at),
                spec,
                spec,
                spec,
            ],
            out_specs=[spec] * 3,
        ),
        out_shape=[jax.ShapeDtypeStruct(weight.shape, WIDE)] * 3,
        compiler_params=pltpu.CompilerParams(vmem_limit_bytes=VMEM_BYTES),
        cost_estimate=pl.CostEstimate(
            flops=12 * weight.size, bytes_accessed=26 * weight.size, transcendentals=weight.size
        ),
    )(spot, factor, pieces, weight, moment, square)


def step_pair_kernel(spot_ref, factor_ref, grad_ref, *refs):
    core, start = spot_ref[0], spot_ref[1]
    factor = factor_ref[0, 0]
    for group in range(4):
        turned = group ^ start
        slot = turned // 2 + (turned % 2) * 2
        first = grad_ref[core * 4 + slot].astype(WIDE) * factor
        second = grad_ref[(1 - core) * 4 + slot].astype(WIDE) * factor
        low = first_lanes(first.shape)
        lanes = pl.ds(group * LANES, LANES)
        key_grad = jnp.where(low, first, pltpu.roll(second, HEAD_SIZE, 1))
        value_grad = jnp.where(low, pltpu.roll(first, HEAD_SIZE, 1), second)
        for gradient, at in ((key_grad, 0), (value_grad, 1)):
            weight_ref, moment_ref, square_ref = refs[3 * at : 3 * at + 3]
            following, variance = adam(
                weight_ref[:, lanes],
                gradient,
                moment_ref[:, lanes],
                square_ref[:, lanes],
                DECAY,
                LEARN,
            )
            outs = refs[6 + 3 * at : 9 + 3 * at]
            outs[0][:, lanes] = gradient
            outs[1][:, lanes] = following
            outs[2][:, lanes] = variance


def step_pair(spot, factor, pieces, key, value):
    rows, columns = key[0].shape
    block_rows = 128
    spec = pl.BlockSpec((block_rows, columns), lambda i, *_: (i, 0))
    outs = pl.pallas_call(
        step_pair_kernel,
        grid_spec=pltpu.PrefetchScalarGridSpec(
            num_scalar_prefetch=1,
            grid=(rows // block_rows,),
            in_specs=[
                pl.BlockSpec(memory_space=pltpu.SMEM),
                pl.BlockSpec((8, block_rows, LANES), lambda i, *_: (0, i, 0)),
            ]
            + [spec] * 6,
            out_specs=[spec] * 6,
        ),
        out_shape=[jax.ShapeDtypeStruct((rows, columns), WIDE)] * 6,
        compiler_params=pltpu.CompilerParams(vmem_limit_bytes=VMEM_BYTES),
        cost_estimate=pl.CostEstimate(
            flops=24 * rows * columns,
            bytes_accessed=52 * rows * columns,
            transcendentals=2 * rows * columns,
        ),
    )(spot, factor, pieces, *key, *value)
    return outs[:3], outs[3:]


def slot_tables(place):
    half = HEAD_SIZE // 2
    frequency = THETA ** (-(jnp.arange(half, dtype=WIDE) * 2.0 / HEAD_SIZE))
    chunk = jnp.arange(4, dtype=jnp.int32) ^ place
    position = (chunk[:, None] * CHUNK + jnp.arange(CHUNK)[None, :]).astype(WIDE)
    angles = position[:, :, None] * frequency[None, None, :]
    cosine, sine = jnp.cos(angles), jnp.sin(angles)
    return (
        jnp.concatenate([cosine] * 4, axis=2),
        jnp.concatenate([-sine, sine, -sine, sine], axis=2),
    )


def exchange(pieces):
    return [
        pieces[0],
        swap_x(pieces[1]),
        swap_near(pieces[2]),
        swap_corner(pieces[3]),
    ]


def rows_norm(values):
    factor = lax.rsqrt(
        jnp.sum(values * values, axis=1, keepdims=True) / MODEL_WIDTH + EPS_NORM
    )
    return values * factor, factor


def rows_norm_back(gradient, normed, factor, gain_row):
    weighted = gradient * gain_row
    inner = jnp.sum(weighted * normed, axis=1, keepdims=True) / MODEL_WIDTH
    return factor * (weighted - normed * inner), jnp.sum(gradient * normed, axis=0)


def swapped_shards(
    tokens,
    cotangent,
    prefix,
    query_weight,
    key_projection,
    value_projection,
    out_weight,
    gate_weight,
    up_weight,
    down_weight,
    norm_gains,
    query_moment,
    key_first_moment,
    value_first_moment,
    out_moment,
    gate_moment,
    up_moment,
    down_moment,
    gains_moment,
    query_square,
    key_second_moment,
    value_second_moment,
    out_square,
    gate_square,
    up_square,
    down_square,
    gains_square,
):
    row = lax.axis_index("row")
    col = lax.axis_index("col")
    dp = lax.axis_index("dp")
    core = dp % 2
    side = dp // 2
    near = col % 2
    far = col // 2
    place = near * 2 + row
    half_rows = tokens.shape[0] // 2
    half_width = tokens.shape[1]

    swapped = [1, 0, 3, 2]
    wide = 3 * LANES
    owner = [col ^ (2 * row), col ^ (2 - 2 * row), col ^ (1 + 2 * row), col ^ (3 - 2 * row)]

    def reorder(blocks):
        return jnp.stack([blocks[place_at] for place_at in swapped])

    def ordered_halves(matrix, axis):
        start = core * 2 * LANES
        return jnp.concatenate(
            [
                cut(matrix, start + side * LANES, LANES, axis),
                cut(matrix, start + (1 - side) * LANES, LANES, axis),
            ],
            axis=axis,
        ).astype(LOW)

    def halves_of(values):
        own = cut(values, row * half_rows, half_rows, 0)
        return own, cut(values, (1 - row) * half_rows, half_rows, 0)

    def leave(values, others):
        back = after(swap_x(after(values[:, half_width:], others[0])), others[1])
        return in_order(row, values[:, :half_width], back, 0)

    def add_low(kept, got):
        return (kept.astype(WIDE) + got.astype(WIDE)).astype(LOW)

    own_rows, other_rows = halves_of(tokens)
    got_rows = swap_x(other_rows)
    gains = jnp.concatenate([norm_gains, swap_x(norm_gains)], axis=1)
    prefixes = [prefix[far], swap_core(prefix)[far]]
    spot = jnp.stack([place, *prefixes])
    cosine, sine = slot_tables(place)

    def heads_of(matrix):
        return jnp.stack(
            [cut(matrix, (at * 2 + core) * HEAD_SIZE, HEAD_SIZE, 1) for at in owner]
        ).astype(LOW)

    kv_own = jnp.concatenate([heads_of(key_projection), heads_of(value_projection)], axis=2)
    kv_other = swap_x(reorder(kv_own))

    def far_pair(block, other):
        return jnp.stack([jnp.where(row == 0, block, other), jnp.where(row == 0, other, block)])

    units = gate_weight.shape[1] // 2

    def hidden_low(matrix, axis, which):
        start = core * units + (side if which == 0 else 1 - side) * (units // 2)
        return cut(matrix, start, units // 2, axis).astype(LOW)

    pair_own = [
        jnp.stack([hidden_low(gate_weight, 1, which), hidden_low(up_weight, 1, which)])
        for which in range(2)
    ]
    down_own = [hidden_low(down_weight, 0, which) for which in range(2)]
    q_low, o_low = ordered_halves(query_weight, 1), ordered_halves(out_weight, 0)

    q_far = swap_far(q_low)
    q_pair = after(far_pair(q_low, q_far), kv_other)
    q_near = swap_near(q_pair)
    q_pair_x = swap_x(jnp.stack([q_pair[1, :, :LANES], q_pair[0, :, :LANES]]))
    q_near_x = swap_near(after(q_pair_x, q_near))
    q_pair_y = swap_y(q_pair_x)
    pair_x = swap_x(after(pair_own[0], q_pair_x))
    q_near_y = swap_y(after(q_near_x, q_pair_y))
    o_far = swap_far(after(o_low, q_near_x))
    pair_far = swap_far(after(pair_own[0], o_far))
    o_pair = far_pair(o_low, o_far)
    o_near = swap_near(o_pair)

    in_pieces = (
        jnp.concatenate([q_pair, q_near]),
        kv_own,
        jnp.concatenate([q_pair_x, q_near_x]),
        jnp.concatenate([q_pair_y, q_near_y]),
        kv_other,
    )

    def exchange(pieces):
        return [
            pieces[0],
            swap_x(pieces[1]),
            swap_near(pieces[2]),
            swap_corner(pieces[3]),
        ]

    def tokens_of(pieces):
        return jnp.concatenate(exchange([pieces[slot] for slot in range(4)]), axis=1)

    def slots_of(values):
        size = values.shape[1] // 4
        return jnp.stack(exchange([values[:, at * size : (at + 1) * size] for at in range(4)]))

    x = jnp.concatenate([own_rows, after(got_rows, q_pair_x)], axis=1).astype(WIDE)
    normed_one, factor_one = rows_norm(x)
    h_own = (normed_one * gains[0]).astype(LOW)
    h_one = [h_own, swap_core(h_own)]
    h_pair = after(jnp.stack(h_one), pair_x)
    projected = project(h_pair, in_pieces, cosine, sine)
    pair_x_y = swap_y(after(pair_x, projected))
    packed = jnp.stack(exchange([projected[slot] for slot in range(4)]))
    packed = after(packed, pair_far, pair_x_y, o_near)
    pair_far_x = swap_x(after(pair_far, packed))
    pair_far_y = swap_y(after(pair_far, packed))
    o_own = jnp.concatenate([o_pair, o_near])
    o_first = swap_x(after(reorder(o_own[:, :LANES]), packed))
    down_far = swap_far(after(down_own[0], packed))
    attended, logsum = attend(spot, packed)
    attended = after(attended, pair_far_x, pair_far_y, o_first, down_far)
    o_second = swap_y(after(o_first, attended))
    o_back = jnp.concatenate(exchange([attended[slot] for slot in range(4)]), axis=2)
    pair_far_xy = swap_y(after(pair_far_x, o_second))
    o_tokens = [o_back[0], o_back[1]]
    out_weights = jnp.concatenate(
        [o_own, jnp.concatenate([o_first, o_second], axis=1)], axis=2
    ).reshape(4 * 2 * LANES, MODEL_WIDTH)
    out_part = matrix_multiply(o_back.reshape(2 * CHUNK, 4 * 2 * LANES), out_weights)
    residual = x + RESID * fold(out_part[:CHUNK], out_part[CHUNK:], swap_core)
    pairs = (
        ((pair_own[0], pair_far), (pair_x, pair_far_x)),
        ((pair_own[1], pair_far_y), (pair_x_y, pair_far_xy)),
    )

    own_grad, other_grad = halves_of(cotangent)
    got_grad = swap_x(after(other_grad, o_back))
    def columns(values, order, size):
        return jnp.concatenate([values[:, at * size : (at + 1) * size] for at in order], axis=1)

    def rows(values, order, size):
        return jnp.concatenate([values[at * size : (at + 1) * size] for at in order])

    def beyond_of(parts):
        return add_low(parts[0], swap_core(parts[1]))

    def sum_four(parts):
        beyond = swap_near(parts[1])

        def finish(*others):
            own = parts[0][0].astype(WIDE) + swap_core(parts[0][1]).astype(WIDE)
            return own + after(beyond, *others).astype(WIDE)

        return finish

    normed_two, factor_two = rows_norm(residual)
    h_own = (normed_two * gains[1]).astype(LOW)
    h_near = swap_near(h_own)
    h_two = [jnp.concatenate([h_own, swap_core(h_own)]), None]
    down_pair = jnp.stack([down_own[0], down_far])
    down_pair_x = swap_x(after(down_pair, o_back))
    down_far_y = swap_y(after(down_far, pair_far_xy))
    down_pair_xy = swap_y(after(down_pair_x, down_far_y))
    down = (
        ((down_own[0], down_far), (down_pair_x[0], down_pair_x[1])),
        ((down_own[1], down_far_y), (down_pair_xy[0], down_pair_xy[1])),
    )

    hidden, gate_values, up_values = [[], []], [[], []], [[], []]
    for half in range(2):
        if half == 1:
            h_near, got_grad = after(h_near, hidden[0][0]), after(got_grad, hidden[0][0])
            grad_output = jnp.concatenate([own_grad, got_grad], axis=1).astype(WIDE)
            grad_own = (RESID * grad_output).astype(LOW)
            grad_near = swap_near(after(grad_own, h_near))
            h_two[1] = jnp.concatenate([h_near, swap_core(h_near)])
        for which in range(2):
            one, two, three = hidden_units(h_two[half], pairs[which])
            hidden[which].append(one)
            gate_values[which].append(two)
            up_values[which].append(three)

    grad_near = after(grad_near, hidden[0][1])
    grad_mlp = [
        jnp.concatenate([grad_own, swap_core(grad_own)]),
        jnp.concatenate([grad_near, swap_core(grad_near)]),
    ]
    down_sent, down_kept = [
        weight_grad(hidden[which], 0, [grad_mlp], units) for which in (1, 0)
    ]
    part_rows = units // 2
    down_y = swap_y(down_sent[:part_rows])
    down_x = swap_x(
        jnp.concatenate([down_kept[part_rows:, half_width:], down_sent[part_rows:, half_width:]])
    )
    down_first = down_kept[:part_rows]
    down_second = jnp.concatenate(
        [down_kept[part_rows:, :half_width], down_sent[part_rows:, :half_width]]
    )
    down_pair_xy = after(down_pair_xy, down_kept)
    down = (
        ((down_own[0], down_far), (down_pair_x[0], down_pair_x[1])),
        ((down_own[1], down_far_y), (down_pair_xy[0], down_pair_xy[1])),
    )


    grad_gate, grad_up = [[None, None], [None, None]], [[None, None], [None, None]]
    for half in (1, 0):
        grads_here = after(grad_mlp[half], down_sent, down_kept)
        for which in range(2):
            grad_gate[which][half], grad_up[which][half] = hidden_back(
                grads_here, down[which], gate_values[which][half], up_values[which][half]
            )
    up_sent = weight_grad(h_two, 1, grad_up, half_width)
    gate_sent = weight_grad(h_two, 0, grad_gate[1:], MODEL_WIDTH)
    h_two_parts = [None, None]

    def back_of(half, *others):
        grads = [[after(kind[which][half], *others) for which in range(2)]
                 for kind in (grad_gate, grad_up)]
        return normed_back(*grads, pairs)

    h_two_parts[1] = back_of(1, up_sent, gate_sent)
    h_two_beyond = beyond_of(h_two_parts[1])
    down_y, down_x = after(down_y, *h_two_parts[1]), after(down_x, *h_two_parts[1])
    down_first = [
        add_low(down_first[:, at * half_width : (at + 1) * half_width],
                down_y[:, at * half_width : (at + 1) * half_width])
        for at in range(2)
    ]
    down_second = [
        add_low(down_second[at * part_rows : (at + 1) * part_rows],
                down_x[at * part_rows : (at + 1) * part_rows])
        for at in range(2)
    ]
    h_two_parts[0] = back_of(0, h_two_beyond, *down_first, *down_second)
    h_two_sum = sum_four((h_two_parts[0], h_two_beyond))
    hidden_late = [[after(value, *h_two_parts[0]) for value in values] for values in hidden]
    down_parts = [
        down_units([hidden_late[0][half], hidden_late[1][half]], down) for half in (1, 0)
    ][::-1]
    up_kept = weight_grad([after(value, *h_two_parts[0]) for value in h_two], 0, grad_up, half_width)
    up_sum_x = swap_x(up_sent)
    gate_sum_y = swap_y(after(gate_sent, down_y))
    down_first_x, down_second_y = swap_x(down_first[1]), swap_y(down_second[1])

    grad_mid_part, gain_two_part = rows_norm_back(
        h_two_sum(up_kept, *down_parts[0], *down_parts[1]), normed_two, factor_two, gains[1]
    )
    grad_mid = grad_output + grad_mid_part

    grad_attended = [(RESID * grad_mid).astype(LOW)]
    gate_kept = weight_grad(
        [after(value, grad_attended[0]) for value in h_two], 0, grad_gate[:1], MODEL_WIDTH
    )
    layer_sum = sum_four((down_parts[0], beyond_of(down_parts[1])))
    grad_attended.append(swap_core(grad_attended[0]))
    head_grad = right_product(jnp.concatenate(grad_attended), out_weights).astype(LOW)
    head_grad = head_grad.reshape(2, CHUNK, 4 * 2 * LANES)
    head_grad = jnp.stack(
        exchange([head_grad[:, :, at * 2 * LANES : (at + 1) * 2 * LANES] for at in range(4)])
    )
    out_local = [
        weight_grad(o_tokens, 0, [[values[:, half * half_width : (half + 1) * half_width]
                                   for values in grad_attended]], 4 * 2 * LANES)
        for half in range(2)
    ]
    out_near = swap_near(jnp.concatenate([values[4 * LANES :] for values in out_local], axis=1))
    down_first_x, down_second_y, up_sum_x, gate_sum_y = (
        after(value, gate_kept)
        for value in (down_first_x, down_second_y, up_sum_x, gate_sum_y)
    )
    down_part = add_low(down_first[0], down_first_x)
    down_far_sum = swap_far(add_low(down_second[0], down_second_y))
    size = up_kept.shape[1] // 2
    up_kept = [
        add_low(up_kept[:, at * size : (at + 1) * size], up_sum_x[:, at * size : (at + 1) * size])
        for at in range(2)
    ]
    gate_kept = [
        add_low(
            gate_kept[at * half_width : (at + 1) * half_width],
            gate_sum_y[at * half_width : (at + 1) * half_width],
        )
        for at in range(2)
    ]
    gate_sum_x = swap_x(gate_kept[1])
    up_sum_y = swap_y(up_kept[1])
    def sequence_grad(sequence, *others):
        return attend_grad(
            sequence,
            spot,
            packed,
            attended,
            after(head_grad, *others),
            logsum,
            cosine,
            sine,
        )

    packed_first = sequence_grad(0, down_part, *up_kept, *gate_kept)
    up_sum_y, gate_sum_x, down_far_sum, out_near = (
        after(value, packed_first) for value in (up_sum_y, gate_sum_x, down_far_sum, out_near)
    )
    gate_part = add_low(gate_kept[0], gate_sum_x)
    up_part = add_low(up_kept[0], up_sum_y)
    gate_far_sum = swap_far(gate_part[:, units // 2 :])
    in_first = tokens_of(packed_first)
    packed_second = sequence_grad(1, gate_part, up_part)
    gate_far_sum, in_first = after(gate_far_sum, packed_second), after(in_first, packed_second)
    up_far_sum = swap_far(after(up_part[:, units // 2 :], gate_far_sum))
    layer_part = (residual + RESID * layer_sum(packed_second)).astype(LOW)
    in_back = jnp.stack([in_first, tokens_of(after(packed_second, gate_far_sum))])
    down_piece = add_low(down_part, down_far_sum)
    gate_piece = add_low(gate_part[:, : units // 2], gate_far_sum)
    up_piece = add_low(up_part[:, : units // 2], up_far_sum)
    in_grads = [in_back[0], in_back[1]]
    out_kept = add_low(
        jnp.concatenate([values[: 4 * LANES] for values in out_local], axis=1), out_near
    )
    out_kept = add_low(
        out_kept[:, :half_width],
        swap_x(after(rows(out_kept[:, half_width:], [1, 0], 2 * LANES), in_back)),
    )
    in_local = [weight_grad(h_one, half, [in_grads], half_width) for half in (1, 0)][::-1]
    h_one_parts = project_back(after(in_back, up_far_sum), in_pieces)
    grad_in_part, gain_one_part = rows_norm_back(
        h_one_parts[0].astype(WIDE) + swap_core(h_one_parts[1]).astype(WIDE), normed_one, factor_one, gains[0]
    )
    input_part = (grad_mid + grad_in_part).astype(LOW)

    def spread(piece):
        pair = jnp.stack([piece, after(swap_y(piece), h_one_parts)])
        return jnp.concatenate([pair, swap_core(pair)])


    pair = 2 * LANES
    first_cut, second_cut = half_width * 3 // 8, half_width * 5 // 8

    def keep_side(values, got):
        size = values.shape[1] // wide
        kept = jnp.concatenate(
            [
                jnp.concatenate(
                    [
                        values[:, at * wide : at * wide + LANES],
                        values[:, at * wide + pair : (at + 1) * wide],
                    ],
                    axis=1,
                )
                for at in range(size)
            ],
            axis=1,
        )
        return add_low(kept, got)

    def for_side(values):
        size = values.shape[1] // wide
        return jnp.concatenate(
            [values[:, at * wide + LANES : (at + 1) * wide] for at in range(size)], axis=1
        )

    def rows_of(start, stop):
        return [values[start:stop] for values in in_local]

    def near_halves(values):
        size = values.shape[1] // 2
        return values[:, :size], values[:, size:]

    part = rows_of(0, first_cut)
    part = add_low(part[0], swap_x(columns(part[1], swapped, wide)))
    part = keep_side(part, swap_y(for_side(part)))
    kept, sent = near_halves(part)
    ways = [add_low(kept, swap_near(sent))]

    part = jnp.concatenate(rows_of(first_cut, second_cut))
    part = keep_side(part, swap_y(for_side(part)))
    kept, sent = near_halves(part)
    part = add_low(kept, swap_near(sent))
    size = second_cut - first_cut
    ways.append(add_low(part[:size], swap_x(columns(part[size:], [1, 0], pair))))

    part = jnp.concatenate(rows_of(second_cut, half_width))
    kept, sent = near_halves(part)
    part = add_low(kept, swap_near(sent))
    size = half_width - second_cut
    part = add_low(part[:size], swap_x(columns(part[size:], [1, 0], wide)))
    ways.append(keep_side(part, swap_y(for_side(part))))

    in_part = jnp.concatenate(ways)
    in_part = add_low(
        jnp.where(row == 0, in_part[:, :pair], in_part[:, pair:]),
        swap_far(jnp.where(row == 0, in_part[:, pair:], in_part[:, :pair])),
    )
    query_piece = in_part[:, :LANES]
    kv_piece = in_part[:, LANES:]

    out_part = add_low(
        jnp.where(row == 0, out_kept[:pair], out_kept[pair:]),
        swap_far(jnp.where(row == 0, out_kept[pair:], out_kept[:pair])),
    )
    out_piece = add_low(out_part[:LANES], swap_y(out_part[LANES:]))

    gain_sums = jnp.stack([gain_one_part, gain_two_part]).reshape(2, 2, 8, half_width // 8)
    gain_sums = gain_sums[:, 0] + swap_x(gain_sums[:, 1])
    for move in (swap_y, swap_core, swap_near, swap_far):
        gain_sums = gain_sums + move(gain_sums)
    gains_total = gain_sums.reshape(2, half_width)

    kv_pieces = jnp.stack([kv_piece, swap_far(kv_piece)])
    kv_pieces = jnp.concatenate([kv_pieces, swap_near(kv_pieces)])
    kv_pieces = jnp.concatenate([kv_pieces, swap_core(kv_pieces)])

    def squares_of(values):
        values = values.astype(WIDE)
        return jnp.sum(values * values)

    square_local = jnp.where(side == 0, squares_of(kv_piece), 0.0)
    square_local = square_local + jnp.where((col == 0) & (dp == 0), squares_of(gains_total), 0.0)
    for piece in (query_piece, out_piece, gate_piece, up_piece, down_piece):
        square_local = square_local + squares_of(piece)
    square_local = jnp.full((8, LANES), square_local, WIDE)
    for move in (swap_y, swap_core):
        square_local = square_local + move(square_local)
    grad_norm = jnp.sqrt(lax.psum(square_local[0, 0], ("row", "col")))
    factor = jnp.minimum(1.0, CLIP / grad_norm)
    factor_cell = factor.reshape(1, 1)
    spot = dp_spot(dp)

    def step(piece, axis, weight, moment, square):
        return step_weight(spot, factor_cell, spread(piece), axis, weight, moment, square)

    query_out = step(query_piece, 1, query_weight, query_moment, query_square)
    out_out = step(out_piece, 0, out_weight, out_moment, out_square)
    gate_out = step(gate_piece, 1, gate_weight, gate_moment, gate_square)
    up_out = step(up_piece, 1, up_weight, up_moment, up_square)
    down_out = step(down_piece, 0, down_weight, down_moment, down_square)
    layer_out = leave(layer_part, (in_part, up_out[0]))
    input_grad = leave(input_part, (in_part, up_out[0]))
    kv_spot = jnp.stack([core, col])
    key_out, value_out = step_pair(
        kv_spot,
        factor_cell,
        kv_pieces,
        (key_projection, key_first_moment, key_second_moment),
        (value_projection, value_first_moment, value_second_moment),
    )
    results = (query_out, key_out, value_out, out_out, gate_out, up_out, down_out)
    clipped, nexts, variances = zip(*results)
    gains_grad = gains_total * factor
    gains_next, gains_variance = adam(
        norm_gains, gains_grad, gains_moment, gains_square, 0.0, GAINS_LEARN
    )
    return (
        layer_out,
        input_grad,
        *clipped,
        gains_grad,
        *nexts,
        gains_next,
        *variances,
        gains_variance,
        grad_norm,
    )


def solution(mesh):
    placed = (
        P(("dp", "col"), "row"),
        P(("dp", "col"), "row"),
        P("dp"),
        P("row", "col"),
        P("row", None),
        P("row", None),
        P("col", "row"),
        P("row", "col"),
        P("row", "col"),
        P("col", "row"),
        P(None, "row"),
        P("row", "col"),
        P("row", None),
        P("row", None),
        P("col", "row"),
        P("row", "col"),
        P("row", "col"),
        P("col", "row"),
        P(None, "row"),
        P("row", "col"),
        P("row", None),
        P("row", None),
        P("col", "row"),
        P("row", "col"),
        P("row", "col"),
        P("col", "row"),
        P(None, "row"),
    )
    return jax.shard_map(
        swapped_shards if swaps_fit(mesh) else shards,
        mesh=mesh,
        in_specs=placed,
        out_specs=(
            P(("dp", "col"), "row"),
            P(("dp", "col"), "row"),
            P("row", "col"),
            P("row", None),
            P("row", None),
            P("col", "row"),
            P("row", "col"),
            P("row", "col"),
            P("col", "row"),
            P(None, "row"),
            P("row", "col"),
            P("row", None),
            P("row", None),
            P("col", "row"),
            P("row", "col"),
            P("row", "col"),
            P("col", "row"),
            P(None, "row"),
            P("row", "col"),
            P("row", None),
            P("row", None),
            P("col", "row"),
            P("row", "col"),
            P("row", "col"),
            P("col", "row"),
            P(None, "row"),
            P(),
        ),
        check_vma=False,
    )
```

```python
import functools

import jax
import jax.numpy as jnp
from jax import lax
from jax.experimental import pallas as pl
from jax.experimental.pallas import tpu as pltpu
from jax.sharding import PartitionSpec as P

MODEL_WIDTH = 2048
QUERY_HEADS = 32
KEY_VALUE_HEADS = 8
HEAD_SIZE = 64
SEQUENCE_LENGTH = 2048
STEP = 5


EPS_NORM = 1e-05
RESID = 0.22
ATTN_SCALE = 1.0 / 64.0
THETA = 10000000.0
LEARN = 0.1
GAINS_LEARN = 0.5
BETA_ONE = 0.5
BETA_TWO = 0.5
ADAM_EPS = 1e-08
DECAY = 0.1
CLIP = 1.0


def matrix_multiply(left_side, right_side):
    return jnp.dot(left_side, right_side, preferred_element_type=jnp.float32)


def left_product(left_side, right_side):
    return lax.dot_general(
        left_side, right_side, (((0,), (0,)), ((), ())), preferred_element_type=jnp.float32
    )


def right_product(left_side, right_side):
    return lax.dot_general(
        left_side, right_side, (((1,), (1,)), ((), ())), preferred_element_type=jnp.float32
    )


def width_total(values):
    return lax.psum(values, "row")


def gather_tokens(values):
    return lax.all_gather(values, "col", axis=0, tiled=True)


def sum_tokens(term, tok_rows):
    return lax.psum_scatter(
        term(jnp.int32(0), lax.axis_size("col") * tok_rows).astype(jnp.bfloat16),
        "col",
        scatter_dimension=0,
        tiled=True,
    ).astype(jnp.float32)


def fetch_weights(first, second, third, fourth, fifth):
    return (
        lax.all_gather(first, "row", axis=0, tiled=True),
        lax.all_gather(second, "row", axis=0, tiled=True),
        lax.all_gather(third, "row", axis=0, tiled=True),
        lax.all_gather(fourth, "row", axis=1, tiled=True),
        lax.all_gather(fifth, "row", axis=1, tiled=True),
    )


def enter_rows(values):
    return lax.all_to_all(values, "row", split_axis=0, concat_axis=1, tiled=True)


def leave_rows(values):
    return lax.all_to_all(
        values.astype(jnp.bfloat16), "row", split_axis=1, concat_axis=0, tiled=True
    ).astype(values.dtype)


def reduce_rows(first, second, third, fourth, fifth):
    return (
        lax.psum_scatter(first.astype(jnp.bfloat16), "row", scatter_dimension=0, tiled=True).astype(
            jnp.float32
        ),
        lax.psum_scatter(
            second.astype(jnp.bfloat16), "row", scatter_dimension=0, tiled=True
        ).astype(jnp.float32),
        lax.psum_scatter(third.astype(jnp.bfloat16), "row", scatter_dimension=1, tiled=True).astype(
            jnp.float32
        ),
        lax.psum_scatter(
            fourth.astype(jnp.bfloat16), "row", scatter_dimension=0, tiled=True
        ).astype(jnp.float32),
        lax.psum_scatter(fifth.astype(jnp.bfloat16), "row", scatter_dimension=1, tiled=True).astype(
            jnp.float32
        ),
    )


def rope_tables(length):
    half_width = HEAD_SIZE // 2
    frequency = THETA ** (-(jnp.arange(half_width, dtype=jnp.float32) * 2.0 / HEAD_SIZE))
    angles = jnp.arange(length, dtype=jnp.float32)[:, None] * frequency[None, :]
    angles = jnp.concatenate([angles, angles], axis=1)
    return (jnp.cos(angles), jnp.sin(angles))


def rotate(values):
    half_width = values.shape[-1] // 2
    return jnp.concatenate([-values[..., half_width:], values[..., :half_width]], axis=-1)


def rope(values, cosine_table, sine_table):
    return values * cosine_table[:, None, :] + rotate(values) * sine_table[:, None, :]


def rope_back(gradient, cosine_table, sine_table):
    return gradient * cosine_table[:, None, :] - rotate(gradient * sine_table[:, None, :])


def rms_forward(values, gain_row):
    squares = width_total(jnp.sum(values * values, axis=1))
    factor = lax.rsqrt(squares[:, None] / MODEL_WIDTH + EPS_NORM)
    normed = values * factor
    return ((normed * gain_row).astype(jnp.bfloat16), normed, factor)


def rms_backward(grad_normed, normed, factor, gain_row):
    weighted = grad_normed * gain_row
    inner_sum = width_total(jnp.sum(weighted * normed, axis=1))
    grad_input = factor * (weighted - normed * (inner_sum[:, None] / MODEL_WIDTH))
    return (grad_input, jnp.sum(grad_normed * normed, axis=0))


def attend_sequence(
    heads_of_queries, heads_of_keys, heads_of_values, prefix_length, rows_per_block
):
    length = heads_of_keys.shape[0]
    key_place = jnp.arange(length)

    def one_block(inputs):
        query_block, positions = inputs
        scores = jnp.einsum(
            "qhgd,khd->hgqk", query_block, heads_of_keys, preferred_element_type=jnp.float32
        )
        visible = (key_place[None, :] <= positions[:, None]) | (key_place[None, :] < prefix_length)
        scores = jnp.where(visible, scores, -1e30)
        row_max = jnp.max(scores, axis=-1, keepdims=True)
        exponent = jnp.exp(scores - row_max)
        total_sum = jnp.sum(exponent, axis=-1, keepdims=True)
        probability = (exponent / total_sum).astype(jnp.bfloat16)
        result = jnp.einsum(
            "hgqk,khd->qhgd", probability, heads_of_values, preferred_element_type=jnp.float32
        )
        return (result, row_max[..., 0] + jnp.log(total_sum[..., 0]))

    block_count = length // rows_per_block
    shaped = heads_of_queries.reshape((block_count, rows_per_block) + heads_of_queries.shape[1:])
    positions = jnp.arange(length).reshape(block_count, rows_per_block)
    result, logsum = lax.map(one_block, (shaped, positions))
    return (result.reshape(heads_of_queries.shape), logsum)


def attend_back(
    heads_of_queries,
    heads_of_keys,
    heads_of_values,
    prefix_length,
    logsum,
    grad_heads,
    rows_per_block,
):
    length = heads_of_keys.shape[0]
    key_place = jnp.arange(length)
    block_count = length // rows_per_block

    def one_block(carried, inputs):
        query_block, grad_block, logsum_block, positions = inputs
        scores = jnp.einsum(
            "qhgd,khd->hgqk", query_block, heads_of_keys, preferred_element_type=jnp.float32
        )
        visible = (key_place[None, :] <= positions[:, None]) | (key_place[None, :] < prefix_length)
        scores = jnp.where(visible, scores, -1e30)
        probability = jnp.exp(scores - logsum_block[..., None])
        grad_prob = jnp.einsum(
            "qhgd,khd->hgqk", grad_block, heads_of_values, preferred_element_type=jnp.float32
        )
        delta_sum = jnp.sum(probability * grad_prob, axis=-1, keepdims=True)
        grad_scores = (probability * (grad_prob - delta_sum)).astype(jnp.bfloat16)
        grad_query = jnp.einsum(
            "hgqk,khd->qhgd", grad_scores, heads_of_keys, preferred_element_type=jnp.float32
        )
        grad_keys = jnp.einsum(
            "hgqk,qhgd->khd", grad_scores, query_block, preferred_element_type=jnp.float32
        )
        grad_values = jnp.einsum(
            "hgqk,qhgd->khd",
            probability.astype(jnp.bfloat16),
            grad_block,
            preferred_element_type=jnp.float32,
        )
        return ((carried[0] + grad_keys, carried[1] + grad_values), grad_query)

    block_shape = (block_count, rows_per_block) + heads_of_queries.shape[1:]
    initial = (
        jnp.zeros(heads_of_keys.shape, jnp.float32),
        jnp.zeros(heads_of_values.shape, jnp.float32),
    )
    positions = jnp.arange(length).reshape(block_count, rows_per_block)
    inputs = (
        heads_of_queries.reshape(block_shape),
        grad_heads.reshape(block_shape),
        logsum,
        positions,
    )
    (grad_keys, grad_values), grad_query = lax.scan(one_block, initial, inputs)
    return (grad_query.reshape(heads_of_queries.shape), grad_keys, grad_values)


def adam(weight, gradient, moment_one, moment_two, decay_rate, learn_rate):
    moment_new = BETA_ONE * moment_one + (1.0 - BETA_ONE) * gradient
    square_new = BETA_TWO * moment_two + (1.0 - BETA_TWO) * gradient * gradient
    moment_hat = moment_new / (1.0 - BETA_ONE**STEP)
    square_hat = square_new / (1.0 - BETA_TWO**STEP)
    return (
        weight
        - learn_rate * (moment_hat / (jnp.sqrt(square_hat) + ADAM_EPS) + decay_rate * weight),
        square_new,
    )


def shards(
    tokens,
    cotangent,
    prefix,
    query_weight,
    key_projection,
    value_projection,
    out_weight,
    gate_weight,
    up_weight,
    down_weight,
    norm_gains,
    query_moment,
    key_first_moment,
    value_first_moment,
    out_moment,
    gate_moment,
    up_moment,
    down_moment,
    gains_moment,
    query_square,
    key_second_moment,
    value_second_moment,
    out_square,
    gate_square,
    up_square,
    down_square,
    gains_square,
):
    tok_rows = tokens.shape[0]
    query_cols = query_weight.shape[1]
    kv_all = key_projection.shape[1]
    ffn_cols = gate_weight.shape[1]
    row_size = lax.axis_size("row")
    col_size = lax.axis_size("col")
    row_index = lax.axis_index("row")
    col_index = lax.axis_index("col")
    tok_count = tok_rows * col_size
    seq_count = prefix.shape[0]
    group_width = QUERY_HEADS // KEY_VALUE_HEADS
    rows_per_block = min(512, SEQUENCE_LENGTH)
    col_heads = query_cols // HEAD_SIZE
    frame_used = max(1, col_heads // group_width)
    frame_start = col_index * col_heads // group_width
    frame_width = frame_used * HEAD_SIZE
    key_here = lax.dynamic_slice_in_dim(key_projection, frame_start * HEAD_SIZE, frame_width, 1)
    value_here = lax.dynamic_slice_in_dim(value_projection, frame_start * HEAD_SIZE, frame_width, 1)
    query_mat = query_weight.astype(jnp.bfloat16)
    kv_mat = (
        jnp.stack([key_here, value_here], axis=1)
        .astype(jnp.bfloat16)
        .reshape(key_here.shape[0], 2 * frame_width)
    )
    out_mat = out_weight.astype(jnp.bfloat16)
    ffn_mat = (
        jnp.stack([gate_weight, up_weight], axis=1)
        .astype(jnp.bfloat16)
        .reshape(gate_weight.shape[0], 2 * ffn_cols)
    )
    down_mat = down_weight.astype(jnp.bfloat16)
    gain_one = norm_gains[0]
    gain_two = norm_gains[1]
    query_use, kv_use, ffn_use, out_use, down_use = fetch_weights(
        query_mat, kv_mat, ffn_mat, out_mat, down_mat
    )
    use_rows = tok_count // row_size
    seq_use = seq_count // row_size
    prefix_use = lax.dynamic_slice_in_dim(prefix, row_index * seq_use, seq_use, 0)
    kv_used = max(1, col_heads // group_width)
    group_here = col_heads // kv_used
    cosine_one, sine_one = rope_tables(SEQUENCE_LENGTH)
    cosine_table = jnp.tile(cosine_one, (seq_use, 1))
    sine_table = jnp.tile(sine_one, (seq_use, 1))

    def spread(values):
        return enter_rows(values)

    def to_tokens(product_fn):
        whole = leave_rows(product_fn(0, use_rows))

        def term(start_row, rows_here):
            return whole

        return sum_tokens(term, tok_rows)

    input_float = tokens.astype(jnp.float32)
    hidden_first, normed_one, factor_one = rms_forward(input_float, gain_one)
    h_one_use = spread(gather_tokens(hidden_first))
    query_sum = matrix_multiply(h_one_use, query_use)
    kv_frame = matrix_multiply(h_one_use, kv_use).reshape(use_rows, 2, frame_width)
    query_round = (
        rope(query_sum.reshape(use_rows, col_heads, HEAD_SIZE), cosine_table, sine_table)
        * ATTN_SCALE
    ).astype(jnp.bfloat16)
    key_round = rope(
        kv_frame[:, 0].reshape(use_rows, kv_used, HEAD_SIZE), cosine_table, sine_table
    ).astype(jnp.bfloat16)
    value_round = kv_frame[:, 1].reshape(use_rows, kv_used, HEAD_SIZE).astype(jnp.bfloat16)
    query_seq = query_round.reshape(seq_use, SEQUENCE_LENGTH, kv_used, group_here, HEAD_SIZE)
    key_seq = key_round.reshape(seq_use, SEQUENCE_LENGTH, kv_used, HEAD_SIZE)
    value_seq = value_round.reshape(seq_use, SEQUENCE_LENGTH, kv_used, HEAD_SIZE)

    def forward_sequence(inputs):
        return attend_sequence(inputs[0], inputs[1], inputs[2], inputs[3], rows_per_block)

    attended, logsum = lax.map(forward_sequence, (query_seq, key_seq, value_seq, prefix_use))
    head_round = attended.reshape(use_rows, col_heads * HEAD_SIZE).astype(jnp.bfloat16)

    def out_term(start_row, rows_here):
        return matrix_multiply(head_round, out_use)

    residual_mid = input_float + RESID * to_tokens(out_term)
    h_two, normed_two, factor_two = rms_forward(residual_mid, gain_two)
    h_two_use = spread(gather_tokens(h_two))
    ffn_part = matrix_multiply(h_two_use, ffn_use).reshape(use_rows, 2, ffn_cols)
    gate_value = ffn_part[:, 0]
    up_value = ffn_part[:, 1]
    hidden = (jax.nn.silu(gate_value) * up_value).astype(jnp.bfloat16)

    def down_term(start_row, rows_here):
        return matrix_multiply(hidden, down_use)

    layer_out = (residual_mid + RESID * to_tokens(down_term)).astype(jnp.bfloat16)
    grad_output = cotangent.astype(jnp.float32)
    grad_mlp = (RESID * grad_output).astype(jnp.bfloat16)
    grad_mlp_use = spread(gather_tokens(grad_mlp))
    down_local = left_product(hidden, grad_mlp_use)
    hidden_part = right_product(grad_mlp_use, down_use)
    sigmoid_gate = jax.nn.sigmoid(gate_value)
    grad_gate = hidden_part * up_value * sigmoid_gate * (1.0 + gate_value * (1.0 - sigmoid_gate))
    grad_up = hidden_part * (gate_value * sigmoid_gate)
    grad_pair = jnp.stack([grad_gate, grad_up], axis=1).astype(jnp.bfloat16)
    pair_flat = grad_pair.reshape(use_rows, 2 * ffn_cols)
    ffn_local = left_product(h_two_use, pair_flat).reshape(-1, 2, ffn_cols)

    def ffn_back_term(start_row, rows_here):
        return right_product(pair_flat, ffn_use)

    grad_mid_part, gain_two_part = rms_backward(
        to_tokens(ffn_back_term), normed_two, factor_two, gain_two
    )
    grad_mid = grad_output + grad_mid_part
    grad_attended = (RESID * grad_mid).astype(jnp.bfloat16)
    grad_attended_use = spread(gather_tokens(grad_attended))
    out_local = left_product(head_round, grad_attended_use)
    head_part = right_product(grad_attended_use, out_use)
    head_grad = head_part
    head_grad = head_grad.astype(jnp.bfloat16).reshape(
        seq_use, SEQUENCE_LENGTH, kv_used, group_here, HEAD_SIZE
    )

    def backward_sequence(inputs):
        return attend_back(
            inputs[0], inputs[1], inputs[2], inputs[3], inputs[4], inputs[5], rows_per_block
        )

    query_back, key_back, value_back = lax.map(
        backward_sequence, (query_seq, key_seq, value_seq, prefix_use, logsum, head_grad)
    )
    query_grad_heads = rope_back(
        query_back.reshape(use_rows, col_heads, HEAD_SIZE) * ATTN_SCALE, cosine_table, sine_table
    )
    query_grad_round = query_grad_heads.reshape(use_rows, col_heads * HEAD_SIZE).astype(
        jnp.bfloat16
    )
    key_grad_heads = rope_back(
        key_back.reshape(use_rows, kv_used, HEAD_SIZE), cosine_table, sine_table
    )
    kv_grad_used = jnp.stack(
        [
            key_grad_heads.reshape(use_rows, kv_used * HEAD_SIZE),
            value_back.reshape(use_rows, kv_used * HEAD_SIZE),
        ],
        axis=1,
    )
    kv_grad = kv_grad_used.astype(jnp.bfloat16)
    kv_flat = kv_grad.reshape(use_rows, 2 * frame_width)
    query_local = left_product(h_one_use, query_grad_round)
    kv_frame_local = left_product(h_one_use, kv_flat).reshape(-1, 2, frame_width)
    kv_local = lax.dynamic_update_slice_in_dim(
        jnp.zeros((kv_frame_local.shape[0], 2, kv_all), jnp.float32),
        kv_frame_local,
        frame_start * HEAD_SIZE,
        2,
    )

    def input_term(start_row, rows_here):
        return right_product(query_grad_round, query_use) + right_product(kv_flat, kv_use)

    grad_in_part, gain_one_part = rms_backward(
        to_tokens(input_term), normed_one, factor_one, gain_one
    )
    input_grad = (grad_mid + grad_in_part).astype(jnp.bfloat16)
    local_grads = reduce_rows(query_local, kv_local, out_local, ffn_local, down_local)
    summed = (
        lax.psum(local_grads[0].astype(jnp.bfloat16), "dp").astype(jnp.float32),
        lax.psum(local_grads[2].astype(jnp.bfloat16), "dp").astype(jnp.float32),
        lax.psum(local_grads[3].astype(jnp.bfloat16), "dp").astype(jnp.float32),
        lax.psum(local_grads[4].astype(jnp.bfloat16), "dp").astype(jnp.float32),
    )
    kv_summed, gains_total = lax.psum(
        (local_grads[1], jnp.stack([gain_one_part, gain_two_part])), ("dp", "col")
    )
    raw_grads = (
        summed[0],
        kv_summed[:, 0],
        kv_summed[:, 1],
        summed[1],
        summed[2][:, 0],
        summed[2][:, 1],
        summed[3],
    )
    masters = (
        query_weight,
        key_projection,
        value_projection,
        out_weight,
        gate_weight,
        up_weight,
        down_weight,
    )
    moments = (
        query_moment,
        key_first_moment,
        value_first_moment,
        out_moment,
        gate_moment,
        up_moment,
        down_moment,
    )
    squares = (
        query_square,
        key_second_moment,
        value_second_moment,
        out_square,
        gate_square,
        up_square,
        down_square,
    )
    copied_sum = jnp.sum(gains_total * gains_total) + jnp.sum(kv_summed * kv_summed)
    square_local = jnp.where(col_index == 0, copied_sum, 0.0)
    for position in (0, 3, 4, 5, 6):
        square_local = square_local + jnp.sum(raw_grads[position] * raw_grads[position])
    total_sum = lax.psum(square_local, ("row", "col"))
    grad_norm = jnp.sqrt(total_sum)
    factor = jnp.minimum(1.0, CLIP / grad_norm)
    clipped = []
    nexts = []
    variances = []
    for position in range(7):
        gradient = raw_grads[position] * factor
        weight_next, variance = adam(
            masters[position], gradient, moments[position], squares[position], DECAY, LEARN
        )
        clipped.append(gradient)
        nexts.append(weight_next)
        variances.append(variance)
    gains_grad = gains_total * factor
    gains_next, gains_variance = adam(
        norm_gains, gains_grad, gains_moment, gains_square, 0.0, GAINS_LEARN
    )
    return (
        layer_out,
        input_grad,
        clipped[0],
        clipped[1],
        clipped[2],
        clipped[3],
        clipped[4],
        clipped[5],
        clipped[6],
        gains_grad,
        nexts[0],
        nexts[1],
        nexts[2],
        nexts[3],
        nexts[4],
        nexts[5],
        nexts[6],
        gains_next,
        variances[0],
        variances[1],
        variances[2],
        variances[3],
        variances[4],
        variances[5],
        variances[6],
        gains_variance,
        grad_norm,
    )


LOW = jnp.bfloat16
WIDE = jnp.float32
CHUNK = 512
LANES = 128
MASKED = -1e30
VMEM_BYTES = 48 * 1024 * 1024


def swaps_fit(mesh):
    return dict(mesh.shape) == {"dp": 4, "row": 2, "col": 4}


def swap(values, axis, bit):
    size = lax.axis_size(axis)
    return lax.ppermute(values, axis, [(place, place ^ bit) for place in range(size)])


def swap_core(values):
    return swap(values, "dp", 1)


def swap_y(values):
    return swap(values, "dp", 2)


def swap_x(values):
    return swap(values, "row", 1)


def swap_near(values):
    return swap(values, "col", 1)


def swap_far(values):
    return swap(values, "col", 2)


def swap_corner(values):
    cols = lax.axis_size("col")
    pairs = [
        (row * cols + col, (row ^ 1) * cols + (col ^ 1))
        for row in range(lax.axis_size("row"))
        for col in range(cols)
    ]
    return lax.ppermute(values, ("row", "col"), pairs)


def after(value, *others):
    return lax.optimization_barrier((value,) + others)[0]


def fold(kept, sent, move):
    return kept + move(sent.astype(LOW)).astype(WIDE)


def in_order(place, own, other, axis):
    return jnp.concatenate(
        [jnp.where(place == 0, own, other), jnp.where(place == 0, other, own)], axis=axis
    )


def cut(values, start, size, axis):
    return lax.dynamic_slice_in_dim(values, start, size, axis)


def partner_lanes(values):
    lane = lax.broadcasted_iota(jnp.int32, values.shape, 1)
    half = HEAD_SIZE // 2
    ahead = pltpu.roll(values, values.shape[1] - half, 1)
    behind = pltpu.roll(values, half, 1)
    return jnp.where(lane % HEAD_SIZE < half, ahead, behind)


def first_lanes(shape):
    return lax.broadcasted_iota(jnp.int32, shape, 1) < HEAD_SIZE


def dot_nt(left_side, right_side):
    return lax.dot_general(
        left_side, right_side, (((1,), (1,)), ((), ())), preferred_element_type=WIDE
    )


def dot_tn(left_side, right_side):
    return lax.dot_general(
        left_side, right_side, (((0,), (0,)), ((), ())), preferred_element_type=WIDE
    )


WIDE_BLOCK = 512
COST_SHARE = 1


def one_buffer(shape, index_map):
    return pl.BlockSpec(shape, index_map, pipeline_mode=pl.Buffered(1))


def cost(flops, read, written):
    return pl.CostEstimate(
        flops=int(flops * COST_SHARE),
        bytes_accessed=int(2 * (read + written) * COST_SHARE),
        transcendentals=0,
    )


def mm(left_side, right_side):
    return jnp.dot(left_side, right_side, preferred_element_type=WIDE)


def both(refs, axis):
    return jnp.concatenate([ref[...] for ref in refs], axis=axis)


def flat(*blocks):
    return [array for block in blocks for array in block]


def both_of(refs, which, axis):
    return jnp.concatenate([ref[which] for ref in refs], axis=axis)


def hidden_kernel(normed_ref, *refs):
    hidden_ref, gate_ref, up_ref = refs[4:]
    half = normed_ref.shape[1] // 2
    left, right = normed_ref[:, :half], normed_ref[:, half:]
    gate = mm(left, both_of(refs[0:2], 0, 1)) + mm(right, both_of(refs[2:4], 0, 1))
    up = mm(left, both_of(refs[0:2], 1, 1)) + mm(right, both_of(refs[2:4], 1, 1))
    hidden_ref[...] = (gate * jax.nn.sigmoid(gate) * up).astype(LOW)
    gate_ref[...] = gate.astype(LOW)
    up_ref[...] = up.astype(LOW)


def hidden_units(normed, pairs):
    tokens, width = normed.shape
    weights = flat(*pairs)
    units = 2 * weights[0].shape[2]
    block = WIDE_BLOCK
    weight = one_buffer(weights[0].shape, lambda i: (0, 0, 0))
    out = pl.BlockSpec((block, units), lambda i: (i, 0))
    return pl.pallas_call(
        hidden_kernel,
        grid=(tokens // block,),
        in_specs=[pl.BlockSpec((block, width), lambda i: (i, 0))] + [weight] * 4,
        out_specs=[out] * 3,
        out_shape=[jax.ShapeDtypeStruct((tokens, units), LOW)] * 3,
        compiler_params=pltpu.CompilerParams(vmem_limit_bytes=VMEM_BYTES),
        cost_estimate=cost(
            4 * tokens * width * units, tokens * width + 2 * width * units, 3 * tokens * units
        ),
    )(normed, *weights)


def down_kernel(h0, h1, *refs):
    weights, outs = refs[:8], refs[8:]
    half = weights[0].shape[1]
    for at, out_ref in enumerate(outs):

        @pl.when(pl.program_id(0) == at)
        def _(out_ref=out_ref):
            for side in range(2):
                total = mm(h0[...], both(weights[2 * side : 2 * side + 2], 0))
                total = total + mm(h1[...], both(weights[4 + 2 * side : 6 + 2 * side], 0))
                out_ref[:, side * half : (side + 1) * half] = total.astype(LOW)


def down_units(hidden, down):
    tokens, units = hidden[0].shape
    weights = flat(*down[0], *down[1])
    half = weights[0].shape[1]
    block = WIDE_BLOCK
    weight = one_buffer(weights[0].shape, lambda i: (0, 0))
    left = pl.BlockSpec((block, units), lambda i: (i, 0))
    return pl.pallas_call(
        down_kernel,
        grid=(tokens // block,),
        in_specs=[left] * 2 + [weight] * 8,
        out_specs=[one_buffer((block, 2 * half), lambda i: (0, 0))] * (tokens // block),
        out_shape=[jax.ShapeDtypeStruct((block, 2 * half), LOW)] * (tokens // block),
        compiler_params=pltpu.CompilerParams(vmem_limit_bytes=VMEM_BYTES),
        cost_estimate=cost(
            8 * tokens * units * half, 2 * tokens * units + 4 * units * half, 2 * tokens * half
        ),
    )(*hidden, *weights)


def hidden_back_kernel(grad_ref, d0, d1, d2, d3, gate_ref, up_ref, grad_gate_ref, grad_up_ref):
    half = d0.shape[1]
    part = dot_nt(grad_ref[:, :half], both((d0, d1), 0))
    part = part + dot_nt(grad_ref[:, half:], both((d2, d3), 0))
    gate = gate_ref[...].astype(WIDE)
    up = up_ref[...].astype(WIDE)
    sigmoid = jax.nn.sigmoid(gate)
    grad_gate_ref[...] = (part * up * sigmoid * (1.0 + gate * (1.0 - sigmoid))).astype(LOW)
    grad_up_ref[...] = (part * (gate * sigmoid)).astype(LOW)


def hidden_back(grads, down, gate, up):
    tokens, width = grads.shape
    weights = flat(*down)
    units = 2 * weights[0].shape[0]
    block = WIDE_BLOCK
    weight = one_buffer(weights[0].shape, lambda i: (0, 0))
    row = pl.BlockSpec((block, units), lambda i: (i, 0))
    return pl.pallas_call(
        hidden_back_kernel,
        grid=(tokens // block,),
        in_specs=[pl.BlockSpec((block, width), lambda i: (i, 0))] + [weight] * 4 + [row] * 2,
        out_specs=[row] * 2,
        out_shape=[jax.ShapeDtypeStruct((tokens, units), LOW)] * 2,
        compiler_params=pltpu.CompilerParams(vmem_limit_bytes=VMEM_BYTES),
        cost_estimate=cost(
            2 * tokens * width * units,
            tokens * width + width * units + 2 * tokens * units,
            2 * tokens * units,
        ),
    )(grads, *weights, gate, up)


def normed_back_kernel(a0, a1, b0, b1, *refs):
    weights, outs = refs[:8], refs[8:]
    half = weights[0].shape[1]
    for at, out_ref in enumerate(outs):

        @pl.when(pl.program_id(0) == at)
        def _(out_ref=out_ref):
            for side in range(2):
                total = jnp.zeros((a0.shape[0], half), WIDE)
                for which, lefts in enumerate(((a0, b0), (a1, b1))):
                    start = 4 * which + 2 * side
                    for kind, left in enumerate(lefts):
                        right = both_of(weights[start : start + 2], kind, 1)
                        total = total + dot_nt(left[...], right)
                out_ref[:, side * half : (side + 1) * half] = total.astype(LOW)


def normed_back(grad_gate, grad_up, pairs):
    tokens, units = grad_gate[0].shape
    weights = flat(*pairs[0], *pairs[1])
    half = weights[0].shape[1]
    block = WIDE_BLOCK
    weight = one_buffer(weights[0].shape, lambda i: (0, 0, 0))
    left = pl.BlockSpec((block, units), lambda i: (i, 0))
    return pl.pallas_call(
        normed_back_kernel,
        grid=(tokens // block,),
        in_specs=[left] * 4 + [weight] * 8,
        out_specs=[one_buffer((block, 2 * half), lambda i: (0, 0))] * (tokens // block),
        out_shape=[jax.ShapeDtypeStruct((block, 2 * half), LOW)] * (tokens // block),
        compiler_params=pltpu.CompilerParams(vmem_limit_bytes=VMEM_BYTES),
        cost_estimate=cost(
            16 * tokens * units * half, 4 * tokens * units + 8 * units * half, 2 * tokens * half
        ),
    )(*grad_gate, *grad_up, *weights)


def weight_grad(lefts, place, rights, columns):
    count, tokens, parts = len(rights), lefts[0].shape[0], len(lefts)
    span = rights[0][0].shape[1]
    block = WIDE_BLOCK

    def kernel(*refs):
        left_refs, out_ref = refs[:parts], refs[-1]
        for at in range(count):
            right_refs = refs[parts * (at + 1) : parts * (at + 2)]
            total = dot_tn(left_refs[0][...], right_refs[0][...])
            for left_ref, right_ref in zip(left_refs[1:], right_refs[1:]):
                total = total + dot_tn(left_ref[...], right_ref[...])
            out_ref[:, at * span : (at + 1) * span] = total.astype(LOW)

    start = place * columns // block
    return pl.pallas_call(
        kernel,
        grid=(columns // block,),
        in_specs=[pl.BlockSpec((tokens, block), lambda i: (0, i + start))] * parts
        + [one_buffer((tokens, span), lambda i: (0, 0))] * (count * parts),
        out_specs=pl.BlockSpec((block, count * span), lambda i: (i, 0)),
        out_shape=jax.ShapeDtypeStruct((columns, count * span), LOW),
        compiler_params=pltpu.CompilerParams(vmem_limit_bytes=VMEM_BYTES),
        cost_estimate=cost(
            2 * count * parts * tokens * columns * span,
            parts * tokens * (columns + count * span),
            count * columns * span,
        ),
    )(*lefts, *[value for right in rights for value in right])


def project_kernel(
    normed_ref, own_ref, kv_ref, first_ref, second_ref, kv_other_ref, cosine_ref, sine_ref, out_ref
):
    half = own_ref.shape[1]
    near_rows = jnp.concatenate([own_ref[0], kv_ref[0]], axis=1)
    other_rows = jnp.concatenate([first_ref[0], second_ref[0], kv_other_ref[0]], axis=1)
    product = mm(normed_ref[0, :, :half], near_rows) + mm(normed_ref[0, :, half:], other_rows)
    cosine = cosine_ref[0]
    sine = sine_ref[0]
    for tile in range(3):
        part = product[:, tile * LANES : (tile + 1) * LANES]
        turned = part * cosine + partner_lanes(part) * sine
        if tile < 2:
            turned = turned * ATTN_SCALE
        else:
            turned = jnp.where(first_lanes(part.shape), turned, part)
        out_ref[0, 0, :, tile * LANES : (tile + 1) * LANES] = turned.astype(LOW)


def piece_specs(pieces):
    return [pl.BlockSpec((1,) + piece.shape[1:], lambda j, i: (j, 0, 0)) for piece in pieces]


def project(normed, pieces, cosine, sine):
    groups = 4
    wide = 3 * LANES
    table = pl.BlockSpec((1, CHUNK, LANES), lambda j, i: (0, 0, 0))
    return pl.pallas_call(
        project_kernel,
        grid=(groups, 2),
        in_specs=[pl.BlockSpec((1, CHUNK, MODEL_WIDTH), lambda j, i: (i, 0, 0))]
        + piece_specs(pieces)
        + [table, table],
        out_specs=pl.BlockSpec((1, 1, CHUNK, wide), lambda j, i: (j, i, 0, 0)),
        out_shape=jax.ShapeDtypeStruct((groups, 2, CHUNK, wide), LOW),
        compiler_params=pltpu.CompilerParams(vmem_limit_bytes=VMEM_BYTES),
        cost_estimate=cost(
            2 * CHUNK * MODEL_WIDTH * groups * wide, MODEL_WIDTH * (CHUNK + groups * wide), 0
        ),
    )(normed, *pieces, cosine, sine)


def project_back_kernel(
    grad_ref, own_ref, kv_ref, first_ref, second_ref, kv_other_ref, out_ref, acc
):
    group, tokens = pl.program_id(0), pl.program_id(1)
    half = own_ref.shape[1]

    @pl.when(group == 0)
    def _():
        acc[tokens] = jnp.zeros(acc.shape[1:], WIDE)

    near_rows = jnp.concatenate([own_ref[0], kv_ref[0]], axis=1)
    other_rows = jnp.concatenate([first_ref[0], second_ref[0], kv_other_ref[0]], axis=1)
    acc[tokens, :, :half] += dot_nt(grad_ref[0], near_rows)
    acc[tokens, :, half:] += dot_nt(grad_ref[0], other_rows)

    @pl.when(group == pl.num_programs(0) - 1)
    def _():
        out_ref[tokens] = acc[tokens].astype(LOW)


def project_back(grads, pieces):
    groups = 4
    wide = 3 * LANES
    return pl.pallas_call(
        project_back_kernel,
        grid=(groups, 2),
        in_specs=[pl.BlockSpec((1, CHUNK, wide), lambda j, i: (i, 0, j))] + piece_specs(pieces),
        out_specs=pl.BlockSpec((2, CHUNK, MODEL_WIDTH), lambda j, i: (0, 0, 0)),
        out_shape=jax.ShapeDtypeStruct((2, CHUNK, MODEL_WIDTH), LOW),
        scratch_shapes=[pltpu.VMEM((2, CHUNK, MODEL_WIDTH), WIDE)],
        compiler_params=pltpu.CompilerParams(vmem_limit_bytes=VMEM_BYTES),
        cost_estimate=cost(
            2 * CHUNK * MODEL_WIDTH * groups * wide, MODEL_WIDTH * (CHUNK + groups * wide), 0
        ),
    )(grads, *pieces)


def split_heads(tiles, lanes_from):
    heads = []
    for head in range(4):
        tile = tiles[:, (head // 2) * LANES : (head // 2 + 1) * LANES].astype(WIDE)
        if (head % 2) * HEAD_SIZE != lanes_from:
            tile = pltpu.roll(tile, HEAD_SIZE, 1)
        low = first_lanes(tile.shape)
        heads.append(jnp.where(low if lanes_from == 0 else ~low, tile, 0.0).astype(LOW))
    return heads


def join_heads(heads, lanes_from):
    tiles = []
    for pair in range(2):
        even, odd = heads[2 * pair], heads[2 * pair + 1]
        if lanes_from == 0:
            odd = pltpu.roll(odd, HEAD_SIZE, 1)
        else:
            even = pltpu.roll(even, HEAD_SIZE, 1)
        tiles.append(jnp.where(first_lanes(even.shape), even, odd))
    return tiles


def visible_chunks(chunk, prefix):
    whole = jnp.maximum(chunk, prefix // CHUNK)
    some = jnp.maximum(chunk + 1, (prefix + CHUNK - 1) // CHUNK)
    return whole, some


def attend_kernel(place_ref, q_ref, kv_ref, *rest):
    o_ref, lse_ref, heads, top, total, acc = rest[-6:]
    place = place_ref[0]
    prefix = place_ref[1 + pl.program_id(0)]
    chunk = pl.program_id(1) ^ place
    for head, tile in enumerate(split_heads(q_ref[0, 0], 0)):
        heads[head] = tile
        top[head] = jnp.full((CHUNK, LANES), MASKED, WIDE)
        total[head] = jnp.zeros((CHUNK, LANES), WIDE)
        acc[head] = jnp.zeros((CHUNK, LANES), WIDE)

    def step(masked, other, carry):
        kv = kv_ref[other ^ place, 0]
        if masked:
            row = lax.broadcasted_iota(jnp.int32, (CHUNK, CHUNK), 0) + chunk * CHUNK
            key = lax.broadcasted_iota(jnp.int32, (CHUNK, CHUNK), 1) + other * CHUNK
            visible = key <= jnp.maximum(row, prefix - 1)
        for head in range(4):
            scores = dot_nt(heads[head], kv)
            if masked:
                scores = jnp.where(visible, scores, MASKED)
            old = top[head]
            new = jnp.maximum(old, jnp.max(scores, axis=1, keepdims=True))
            exponent = jnp.exp(scores - new[:, :1])
            shrink = jnp.exp(old - new)
            top[head] = new
            total[head] = total[head] * shrink + jnp.sum(exponent, axis=1, keepdims=True)
            acc[head] = acc[head] * shrink + jnp.dot(
                exponent.astype(LOW), kv, preferred_element_type=WIDE
            )
        return carry

    whole, some = visible_chunks(chunk, prefix)
    lax.fori_loop(0, whole, functools.partial(step, False), 0)
    lax.fori_loop(whole, some, functools.partial(step, True), 0)
    lane = lax.broadcasted_iota(jnp.int32, (CHUNK, LANES), 1)
    logs = jnp.zeros((CHUNK, LANES), WIDE)
    results = []
    for head in range(4):
        results.append(acc[head] / total[head])
        logs = jnp.where(lane == head, top[head] + jnp.log(total[head]), logs)
    lse_ref[0, 0] = jnp.transpose(logs)[:8]
    for pair, tile in enumerate(join_heads(results, HEAD_SIZE)):
        o_ref[0, 0, :, pair * LANES : (pair + 1) * LANES] = tile.astype(LOW)


def attend(spot, packed, holds=()):
    units = 2 * 4 * 10
    return pl.pallas_call(
        attend_kernel,
        grid_spec=pltpu.PrefetchScalarGridSpec(
            num_scalar_prefetch=1,
            grid=(2, 4),
            in_specs=[
                pl.BlockSpec((1, 1, CHUNK, 2 * LANES), lambda i, j, *_: (j, i, 0, 0)),
                pl.BlockSpec((4, 1, CHUNK, LANES), lambda i, j, *_: (0, i, 0, 2)),
            ]
            + [pl.BlockSpec(memory_space=pl.ANY)] * len(holds),
            out_specs=[
                pl.BlockSpec((1, 1, CHUNK, 2 * LANES), lambda i, j, *_: (j, i, 0, 0)),
                pl.BlockSpec((1, 1, 8, CHUNK), lambda i, j, *_: (j, i, 0, 0)),
            ],
            scratch_shapes=[
                pltpu.VMEM((4, CHUNK, LANES), LOW),
                pltpu.VMEM((4, CHUNK, LANES), WIDE),
                pltpu.VMEM((4, CHUNK, LANES), WIDE),
                pltpu.VMEM((4, CHUNK, LANES), WIDE),
            ],
        ),
        out_shape=[
            jax.ShapeDtypeStruct((4, 2, CHUNK, 2 * LANES), LOW),
            jax.ShapeDtypeStruct((4, 2, 8, CHUNK), WIDE),
        ],
        compiler_params=pltpu.CompilerParams(vmem_limit_bytes=VMEM_BYTES),
        cost_estimate=pl.CostEstimate(
            flops=int(units * 4 * CHUNK * CHUNK * 256 * 2 * 2 * COST_SHARE),
            bytes_accessed=1024 * 1024,
            transcendentals=0,
        ),
    )(spot, packed, packed, *holds)


def attend_back_kernel(
    sequence, place_ref, q_ref, kv_ref, o_ref, do_ref, lse_ref, cosine_ref, sine_ref, *rest
):
    out_ref, heads, grads, deltas, q_acc, kv_acc = rest[-6:]
    slot = pl.program_id(0)
    place = place_ref[0]
    prefix = place_ref[1 + sequence]
    chunk = slot ^ place

    @pl.when(slot == 0)
    def _():
        kv_acc[...] = jnp.zeros_like(kv_acc)

    ones = jnp.ones((8, LANES), WIDE)
    out_heads = split_heads(o_ref[0, 0], HEAD_SIZE)
    grad_heads = split_heads(do_ref[0, 0], HEAD_SIZE)
    for head, tile in enumerate(split_heads(q_ref[0, 0], 0)):
        heads[head] = tile
        grads[head] = grad_heads[head]
        product = out_heads[head].astype(WIDE) * grad_heads[head].astype(WIDE)
        deltas[head] = lax.dot_general(
            ones,
            product,
            (((1,), (1,)), ((), ())),
            precision=lax.Precision.HIGHEST,
            preferred_element_type=WIDE,
        )
        q_acc[head] = jnp.zeros((CHUNK, LANES), WIDE)

    def step(masked, other, carry):
        other_slot = other ^ place
        kv = kv_ref[other_slot, 0]
        if masked:
            key = lax.broadcasted_iota(jnp.int32, (CHUNK, CHUNK), 0) + other * CHUNK
            row = lax.broadcasted_iota(jnp.int32, (CHUNK, CHUNK), 1) + chunk * CHUNK
            visible = key <= jnp.maximum(row, prefix - 1)
        for head in range(4):
            scores = dot_nt(kv, heads[head])
            if masked:
                scores = jnp.where(visible, scores, MASKED)
            probability = jnp.exp(scores - lse_ref[0, 0, head : head + 1])
            grad_prob = dot_nt(kv, grads[head])
            grad_scores = (probability * (grad_prob - deltas[head][:1])).astype(LOW)
            kv_acc[other_slot] += jnp.dot(
                grad_scores, heads[head], preferred_element_type=WIDE
            ) + jnp.dot(probability.astype(LOW), grads[head], preferred_element_type=WIDE)
            q_acc[head] += dot_tn(grad_scores, kv)
        return carry

    whole, some = visible_chunks(chunk, prefix)
    lax.fori_loop(0, whole, functools.partial(step, False), 0)
    lax.fori_loop(whole, some, functools.partial(step, True), 0)
    cosine = cosine_ref[slot]
    sine = sine_ref[slot]
    for pair, tile in enumerate(join_heads([q_acc[head] for head in range(4)], 0)):
        tile = tile * ATTN_SCALE
        turned = tile * cosine + partner_lanes(tile * sine)
        out_ref[slot, :, pair * LANES : (pair + 1) * LANES] = turned.astype(LOW)

    @pl.when(slot == 3)
    def _():
        for other in range(4):
            tile = kv_acc[other]
            turned = tile * cosine_ref[other] + partner_lanes(tile * sine_ref[other])
            turned = jnp.where(first_lanes(tile.shape), turned, tile)
            out_ref[other, :, 2 * LANES :] = turned.astype(LOW)


def attend_grad(sequence, spot, packed, attended, grad_attended, logsum, cosine, sine, holds=()):
    units = 4 * 10
    tile = pl.BlockSpec((1, 1, CHUNK, 2 * LANES), lambda j, *_: (j, sequence, 0, 0))
    table = pl.BlockSpec((4, CHUNK, LANES), lambda j, *_: (0, 0, 0))
    return pl.pallas_call(
        functools.partial(attend_back_kernel, sequence),
        grid_spec=pltpu.PrefetchScalarGridSpec(
            num_scalar_prefetch=1,
            grid=(4,),
            in_specs=[
                tile,
                pl.BlockSpec((4, 1, CHUNK, LANES), lambda j, *_: (0, sequence, 0, 2)),
                tile,
                tile,
                pl.BlockSpec((1, 1, 8, CHUNK), lambda j, *_: (j, sequence, 0, 0)),
                table,
                table,
            ]
            + [pl.BlockSpec(memory_space=pl.ANY)] * len(holds),
            out_specs=pl.BlockSpec((4, CHUNK, 3 * LANES), lambda j, *_: (0, 0, 0)),
            scratch_shapes=[
                pltpu.VMEM((4, CHUNK, LANES), LOW),
                pltpu.VMEM((4, CHUNK, LANES), LOW),
                pltpu.VMEM((4, 8, CHUNK), WIDE),
                pltpu.VMEM((4, CHUNK, LANES), WIDE),
                pltpu.VMEM((4, CHUNK, LANES), WIDE),
            ],
        ),
        out_shape=jax.ShapeDtypeStruct((4, CHUNK, 3 * LANES), LOW),
        compiler_params=pltpu.CompilerParams(vmem_limit_bytes=VMEM_BYTES),
        cost_estimate=pl.CostEstimate(
            flops=int(units * 4 * CHUNK * CHUNK * 256 * 2 * 5 * COST_SHARE),
            bytes_accessed=1024 * 1024,
            transcendentals=0,
        ),
    )(spot, packed, packed, attended, grad_attended, logsum, cosine, sine, *holds)


def dp_spot(dp):
    return dp.reshape(1)


def step_kernel(spot_ref, factor_ref, grad_ref, weight_ref, moment_ref, square_ref, *outs):
    gradient = grad_ref[0].astype(WIDE) * factor_ref[0, 0]
    following, variance = adam(
        weight_ref[...], gradient, moment_ref[...], square_ref[...], DECAY, LEARN
    )
    outs[0][...] = gradient
    outs[1][...] = following
    outs[2][...] = variance


def step_weight(spot, factor, pieces, axis, weight, moment, square):
    count, rows, columns = pieces.shape
    block_rows = min(rows, (1 << 19) // columns)
    parts = rows // block_rows

    def piece_at(block, part, spot_ref):
        code = spot_ref[0]
        return (block ^ ((code % 2) * 2 + code // 2), part, 0)

    def weight_at(block, part, spot_ref):
        return (part, block) if axis == 1 else (block * parts + part, 0)

    spec = pl.BlockSpec((block_rows, columns), weight_at)
    return pl.pallas_call(
        step_kernel,
        grid_spec=pltpu.PrefetchScalarGridSpec(
            num_scalar_prefetch=1,
            grid=(count, parts),
            in_specs=[
                pl.BlockSpec(memory_space=pltpu.SMEM),
                pl.BlockSpec((1, block_rows, columns), piece_at),
                spec,
                spec,
                spec,
            ],
            out_specs=[spec] * 3,
        ),
        out_shape=[jax.ShapeDtypeStruct(weight.shape, WIDE)] * 3,
        compiler_params=pltpu.CompilerParams(vmem_limit_bytes=VMEM_BYTES),
        cost_estimate=pl.CostEstimate(
            flops=12 * weight.size, bytes_accessed=26 * weight.size, transcendentals=weight.size
        ),
    )(spot, factor, pieces, weight, moment, square)


def step_pair_kernel(spot_ref, factor_ref, grad_ref, *refs):
    core, start = spot_ref[0], spot_ref[1]
    factor = factor_ref[0, 0]
    for group in range(4):
        turned = group ^ start
        slot = turned // 2 + (turned % 2) * 2
        first = grad_ref[core * 4 + slot].astype(WIDE) * factor
        second = grad_ref[(1 - core) * 4 + slot].astype(WIDE) * factor
        low = first_lanes(first.shape)
        lanes = pl.ds(group * LANES, LANES)
        key_grad = jnp.where(low, first, pltpu.roll(second, HEAD_SIZE, 1))
        value_grad = jnp.where(low, pltpu.roll(first, HEAD_SIZE, 1), second)
        for gradient, at in ((key_grad, 0), (value_grad, 1)):
            weight_ref, moment_ref, square_ref = refs[3 * at : 3 * at + 3]
            following, variance = adam(
                weight_ref[:, lanes],
                gradient,
                moment_ref[:, lanes],
                square_ref[:, lanes],
                DECAY,
                LEARN,
            )
            outs = refs[6 + 3 * at : 9 + 3 * at]
            outs[0][:, lanes] = gradient
            outs[1][:, lanes] = following
            outs[2][:, lanes] = variance


def step_pair(spot, factor, pieces, key, value):
    rows, columns = key[0].shape
    block_rows = 128
    spec = pl.BlockSpec((block_rows, columns), lambda i, *_: (i, 0))
    outs = pl.pallas_call(
        step_pair_kernel,
        grid_spec=pltpu.PrefetchScalarGridSpec(
            num_scalar_prefetch=1,
            grid=(rows // block_rows,),
            in_specs=[
                pl.BlockSpec(memory_space=pltpu.SMEM),
                pl.BlockSpec((8, block_rows, LANES), lambda i, *_: (0, i, 0)),
            ]
            + [spec] * 6,
            out_specs=[spec] * 6,
        ),
        out_shape=[jax.ShapeDtypeStruct((rows, columns), WIDE)] * 6,
        compiler_params=pltpu.CompilerParams(vmem_limit_bytes=VMEM_BYTES),
        cost_estimate=pl.CostEstimate(
            flops=24 * rows * columns,
            bytes_accessed=52 * rows * columns,
            transcendentals=2 * rows * columns,
        ),
    )(spot, factor, pieces, *key, *value)
    return outs[:3], outs[3:]


def slot_tables(place):
    half = HEAD_SIZE // 2
    frequency = THETA ** (-(jnp.arange(half, dtype=WIDE) * 2.0 / HEAD_SIZE))
    chunk = jnp.arange(4, dtype=jnp.int32) ^ place
    position = (chunk[:, None] * CHUNK + jnp.arange(CHUNK)[None, :]).astype(WIDE)
    angles = position[:, :, None] * frequency[None, None, :]
    cosine, sine = jnp.cos(angles), jnp.sin(angles)
    return (
        jnp.concatenate([cosine] * 4, axis=2),
        jnp.concatenate([-sine, sine, -sine, sine], axis=2),
    )


def exchange(pieces):
    return [
        pieces[0],
        swap_x(pieces[1]),
        swap_near(pieces[2]),
        swap_corner(pieces[3]),
    ]


def rows_norm(values):
    factor = lax.rsqrt(
        jnp.sum(values * values, axis=1, keepdims=True) / MODEL_WIDTH + EPS_NORM
    )
    return values * factor, factor


def rows_norm_back(gradient, normed, factor, gain_row):
    weighted = gradient * gain_row
    inner = jnp.sum(weighted * normed, axis=1, keepdims=True) / MODEL_WIDTH
    return factor * (weighted - normed * inner), jnp.sum(gradient * normed, axis=0)


def swapped_shards(
    tokens,
    cotangent,
    prefix,
    query_weight,
    key_projection,
    value_projection,
    out_weight,
    gate_weight,
    up_weight,
    down_weight,
    norm_gains,
    query_moment,
    key_first_moment,
    value_first_moment,
    out_moment,
    gate_moment,
    up_moment,
    down_moment,
    gains_moment,
    query_square,
    key_second_moment,
    value_second_moment,
    out_square,
    gate_square,
    up_square,
    down_square,
    gains_square,
):
    row = lax.axis_index("row")
    col = lax.axis_index("col")
    dp = lax.axis_index("dp")
    core = dp % 2
    side = dp // 2
    near = col % 2
    far = col // 2
    place = near * 2 + row
    half_rows = tokens.shape[0] // 2
    half_width = tokens.shape[1]

    swapped = [1, 0, 3, 2]
    wide = 3 * LANES
    owner = [col ^ (2 * row), col ^ (2 - 2 * row), col ^ (1 + 2 * row), col ^ (3 - 2 * row)]

    def reorder(blocks):
        return jnp.stack([blocks[place_at] for place_at in swapped])

    def ordered_halves(matrix, axis):
        start = core * 2 * LANES
        return jnp.concatenate(
            [
                cut(matrix, start + side * LANES, LANES, axis),
                cut(matrix, start + (1 - side) * LANES, LANES, axis),
            ],
            axis=axis,
        ).astype(LOW)

    def halves_of(values):
        own = cut(values, row * half_rows, half_rows, 0)
        return own, cut(values, (1 - row) * half_rows, half_rows, 0)

    def leave(values, others):
        back = after(swap_x(after(values[:, half_width:], others[0])), others[1])
        return in_order(row, values[:, :half_width], back, 0)

    def add_low(kept, got):
        return (kept.astype(WIDE) + got.astype(WIDE)).astype(LOW)

    own_rows, other_rows = halves_of(tokens)
    got_rows = swap_x(other_rows)
    gains = jnp.concatenate([norm_gains, swap_x(norm_gains)], axis=1)
    prefixes = [prefix[far], swap_core(prefix)[far]]
    spot = jnp.stack([place, *prefixes])
    cosine, sine = slot_tables(place)

    def heads_of(matrix):
        return jnp.stack(
            [cut(matrix, (at * 2 + core) * HEAD_SIZE, HEAD_SIZE, 1) for at in owner]
        ).astype(LOW)

    kv_own = jnp.concatenate([heads_of(key_projection), heads_of(value_projection)], axis=2)
    kv_other = swap_x(reorder(kv_own))

    def far_pair(block, other):
        return jnp.stack([jnp.where(row == 0, block, other), jnp.where(row == 0, other, block)])

    units = gate_weight.shape[1] // 2

    def hidden_low(matrix, axis, which):
        start = core * units + (side if which == 0 else 1 - side) * (units // 2)
        return cut(matrix, start, units // 2, axis).astype(LOW)

    pair_own = [
        jnp.stack([hidden_low(gate_weight, 1, which), hidden_low(up_weight, 1, which)])
        for which in range(2)
    ]
    down_own = [hidden_low(down_weight, 0, which) for which in range(2)]
    q_low, o_low = ordered_halves(query_weight, 1), ordered_halves(out_weight, 0)

    q_far = swap_far(q_low)
    q_pair = after(far_pair(q_low, q_far), kv_other)
    q_near = swap_near(q_pair)
    q_pair_x = swap_x(jnp.stack([q_pair[1, :, :LANES], q_pair[0, :, :LANES]]))
    q_near_x = swap_near(after(q_pair_x, q_near))
    q_pair_y = swap_y(q_pair_x)
    pair_x = swap_x(after(pair_own[0], q_pair_x))
    q_near_y = swap_y(after(q_near_x, q_pair_y))
    o_far = swap_far(after(o_low, q_near_x))
    pair_far = swap_far(after(pair_own[0], o_far))
    o_pair = far_pair(o_low, o_far)
    o_near = swap_near(o_pair)

    in_pieces = (
        jnp.concatenate([q_pair, q_near]),
        kv_own,
        jnp.concatenate([q_pair_x, q_near_x]),
        jnp.concatenate([q_pair_y, q_near_y]),
        kv_other,
    )

    def exchange(pieces):
        return [
            pieces[0],
            swap_x(pieces[1]),
            swap_near(pieces[2]),
            swap_corner(pieces[3]),
        ]

    def tokens_of(pieces):
        return jnp.concatenate(exchange([pieces[slot] for slot in range(4)]), axis=1)

    def slots_of(values):
        size = values.shape[1] // 4
        return jnp.stack(exchange([values[:, at * size : (at + 1) * size] for at in range(4)]))

    x = jnp.concatenate([own_rows, after(got_rows, q_pair_x)], axis=1).astype(WIDE)
    normed_one, factor_one = rows_norm(x)
    h_own = (normed_one * gains[0]).astype(LOW)
    h_one = [h_own, swap_core(h_own)]
    h_pair = jnp.stack(h_one)
    projected = project(h_pair, in_pieces, cosine, sine)
    pair_x_y = swap_y(after(pair_x, projected))
    packed = jnp.stack(exchange([projected[slot] for slot in range(4)]))
    packed = after(packed, pair_far, pair_x_y, o_near)
    pair_far_x = swap_x(after(pair_far, packed))
    pair_far_y = swap_y(after(pair_far, packed))
    o_own = jnp.concatenate([o_pair, o_near])
    o_first = swap_x(after(reorder(o_own[:, :LANES]), packed))
    down_far = swap_far(after(down_own[0], packed))
    attended, logsum = attend(spot, packed)
    attended = after(attended, pair_far_x, pair_far_y, o_first, down_far)
    o_second = swap_y(after(o_first, attended))
    o_back = jnp.concatenate(exchange([attended[slot] for slot in range(4)]), axis=2)
    pair_far_xy = swap_y(after(pair_far_x, o_second))
    o_tokens = [o_back[0], o_back[1]]
    out_weights = jnp.concatenate(
        [o_own, jnp.concatenate([o_first, o_second], axis=1)], axis=2
    ).reshape(4 * 2 * LANES, MODEL_WIDTH)
    out_part = matrix_multiply(o_back.reshape(2 * CHUNK, 4 * 2 * LANES), out_weights)
    residual = x + RESID * fold(out_part[:CHUNK], out_part[CHUNK:], swap_core)
    pairs = (
        ((pair_own[0], pair_far), (pair_x, pair_far_x)),
        ((pair_own[1], pair_far_y), (pair_x_y, pair_far_xy)),
    )

    own_grad, other_grad = halves_of(cotangent)
    got_grad = swap_x(after(other_grad, o_back))
    def columns(values, order, size):
        return jnp.concatenate([values[:, at * size : (at + 1) * size] for at in order], axis=1)

    def rows(values, order, size):
        return jnp.concatenate([values[at * size : (at + 1) * size] for at in order])

    def beyond_of(parts):
        return add_low(parts[0], swap_core(parts[1]))

    def sum_four(parts):
        beyond = swap_near(parts[1])

        def finish(*others):
            own = parts[0][0].astype(WIDE) + swap_core(parts[0][1]).astype(WIDE)
            return own + after(beyond, *others).astype(WIDE)

        return finish

    normed_two, factor_two = rows_norm(residual)
    h_own = (normed_two * gains[1]).astype(LOW)
    h_near = swap_near(h_own)
    h_two = [jnp.concatenate([h_own, swap_core(h_own)]), None]
    down_pair = jnp.stack([down_own[0], down_far])
    down_pair_x = swap_x(after(down_pair, o_back))
    down_far_y = swap_y(after(down_far, pair_far_xy))
    down_pair_xy = swap_y(after(down_pair_x, down_far_y))
    down = (
        ((down_own[0], down_far), (down_pair_x[0], down_pair_x[1])),
        ((down_own[1], down_far_y), (down_pair_xy[0], down_pair_xy[1])),
    )

    hidden, gate_values, up_values = [[], []], [[], []], [[], []]
    for half in range(2):
        if half == 1:
            h_near, got_grad = after(h_near, hidden[0][0]), after(got_grad, hidden[0][0])
            grad_output = jnp.concatenate([own_grad, got_grad], axis=1).astype(WIDE)
            grad_own = (RESID * grad_output).astype(LOW)
            grad_near = swap_near(after(grad_own, h_near))
            h_two[1] = jnp.concatenate([h_near, swap_core(h_near)])
        for which in range(2):
            one, two, three = hidden_units(h_two[half], pairs[which])
            hidden[which].append(one)
            gate_values[which].append(two)
            up_values[which].append(three)

    grad_near = after(grad_near, hidden[0][1])
    grad_mlp = [
        jnp.concatenate([grad_own, swap_core(grad_own)]),
        jnp.concatenate([grad_near, swap_core(grad_near)]),
    ]
    down_sent, down_kept = [
        weight_grad(hidden[which], 0, [grad_mlp], units) for which in (1, 0)
    ]
    part_rows = units // 2
    down_y = swap_y(down_sent[:part_rows])
    down_x = swap_x(
        jnp.concatenate([down_kept[part_rows:, half_width:], down_sent[part_rows:, half_width:]])
    )
    down_first = down_kept[:part_rows]
    down_second = jnp.concatenate(
        [down_kept[part_rows:, :half_width], down_sent[part_rows:, :half_width]]
    )
    down_pair_xy = after(down_pair_xy, down_kept)
    down = (
        ((down_own[0], down_far), (down_pair_x[0], down_pair_x[1])),
        ((down_own[1], down_far_y), (down_pair_xy[0], down_pair_xy[1])),
    )


    grad_gate, grad_up = [[None, None], [None, None]], [[None, None], [None, None]]
    for half in (1, 0):
        grads_here = after(grad_mlp[half], down_sent, down_kept)
        for which in range(2):
            grad_gate[which][half], grad_up[which][half] = hidden_back(
                grads_here, down[which], gate_values[which][half], up_values[which][half]
            )
    up_sent = weight_grad(h_two, 1, grad_up, half_width)
    gate_sent = weight_grad(h_two, 0, grad_gate[1:], MODEL_WIDTH)
    h_two_parts = [None, None]

    def back_of(half, *others):
        grads = [[after(kind[which][half], *others) for which in range(2)]
                 for kind in (grad_gate, grad_up)]
        return normed_back(*grads, pairs)

    h_two_parts[1] = back_of(1, up_sent, gate_sent)
    h_two_beyond = beyond_of(h_two_parts[1])
    down_y, down_x = after(down_y, *h_two_parts[1]), after(down_x, *h_two_parts[1])
    down_first = [
        add_low(down_first[:, at * half_width : (at + 1) * half_width],
                down_y[:, at * half_width : (at + 1) * half_width])
        for at in range(2)
    ]
    down_second = [
        add_low(down_second[at * part_rows : (at + 1) * part_rows],
                down_x[at * part_rows : (at + 1) * part_rows])
        for at in range(2)
    ]
    h_two_parts[0] = back_of(0, h_two_beyond, *down_first, *down_second)
    h_two_sum = sum_four((h_two_parts[0], h_two_beyond))
    hidden_late = [[after(value, *h_two_parts[0]) for value in values] for values in hidden]
    down_parts = [
        down_units([hidden_late[0][half], hidden_late[1][half]], down) for half in (1, 0)
    ][::-1]
    up_kept = weight_grad([after(value, *h_two_parts[0]) for value in h_two], 0, grad_up, half_width)
    up_sum_x = swap_x(up_sent)
    gate_got_y = swap_y(after(gate_sent[:, :part_rows], down_y))
    down_first_x, down_second_y = swap_x(down_first[1]), swap_y(down_second[1])

    grad_mid_part, gain_two_part = rows_norm_back(
        h_two_sum(up_kept, *down_parts[0], *down_parts[1]), normed_two, factor_two, gains[1]
    )
    grad_mid = grad_output + grad_mid_part

    grad_attended = [(RESID * grad_mid).astype(LOW)]
    gate_kept = weight_grad(
        [after(value, grad_attended[0]) for value in h_two], 0, grad_gate[:1], MODEL_WIDTH
    )
    gate_got_x = swap_x(
        jnp.concatenate([gate_kept[half_width:, part_rows:], gate_sent[half_width:, part_rows:]])
    )
    layer_sum = sum_four((down_parts[0], beyond_of(down_parts[1])))
    grad_attended.append(swap_core(grad_attended[0]))
    head_grad = right_product(jnp.concatenate(grad_attended), out_weights).astype(LOW)
    head_grad = head_grad.reshape(2, CHUNK, 4 * 2 * LANES)
    head_grad = jnp.stack(
        exchange([head_grad[:, :, at * 2 * LANES : (at + 1) * 2 * LANES] for at in range(4)])
    )
    out_local = [
        weight_grad(o_tokens, 0, [[values[:, half * half_width : (half + 1) * half_width]
                                   for values in grad_attended]], 4 * 2 * LANES)
        for half in range(2)
    ]
    out_near = swap_near(jnp.concatenate([values[4 * LANES :] for values in out_local], axis=1))
    down_first_x, down_second_y, up_sum_x = (
        after(value, gate_kept) for value in (down_first_x, down_second_y, up_sum_x)
    )
    gate_got_y, gate_got_x = after(gate_got_y, *out_local), after(gate_got_x, *out_local)
    down_part = add_low(down_first[0], down_first_x)
    down_far_sum = swap_far(add_low(down_second[0], down_second_y))
    size = up_kept.shape[1] // 2
    up_kept = [
        add_low(up_kept[:, at * size : (at + 1) * size], up_sum_x[:, at * size : (at + 1) * size])
        for at in range(2)
    ]
    gate_first = add_low(gate_kept[:half_width, :part_rows], gate_got_y[:half_width])
    gate_second = add_low(gate_kept[:half_width, part_rows:], gate_got_x[:half_width])
    gate_first_x = swap_x(add_low(gate_kept[half_width:, :part_rows], gate_got_y[half_width:]))
    gate_second_y = swap_y(add_low(gate_sent[:half_width, part_rows:], gate_got_x[half_width:]))
    up_sum_y = swap_y(up_kept[1])

    def sequence_grad(sequence, *others):
        return attend_grad(
            sequence,
            spot,
            packed,
            attended,
            after(head_grad, *others),
            logsum,
            cosine,
            sine,
        )

    packed_first = sequence_grad(0, down_part, *up_kept, gate_first, gate_second)
    gate_first_x, gate_second_y, down_far_sum, out_near = (
        after(value, packed_first)
        for value in (gate_first_x, gate_second_y, down_far_sum, out_near)
    )
    gate_first = add_low(gate_first, gate_first_x)
    gate_far_sum = swap_far(add_low(gate_second, gate_second_y))
    in_first = tokens_of(packed_first)
    packed_second = sequence_grad(1, gate_first)
    gate_far_sum, in_first, up_sum_y = (
        after(value, packed_second) for value in (gate_far_sum, in_first, up_sum_y)
    )
    up_part = add_low(up_kept[0], up_sum_y)
    up_far_sum = swap_far(after(up_part[:, units // 2 :], gate_far_sum))
    layer_part = (residual + RESID * layer_sum(packed_second)).astype(LOW)
    in_back = jnp.stack([in_first, tokens_of(after(packed_second, gate_far_sum, up_part))])
    down_piece = add_low(down_part, down_far_sum)
    gate_piece = add_low(gate_first, gate_far_sum)
    up_piece = add_low(up_part[:, : units // 2], up_far_sum)
    in_grads = [in_back[0], in_back[1]]
    out_kept = add_low(
        jnp.concatenate([values[: 4 * LANES] for values in out_local], axis=1), out_near
    )
    out_kept = add_low(
        out_kept[:, :half_width],
        swap_x(after(rows(out_kept[:, half_width:], [1, 0], 2 * LANES), in_back)),
    )
    in_local = [weight_grad(h_one, half, [in_grads], half_width) for half in (1, 0)][::-1]
    h_one_parts = project_back(after(in_back, up_far_sum), in_pieces)
    grad_in_part, gain_one_part = rows_norm_back(
        h_one_parts[0].astype(WIDE) + swap_core(h_one_parts[1]).astype(WIDE), normed_one, factor_one, gains[0]
    )
    input_part = (grad_mid + grad_in_part).astype(LOW)

    def spread(piece):
        pair = jnp.stack([piece, after(swap_y(piece), h_one_parts)])
        return jnp.concatenate([pair, swap_core(pair)])


    pair = 2 * LANES
    first_cut, second_cut = half_width * 3 // 8, half_width * 5 // 8

    def keep_side(values, got):
        size = values.shape[1] // wide
        kept = jnp.concatenate(
            [
                jnp.concatenate(
                    [
                        values[:, at * wide : at * wide + LANES],
                        values[:, at * wide + pair : (at + 1) * wide],
                    ],
                    axis=1,
                )
                for at in range(size)
            ],
            axis=1,
        )
        return add_low(kept, got)

    def for_side(values):
        size = values.shape[1] // wide
        return jnp.concatenate(
            [values[:, at * wide + LANES : (at + 1) * wide] for at in range(size)], axis=1
        )

    def rows_of(start, stop):
        return [values[start:stop] for values in in_local]

    def near_halves(values):
        size = values.shape[1] // 2
        return values[:, :size], values[:, size:]

    part = rows_of(0, first_cut)
    part = add_low(part[0], swap_x(columns(part[1], swapped, wide)))
    part = keep_side(part, swap_y(for_side(part)))
    kept, sent = near_halves(part)
    ways = [add_low(kept, swap_near(sent))]

    part = jnp.concatenate(rows_of(first_cut, second_cut))
    part = keep_side(part, swap_y(for_side(part)))
    kept, sent = near_halves(part)
    part = add_low(kept, swap_near(sent))
    size = second_cut - first_cut
    ways.append(add_low(part[:size], swap_x(columns(part[size:], [1, 0], pair))))

    part = jnp.concatenate(rows_of(second_cut, half_width))
    kept, sent = near_halves(part)
    part = add_low(kept, swap_near(sent))
    size = half_width - second_cut
    part = add_low(part[:size], swap_x(columns(part[size:], [1, 0], wide)))
    ways.append(keep_side(part, swap_y(for_side(part))))

    in_part = jnp.concatenate(ways)
    in_part = add_low(
        jnp.where(row == 0, in_part[:, :pair], in_part[:, pair:]),
        swap_far(jnp.where(row == 0, in_part[:, pair:], in_part[:, :pair])),
    )
    query_piece = in_part[:, :LANES]
    kv_piece = in_part[:, LANES:]

    out_part = add_low(
        jnp.where(row == 0, out_kept[:pair], out_kept[pair:]),
        swap_far(jnp.where(row == 0, out_kept[pair:], out_kept[:pair])),
    )
    out_piece = add_low(out_part[:LANES], swap_y(out_part[LANES:]))

    gain_sums = jnp.stack([gain_one_part, gain_two_part]).reshape(2, 2, 8, half_width // 8)
    gain_sums = gain_sums[:, 0] + swap_x(gain_sums[:, 1])
    for move in (swap_y, swap_core, swap_near, swap_far):
        gain_sums = gain_sums + move(gain_sums)
    gains_total = gain_sums.reshape(2, half_width)

    kv_pieces = jnp.stack([kv_piece, swap_far(kv_piece)])
    kv_pieces = jnp.concatenate([kv_pieces, swap_near(kv_pieces)])
    kv_pieces = jnp.concatenate([kv_pieces, swap_core(kv_pieces)])

    def squares_of(values):
        values = values.astype(WIDE)
        return jnp.sum(values * values)

    square_local = jnp.where(side == 0, squares_of(kv_piece), 0.0)
    square_local = square_local + jnp.where((col == 0) & (dp == 0), squares_of(gains_total), 0.0)
    for piece in (query_piece, out_piece, gate_piece, up_piece, down_piece):
        square_local = square_local + squares_of(piece)
    square_local = jnp.full((8, LANES), square_local, WIDE)
    for move in (swap_y, swap_core):
        square_local = square_local + move(square_local)
    grad_norm = jnp.sqrt(lax.psum(square_local[0, 0], ("row", "col")))
    factor = jnp.minimum(1.0, CLIP / grad_norm)
    factor_cell = factor.reshape(1, 1)
    spot = dp_spot(dp)

    def step(piece, axis, weight, moment, square):
        return step_weight(spot, factor_cell, spread(piece), axis, weight, moment, square)

    query_out = step(query_piece, 1, query_weight, query_moment, query_square)
    out_out = step(out_piece, 0, out_weight, out_moment, out_square)
    gate_out = step(gate_piece, 1, gate_weight, gate_moment, gate_square)
    up_out = step(up_piece, 1, up_weight, up_moment, up_square)
    down_out = step(down_piece, 0, down_weight, down_moment, down_square)
    layer_out = leave(layer_part, (in_part, up_out[0]))
    input_grad = leave(input_part, (in_part, up_out[0]))
    kv_spot = jnp.stack([core, col])
    key_out, value_out = step_pair(
        kv_spot,
        factor_cell,
        kv_pieces,
        (key_projection, key_first_moment, key_second_moment),
        (value_projection, value_first_moment, value_second_moment),
    )
    results = (query_out, key_out, value_out, out_out, gate_out, up_out, down_out)
    clipped, nexts, variances = zip(*results)
    gains_grad = gains_total * factor
    gains_next, gains_variance = adam(
        norm_gains, gains_grad, gains_moment, gains_square, 0.0, GAINS_LEARN
    )
    return (
        layer_out,
        input_grad,
        *clipped,
        gains_grad,
        *nexts,
        gains_next,
        *variances,
        gains_variance,
        grad_norm,
    )


def solution(mesh):
    placed = (
        P(("dp", "col"), "row"),
        P(("dp", "col"), "row"),
        P("dp"),
        P("row", "col"),
        P("row", None),
        P("row", None),
        P("col", "row"),
        P("row", "col"),
        P("row", "col"),
        P("col", "row"),
        P(None, "row"),
        P("row", "col"),
        P("row", None),
        P("row", None),
        P("col", "row"),
        P("row", "col"),
        P("row", "col"),
        P("col", "row"),
        P(None, "row"),
        P("row", "col"),
        P("row", None),
        P("row", None),
        P("col", "row"),
        P("row", "col"),
        P("row", "col"),
        P("col", "row"),
        P(None, "row"),
    )
    return jax.shard_map(
        swapped_shards if swaps_fit(mesh) else shards,
        mesh=mesh,
        in_specs=placed,
        out_specs=(
            P(("dp", "col"), "row"),
            P(("dp", "col"), "row"),
            P("row", "col"),
            P("row", None),
            P("row", None),
            P("col", "row"),
            P("row", "col"),
            P("row", "col"),
            P("col", "row"),
            P(None, "row"),
            P("row", "col"),
            P("row", None),
            P("row", None),
            P("col", "row"),
            P("row", "col"),
            P("row", "col"),
            P("col", "row"),
            P(None, "row"),
            P("row", "col"),
            P("row", None),
            P("row", None),
            P("col", "row"),
            P("row", "col"),
            P("row", "col"),
            P("col", "row"),
            P(None, "row"),
            P(),
        ),
        check_vma=False,
    )
```

```python
import functools

import jax
import jax.numpy as jnp
from jax import lax
from jax.experimental import pallas as pl
from jax.experimental.pallas import tpu as pltpu
from jax.sharding import PartitionSpec as P

MODEL_WIDTH = 2048
QUERY_HEADS = 32
KEY_VALUE_HEADS = 8
HEAD_SIZE = 64
SEQUENCE_LENGTH = 2048
STEP = 5


EPS_NORM = 1e-05
RESID = 0.22
ATTN_SCALE = 1.0 / 64.0
THETA = 10000000.0
LEARN = 0.1
GAINS_LEARN = 0.5
BETA_ONE = 0.5
BETA_TWO = 0.5
ADAM_EPS = 1e-08
DECAY = 0.1
CLIP = 1.0


def matrix_multiply(left_side, right_side):
    return jnp.dot(left_side, right_side, preferred_element_type=jnp.float32)


def left_product(left_side, right_side):
    return lax.dot_general(
        left_side, right_side, (((0,), (0,)), ((), ())), preferred_element_type=jnp.float32
    )


def right_product(left_side, right_side):
    return lax.dot_general(
        left_side, right_side, (((1,), (1,)), ((), ())), preferred_element_type=jnp.float32
    )


def width_total(values):
    return lax.psum(values, "row")


def gather_tokens(values):
    return lax.all_gather(values, "col", axis=0, tiled=True)


def sum_tokens(term, tok_rows):
    return lax.psum_scatter(
        term(jnp.int32(0), lax.axis_size("col") * tok_rows).astype(jnp.bfloat16),
        "col",
        scatter_dimension=0,
        tiled=True,
    ).astype(jnp.float32)


def fetch_weights(first, second, third, fourth, fifth):
    return (
        lax.all_gather(first, "row", axis=0, tiled=True),
        lax.all_gather(second, "row", axis=0, tiled=True),
        lax.all_gather(third, "row", axis=0, tiled=True),
        lax.all_gather(fourth, "row", axis=1, tiled=True),
        lax.all_gather(fifth, "row", axis=1, tiled=True),
    )


def enter_rows(values):
    return lax.all_to_all(values, "row", split_axis=0, concat_axis=1, tiled=True)


def leave_rows(values):
    return lax.all_to_all(
        values.astype(jnp.bfloat16), "row", split_axis=1, concat_axis=0, tiled=True
    ).astype(values.dtype)


def reduce_rows(first, second, third, fourth, fifth):
    return (
        lax.psum_scatter(first.astype(jnp.bfloat16), "row", scatter_dimension=0, tiled=True).astype(
            jnp.float32
        ),
        lax.psum_scatter(
            second.astype(jnp.bfloat16), "row", scatter_dimension=0, tiled=True
        ).astype(jnp.float32),
        lax.psum_scatter(third.astype(jnp.bfloat16), "row", scatter_dimension=1, tiled=True).astype(
            jnp.float32
        ),
        lax.psum_scatter(
            fourth.astype(jnp.bfloat16), "row", scatter_dimension=0, tiled=True
        ).astype(jnp.float32),
        lax.psum_scatter(fifth.astype(jnp.bfloat16), "row", scatter_dimension=1, tiled=True).astype(
            jnp.float32
        ),
    )


def rope_tables(length):
    half_width = HEAD_SIZE // 2
    frequency = THETA ** (-(jnp.arange(half_width, dtype=jnp.float32) * 2.0 / HEAD_SIZE))
    angles = jnp.arange(length, dtype=jnp.float32)[:, None] * frequency[None, :]
    angles = jnp.concatenate([angles, angles], axis=1)
    return (jnp.cos(angles), jnp.sin(angles))


def rotate(values):
    half_width = values.shape[-1] // 2
    return jnp.concatenate([-values[..., half_width:], values[..., :half_width]], axis=-1)


def rope(values, cosine_table, sine_table):
    return values * cosine_table[:, None, :] + rotate(values) * sine_table[:, None, :]


def rope_back(gradient, cosine_table, sine_table):
    return gradient * cosine_table[:, None, :] - rotate(gradient * sine_table[:, None, :])


def rms_forward(values, gain_row):
    squares = width_total(jnp.sum(values * values, axis=1))
    factor = lax.rsqrt(squares[:, None] / MODEL_WIDTH + EPS_NORM)
    normed = values * factor
    return ((normed * gain_row).astype(jnp.bfloat16), normed, factor)


def rms_backward(grad_normed, normed, factor, gain_row):
    weighted = grad_normed * gain_row
    inner_sum = width_total(jnp.sum(weighted * normed, axis=1))
    grad_input = factor * (weighted - normed * (inner_sum[:, None] / MODEL_WIDTH))
    return (grad_input, jnp.sum(grad_normed * normed, axis=0))


def attend_sequence(
    heads_of_queries, heads_of_keys, heads_of_values, prefix_length, rows_per_block
):
    length = heads_of_keys.shape[0]
    key_place = jnp.arange(length)

    def one_block(inputs):
        query_block, positions = inputs
        scores = jnp.einsum(
            "qhgd,khd->hgqk", query_block, heads_of_keys, preferred_element_type=jnp.float32
        )
        visible = (key_place[None, :] <= positions[:, None]) | (key_place[None, :] < prefix_length)
        scores = jnp.where(visible, scores, -1e30)
        row_max = jnp.max(scores, axis=-1, keepdims=True)
        exponent = jnp.exp(scores - row_max)
        total_sum = jnp.sum(exponent, axis=-1, keepdims=True)
        probability = (exponent / total_sum).astype(jnp.bfloat16)
        result = jnp.einsum(
            "hgqk,khd->qhgd", probability, heads_of_values, preferred_element_type=jnp.float32
        )
        return (result, row_max[..., 0] + jnp.log(total_sum[..., 0]))

    block_count = length // rows_per_block
    shaped = heads_of_queries.reshape((block_count, rows_per_block) + heads_of_queries.shape[1:])
    positions = jnp.arange(length).reshape(block_count, rows_per_block)
    result, logsum = lax.map(one_block, (shaped, positions))
    return (result.reshape(heads_of_queries.shape), logsum)


def attend_back(
    heads_of_queries,
    heads_of_keys,
    heads_of_values,
    prefix_length,
    logsum,
    grad_heads,
    rows_per_block,
):
    length = heads_of_keys.shape[0]
    key_place = jnp.arange(length)
    block_count = length // rows_per_block

    def one_block(carried, inputs):
        query_block, grad_block, logsum_block, positions = inputs
        scores = jnp.einsum(
            "qhgd,khd->hgqk", query_block, heads_of_keys, preferred_element_type=jnp.float32
        )
        visible = (key_place[None, :] <= positions[:, None]) | (key_place[None, :] < prefix_length)
        scores = jnp.where(visible, scores, -1e30)
        probability = jnp.exp(scores - logsum_block[..., None])
        grad_prob = jnp.einsum(
            "qhgd,khd->hgqk", grad_block, heads_of_values, preferred_element_type=jnp.float32
        )
        delta_sum = jnp.sum(probability * grad_prob, axis=-1, keepdims=True)
        grad_scores = (probability * (grad_prob - delta_sum)).astype(jnp.bfloat16)
        grad_query = jnp.einsum(
            "hgqk,khd->qhgd", grad_scores, heads_of_keys, preferred_element_type=jnp.float32
        )
        grad_keys = jnp.einsum(
            "hgqk,qhgd->khd", grad_scores, query_block, preferred_element_type=jnp.float32
        )
        grad_values = jnp.einsum(
            "hgqk,qhgd->khd",
            probability.astype(jnp.bfloat16),
            grad_block,
            preferred_element_type=jnp.float32,
        )
        return ((carried[0] + grad_keys, carried[1] + grad_values), grad_query)

    block_shape = (block_count, rows_per_block) + heads_of_queries.shape[1:]
    initial = (
        jnp.zeros(heads_of_keys.shape, jnp.float32),
        jnp.zeros(heads_of_values.shape, jnp.float32),
    )
    positions = jnp.arange(length).reshape(block_count, rows_per_block)
    inputs = (
        heads_of_queries.reshape(block_shape),
        grad_heads.reshape(block_shape),
        logsum,
        positions,
    )
    (grad_keys, grad_values), grad_query = lax.scan(one_block, initial, inputs)
    return (grad_query.reshape(heads_of_queries.shape), grad_keys, grad_values)


def adam(weight, gradient, moment_one, moment_two, decay_rate, learn_rate):
    moment_new = BETA_ONE * moment_one + (1.0 - BETA_ONE) * gradient
    square_new = BETA_TWO * moment_two + (1.0 - BETA_TWO) * gradient * gradient
    moment_hat = moment_new / (1.0 - BETA_ONE**STEP)
    square_hat = square_new / (1.0 - BETA_TWO**STEP)
    return (
        weight
        - learn_rate * (moment_hat / (jnp.sqrt(square_hat) + ADAM_EPS) + decay_rate * weight),
        square_new,
    )


def shards(
    tokens,
    cotangent,
    prefix,
    query_weight,
    key_projection,
    value_projection,
    out_weight,
    gate_weight,
    up_weight,
    down_weight,
    norm_gains,
    query_moment,
    key_first_moment,
    value_first_moment,
    out_moment,
    gate_moment,
    up_moment,
    down_moment,
    gains_moment,
    query_square,
    key_second_moment,
    value_second_moment,
    out_square,
    gate_square,
    up_square,
    down_square,
    gains_square,
):
    tok_rows = tokens.shape[0]
    query_cols = query_weight.shape[1]
    kv_all = key_projection.shape[1]
    ffn_cols = gate_weight.shape[1]
    row_size = lax.axis_size("row")
    col_size = lax.axis_size("col")
    row_index = lax.axis_index("row")
    col_index = lax.axis_index("col")
    tok_count = tok_rows * col_size
    seq_count = prefix.shape[0]
    group_width = QUERY_HEADS // KEY_VALUE_HEADS
    rows_per_block = min(512, SEQUENCE_LENGTH)
    col_heads = query_cols // HEAD_SIZE
    frame_used = max(1, col_heads // group_width)
    frame_start = col_index * col_heads // group_width
    frame_width = frame_used * HEAD_SIZE
    key_here = lax.dynamic_slice_in_dim(key_projection, frame_start * HEAD_SIZE, frame_width, 1)
    value_here = lax.dynamic_slice_in_dim(value_projection, frame_start * HEAD_SIZE, frame_width, 1)
    query_mat = query_weight.astype(jnp.bfloat16)
    kv_mat = (
        jnp.stack([key_here, value_here], axis=1)
        .astype(jnp.bfloat16)
        .reshape(key_here.shape[0], 2 * frame_width)
    )
    out_mat = out_weight.astype(jnp.bfloat16)
    ffn_mat = (
        jnp.stack([gate_weight, up_weight], axis=1)
        .astype(jnp.bfloat16)
        .reshape(gate_weight.shape[0], 2 * ffn_cols)
    )
    down_mat = down_weight.astype(jnp.bfloat16)
    gain_one = norm_gains[0]
    gain_two = norm_gains[1]
    query_use, kv_use, ffn_use, out_use, down_use = fetch_weights(
        query_mat, kv_mat, ffn_mat, out_mat, down_mat
    )
    use_rows = tok_count // row_size
    seq_use = seq_count // row_size
    prefix_use = lax.dynamic_slice_in_dim(prefix, row_index * seq_use, seq_use, 0)
    kv_used = max(1, col_heads // group_width)
    group_here = col_heads // kv_used
    cosine_one, sine_one = rope_tables(SEQUENCE_LENGTH)
    cosine_table = jnp.tile(cosine_one, (seq_use, 1))
    sine_table = jnp.tile(sine_one, (seq_use, 1))

    def spread(values):
        return enter_rows(values)

    def to_tokens(product_fn):
        whole = leave_rows(product_fn(0, use_rows))

        def term(start_row, rows_here):
            return whole

        return sum_tokens(term, tok_rows)

    input_float = tokens.astype(jnp.float32)
    hidden_first, normed_one, factor_one = rms_forward(input_float, gain_one)
    h_one_use = spread(gather_tokens(hidden_first))
    query_sum = matrix_multiply(h_one_use, query_use)
    kv_frame = matrix_multiply(h_one_use, kv_use).reshape(use_rows, 2, frame_width)
    query_round = (
        rope(query_sum.reshape(use_rows, col_heads, HEAD_SIZE), cosine_table, sine_table)
        * ATTN_SCALE
    ).astype(jnp.bfloat16)
    key_round = rope(
        kv_frame[:, 0].reshape(use_rows, kv_used, HEAD_SIZE), cosine_table, sine_table
    ).astype(jnp.bfloat16)
    value_round = kv_frame[:, 1].reshape(use_rows, kv_used, HEAD_SIZE).astype(jnp.bfloat16)
    query_seq = query_round.reshape(seq_use, SEQUENCE_LENGTH, kv_used, group_here, HEAD_SIZE)
    key_seq = key_round.reshape(seq_use, SEQUENCE_LENGTH, kv_used, HEAD_SIZE)
    value_seq = value_round.reshape(seq_use, SEQUENCE_LENGTH, kv_used, HEAD_SIZE)

    def forward_sequence(inputs):
        return attend_sequence(inputs[0], inputs[1], inputs[2], inputs[3], rows_per_block)

    attended, logsum = lax.map(forward_sequence, (query_seq, key_seq, value_seq, prefix_use))
    head_round = attended.reshape(use_rows, col_heads * HEAD_SIZE).astype(jnp.bfloat16)

    def out_term(start_row, rows_here):
        return matrix_multiply(head_round, out_use)

    residual_mid = input_float + RESID * to_tokens(out_term)
    h_two, normed_two, factor_two = rms_forward(residual_mid, gain_two)
    h_two_use = spread(gather_tokens(h_two))
    ffn_part = matrix_multiply(h_two_use, ffn_use).reshape(use_rows, 2, ffn_cols)
    gate_value = ffn_part[:, 0]
    up_value = ffn_part[:, 1]
    hidden = (jax.nn.silu(gate_value) * up_value).astype(jnp.bfloat16)

    def down_term(start_row, rows_here):
        return matrix_multiply(hidden, down_use)

    layer_out = (residual_mid + RESID * to_tokens(down_term)).astype(jnp.bfloat16)
    grad_output = cotangent.astype(jnp.float32)
    grad_mlp = (RESID * grad_output).astype(jnp.bfloat16)
    grad_mlp_use = spread(gather_tokens(grad_mlp))
    down_local = left_product(hidden, grad_mlp_use)
    hidden_part = right_product(grad_mlp_use, down_use)
    sigmoid_gate = jax.nn.sigmoid(gate_value)
    grad_gate = hidden_part * up_value * sigmoid_gate * (1.0 + gate_value * (1.0 - sigmoid_gate))
    grad_up = hidden_part * (gate_value * sigmoid_gate)
    grad_pair = jnp.stack([grad_gate, grad_up], axis=1).astype(jnp.bfloat16)
    pair_flat = grad_pair.reshape(use_rows, 2 * ffn_cols)
    ffn_local = left_product(h_two_use, pair_flat).reshape(-1, 2, ffn_cols)

    def ffn_back_term(start_row, rows_here):
        return right_product(pair_flat, ffn_use)

    grad_mid_part, gain_two_part = rms_backward(
        to_tokens(ffn_back_term), normed_two, factor_two, gain_two
    )
    grad_mid = grad_output + grad_mid_part
    grad_attended = (RESID * grad_mid).astype(jnp.bfloat16)
    grad_attended_use = spread(gather_tokens(grad_attended))
    out_local = left_product(head_round, grad_attended_use)
    head_part = right_product(grad_attended_use, out_use)
    head_grad = head_part
    head_grad = head_grad.astype(jnp.bfloat16).reshape(
        seq_use, SEQUENCE_LENGTH, kv_used, group_here, HEAD_SIZE
    )

    def backward_sequence(inputs):
        return attend_back(
            inputs[0], inputs[1], inputs[2], inputs[3], inputs[4], inputs[5], rows_per_block
        )

    query_back, key_back, value_back = lax.map(
        backward_sequence, (query_seq, key_seq, value_seq, prefix_use, logsum, head_grad)
    )
    query_grad_heads = rope_back(
        query_back.reshape(use_rows, col_heads, HEAD_SIZE) * ATTN_SCALE, cosine_table, sine_table
    )
    query_grad_round = query_grad_heads.reshape(use_rows, col_heads * HEAD_SIZE).astype(
        jnp.bfloat16
    )
    key_grad_heads = rope_back(
        key_back.reshape(use_rows, kv_used, HEAD_SIZE), cosine_table, sine_table
    )
    kv_grad_used = jnp.stack(
        [
            key_grad_heads.reshape(use_rows, kv_used * HEAD_SIZE),
            value_back.reshape(use_rows, kv_used * HEAD_SIZE),
        ],
        axis=1,
    )
    kv_grad = kv_grad_used.astype(jnp.bfloat16)
    kv_flat = kv_grad.reshape(use_rows, 2 * frame_width)
    query_local = left_product(h_one_use, query_grad_round)
    kv_frame_local = left_product(h_one_use, kv_flat).reshape(-1, 2, frame_width)
    kv_local = lax.dynamic_update_slice_in_dim(
        jnp.zeros((kv_frame_local.shape[0], 2, kv_all), jnp.float32),
        kv_frame_local,
        frame_start * HEAD_SIZE,
        2,
    )

    def input_term(start_row, rows_here):
        return right_product(query_grad_round, query_use) + right_product(kv_flat, kv_use)

    grad_in_part, gain_one_part = rms_backward(
        to_tokens(input_term), normed_one, factor_one, gain_one
    )
    input_grad = (grad_mid + grad_in_part).astype(jnp.bfloat16)
    local_grads = reduce_rows(query_local, kv_local, out_local, ffn_local, down_local)
    summed = (
        lax.psum(local_grads[0].astype(jnp.bfloat16), "dp").astype(jnp.float32),
        lax.psum(local_grads[2].astype(jnp.bfloat16), "dp").astype(jnp.float32),
        lax.psum(local_grads[3].astype(jnp.bfloat16), "dp").astype(jnp.float32),
        lax.psum(local_grads[4].astype(jnp.bfloat16), "dp").astype(jnp.float32),
    )
    kv_summed, gains_total = lax.psum(
        (local_grads[1], jnp.stack([gain_one_part, gain_two_part])), ("dp", "col")
    )
    raw_grads = (
        summed[0],
        kv_summed[:, 0],
        kv_summed[:, 1],
        summed[1],
        summed[2][:, 0],
        summed[2][:, 1],
        summed[3],
    )
    masters = (
        query_weight,
        key_projection,
        value_projection,
        out_weight,
        gate_weight,
        up_weight,
        down_weight,
    )
    moments = (
        query_moment,
        key_first_moment,
        value_first_moment,
        out_moment,
        gate_moment,
        up_moment,
        down_moment,
    )
    squares = (
        query_square,
        key_second_moment,
        value_second_moment,
        out_square,
        gate_square,
        up_square,
        down_square,
    )
    copied_sum = jnp.sum(gains_total * gains_total) + jnp.sum(kv_summed * kv_summed)
    square_local = jnp.where(col_index == 0, copied_sum, 0.0)
    for position in (0, 3, 4, 5, 6):
        square_local = square_local + jnp.sum(raw_grads[position] * raw_grads[position])
    total_sum = lax.psum(square_local, ("row", "col"))
    grad_norm = jnp.sqrt(total_sum)
    factor = jnp.minimum(1.0, CLIP / grad_norm)
    clipped = []
    nexts = []
    variances = []
    for position in range(7):
        gradient = raw_grads[position] * factor
        weight_next, variance = adam(
            masters[position], gradient, moments[position], squares[position], DECAY, LEARN
        )
        clipped.append(gradient)
        nexts.append(weight_next)
        variances.append(variance)
    gains_grad = gains_total * factor
    gains_next, gains_variance = adam(
        norm_gains, gains_grad, gains_moment, gains_square, 0.0, GAINS_LEARN
    )
    return (
        layer_out,
        input_grad,
        clipped[0],
        clipped[1],
        clipped[2],
        clipped[3],
        clipped[4],
        clipped[5],
        clipped[6],
        gains_grad,
        nexts[0],
        nexts[1],
        nexts[2],
        nexts[3],
        nexts[4],
        nexts[5],
        nexts[6],
        gains_next,
        variances[0],
        variances[1],
        variances[2],
        variances[3],
        variances[4],
        variances[5],
        variances[6],
        gains_variance,
        grad_norm,
    )


LOW = jnp.bfloat16
WIDE = jnp.float32
CHUNK = 512
LANES = 128
MASKED = -1e30
VMEM_BYTES = 48 * 1024 * 1024


def swaps_fit(mesh):
    return dict(mesh.shape) == {"dp": 4, "row": 2, "col": 4}


def swap(values, axis, bit):
    size = lax.axis_size(axis)
    return lax.ppermute(values, axis, [(place, place ^ bit) for place in range(size)])


def swap_core(values):
    return swap(values, "dp", 1)


def swap_y(values):
    return swap(values, "dp", 2)


def swap_x(values):
    return swap(values, "row", 1)


def swap_near(values):
    return swap(values, "col", 1)


def swap_far(values):
    return swap(values, "col", 2)


def swap_corner(values):
    cols = lax.axis_size("col")
    pairs = [
        (row * cols + col, (row ^ 1) * cols + (col ^ 1))
        for row in range(lax.axis_size("row"))
        for col in range(cols)
    ]
    return lax.ppermute(values, ("row", "col"), pairs)


def after(value, *others):
    return lax.optimization_barrier((value,) + others)[0]


def fold(kept, sent, move):
    return kept + move(sent.astype(LOW)).astype(WIDE)


def in_order(place, own, other, axis):
    return jnp.concatenate(
        [jnp.where(place == 0, own, other), jnp.where(place == 0, other, own)], axis=axis
    )


def cut(values, start, size, axis):
    return lax.dynamic_slice_in_dim(values, start, size, axis)


def partner_lanes(values):
    lane = lax.broadcasted_iota(jnp.int32, values.shape, 1)
    half = HEAD_SIZE // 2
    ahead = pltpu.roll(values, values.shape[1] - half, 1)
    behind = pltpu.roll(values, half, 1)
    return jnp.where(lane % HEAD_SIZE < half, ahead, behind)


def first_lanes(shape):
    return lax.broadcasted_iota(jnp.int32, shape, 1) < HEAD_SIZE


def dot_nt(left_side, right_side):
    return lax.dot_general(
        left_side, right_side, (((1,), (1,)), ((), ())), preferred_element_type=WIDE
    )


def dot_tn(left_side, right_side):
    return lax.dot_general(
        left_side, right_side, (((0,), (0,)), ((), ())), preferred_element_type=WIDE
    )


WIDE_BLOCK = 512
COST_SHARE = 1


def one_buffer(shape, index_map):
    return pl.BlockSpec(shape, index_map, pipeline_mode=pl.Buffered(1))


def cost(flops, read, written):
    return pl.CostEstimate(
        flops=int(flops * COST_SHARE),
        bytes_accessed=int(2 * (read + written) * COST_SHARE),
        transcendentals=0,
    )


def mm(left_side, right_side):
    return jnp.dot(left_side, right_side, preferred_element_type=WIDE)


def both(refs, axis):
    return jnp.concatenate([ref[...] for ref in refs], axis=axis)


def flat(*blocks):
    return [array for block in blocks for array in block]


def both_of(refs, which, axis):
    return jnp.concatenate([ref[which] for ref in refs], axis=axis)


def hidden_kernel(normed_ref, *refs):
    hidden_ref, gate_ref, up_ref = refs[4:]
    half = normed_ref.shape[1] // 2
    left, right = normed_ref[:, :half], normed_ref[:, half:]
    gate = mm(left, both_of(refs[0:2], 0, 1)) + mm(right, both_of(refs[2:4], 0, 1))
    up = mm(left, both_of(refs[0:2], 1, 1)) + mm(right, both_of(refs[2:4], 1, 1))
    hidden_ref[...] = (gate * jax.nn.sigmoid(gate) * up).astype(LOW)
    gate_ref[...] = gate.astype(LOW)
    up_ref[...] = up.astype(LOW)


def hidden_units(normed, pairs):
    tokens, width = normed.shape
    weights = flat(*pairs)
    units = 2 * weights[0].shape[2]
    block = WIDE_BLOCK
    weight = one_buffer(weights[0].shape, lambda i: (0, 0, 0))
    out = pl.BlockSpec((block, units), lambda i: (i, 0))
    return pl.pallas_call(
        hidden_kernel,
        grid=(tokens // block,),
        in_specs=[pl.BlockSpec((block, width), lambda i: (i, 0))] + [weight] * 4,
        out_specs=[out] * 3,
        out_shape=[jax.ShapeDtypeStruct((tokens, units), LOW)] * 3,
        compiler_params=pltpu.CompilerParams(vmem_limit_bytes=VMEM_BYTES),
        cost_estimate=cost(
            4 * tokens * width * units, tokens * width + 2 * width * units, 3 * tokens * units
        ),
    )(normed, *weights)


def down_kernel(h0, h1, *refs):
    weights, outs = refs[:8], refs[8:]
    half = weights[0].shape[1]
    for at, out_ref in enumerate(outs):

        @pl.when(pl.program_id(0) == at)
        def _(out_ref=out_ref):
            for side in range(2):
                total = mm(h0[...], both(weights[2 * side : 2 * side + 2], 0))
                total = total + mm(h1[...], both(weights[4 + 2 * side : 6 + 2 * side], 0))
                out_ref[:, side * half : (side + 1) * half] = total.astype(LOW)


def down_units(hidden, down):
    tokens, units = hidden[0].shape
    weights = flat(*down[0], *down[1])
    half = weights[0].shape[1]
    block = WIDE_BLOCK
    weight = one_buffer(weights[0].shape, lambda i: (0, 0))
    left = pl.BlockSpec((block, units), lambda i: (i, 0))
    return pl.pallas_call(
        down_kernel,
        grid=(tokens // block,),
        in_specs=[left] * 2 + [weight] * 8,
        out_specs=[one_buffer((block, 2 * half), lambda i: (0, 0))] * (tokens // block),
        out_shape=[jax.ShapeDtypeStruct((block, 2 * half), LOW)] * (tokens // block),
        compiler_params=pltpu.CompilerParams(vmem_limit_bytes=VMEM_BYTES),
        cost_estimate=cost(
            8 * tokens * units * half, 2 * tokens * units + 4 * units * half, 2 * tokens * half
        ),
    )(*hidden, *weights)


def hidden_back_kernel(grad_ref, d0, d1, d2, d3, gate_ref, up_ref, grad_gate_ref, grad_up_ref):
    half = d0.shape[1]
    part = dot_nt(grad_ref[:, :half], both((d0, d1), 0))
    part = part + dot_nt(grad_ref[:, half:], both((d2, d3), 0))
    gate = gate_ref[...].astype(WIDE)
    up = up_ref[...].astype(WIDE)
    sigmoid = jax.nn.sigmoid(gate)
    grad_gate_ref[...] = (part * up * sigmoid * (1.0 + gate * (1.0 - sigmoid))).astype(LOW)
    grad_up_ref[...] = (part * (gate * sigmoid)).astype(LOW)


def hidden_back(grads, down, gate, up):
    tokens, width = grads.shape
    weights = flat(*down)
    units = 2 * weights[0].shape[0]
    block = WIDE_BLOCK
    weight = one_buffer(weights[0].shape, lambda i: (0, 0))
    row = pl.BlockSpec((block, units), lambda i: (i, 0))
    return pl.pallas_call(
        hidden_back_kernel,
        grid=(tokens // block,),
        in_specs=[pl.BlockSpec((block, width), lambda i: (i, 0))] + [weight] * 4 + [row] * 2,
        out_specs=[row] * 2,
        out_shape=[jax.ShapeDtypeStruct((tokens, units), LOW)] * 2,
        compiler_params=pltpu.CompilerParams(vmem_limit_bytes=VMEM_BYTES),
        cost_estimate=cost(
            2 * tokens * width * units,
            tokens * width + width * units + 2 * tokens * units,
            2 * tokens * units,
        ),
    )(grads, *weights, gate, up)


def normed_back_kernel(a0, a1, b0, b1, *refs):
    weights, outs = refs[:8], refs[8:]
    half = weights[0].shape[1]
    for at, out_ref in enumerate(outs):

        @pl.when(pl.program_id(0) == at)
        def _(out_ref=out_ref):
            for side in range(2):
                total = jnp.zeros((a0.shape[0], half), WIDE)
                for which, lefts in enumerate(((a0, b0), (a1, b1))):
                    start = 4 * which + 2 * side
                    for kind, left in enumerate(lefts):
                        right = both_of(weights[start : start + 2], kind, 1)
                        total = total + dot_nt(left[...], right)
                out_ref[:, side * half : (side + 1) * half] = total.astype(LOW)


def normed_back(grad_gate, grad_up, pairs):
    tokens, units = grad_gate[0].shape
    weights = flat(*pairs[0], *pairs[1])
    half = weights[0].shape[1]
    block = WIDE_BLOCK
    weight = one_buffer(weights[0].shape, lambda i: (0, 0, 0))
    left = pl.BlockSpec((block, units), lambda i: (i, 0))
    return pl.pallas_call(
        normed_back_kernel,
        grid=(tokens // block,),
        in_specs=[left] * 4 + [weight] * 8,
        out_specs=[one_buffer((block, 2 * half), lambda i: (0, 0))] * (tokens // block),
        out_shape=[jax.ShapeDtypeStruct((block, 2 * half), LOW)] * (tokens // block),
        compiler_params=pltpu.CompilerParams(vmem_limit_bytes=VMEM_BYTES),
        cost_estimate=cost(
            16 * tokens * units * half, 4 * tokens * units + 8 * units * half, 2 * tokens * half
        ),
    )(*grad_gate, *grad_up, *weights)


def weight_grad(lefts, place, rights, columns):
    count, tokens, parts = len(rights), lefts[0].shape[0], len(lefts)
    span = rights[0][0].shape[1]
    block = WIDE_BLOCK

    def kernel(*refs):
        left_refs, out_ref = refs[:parts], refs[-1]
        for at in range(count):
            right_refs = refs[parts * (at + 1) : parts * (at + 2)]
            total = dot_tn(left_refs[0][...], right_refs[0][...])
            for left_ref, right_ref in zip(left_refs[1:], right_refs[1:]):
                total = total + dot_tn(left_ref[...], right_ref[...])
            out_ref[:, at * span : (at + 1) * span] = total.astype(LOW)

    start = place * columns // block
    return pl.pallas_call(
        kernel,
        grid=(columns // block,),
        in_specs=[pl.BlockSpec((tokens, block), lambda i: (0, i + start))] * parts
        + [one_buffer((tokens, span), lambda i: (0, 0))] * (count * parts),
        out_specs=pl.BlockSpec((block, count * span), lambda i: (i, 0)),
        out_shape=jax.ShapeDtypeStruct((columns, count * span), LOW),
        compiler_params=pltpu.CompilerParams(vmem_limit_bytes=VMEM_BYTES),
        cost_estimate=cost(
            2 * count * parts * tokens * columns * span,
            parts * tokens * (columns + count * span),
            count * columns * span,
        ),
    )(*lefts, *[value for right in rights for value in right])


def project_kernel(
    normed_ref, own_ref, kv_ref, first_ref, second_ref, kv_other_ref, cosine_ref, sine_ref, out_ref
):
    half = own_ref.shape[1]
    near_rows = jnp.concatenate([own_ref[0], kv_ref[0]], axis=1)
    other_rows = jnp.concatenate([first_ref[0], second_ref[0], kv_other_ref[0]], axis=1)
    product = mm(normed_ref[0, :, :half], near_rows) + mm(normed_ref[0, :, half:], other_rows)
    cosine = cosine_ref[0]
    sine = sine_ref[0]
    for tile in range(3):
        part = product[:, tile * LANES : (tile + 1) * LANES]
        turned = part * cosine + partner_lanes(part) * sine
        if tile < 2:
            turned = turned * ATTN_SCALE
        else:
            turned = jnp.where(first_lanes(part.shape), turned, part)
        out_ref[0, 0, :, tile * LANES : (tile + 1) * LANES] = turned.astype(LOW)


def piece_specs(pieces):
    return [pl.BlockSpec((1,) + piece.shape[1:], lambda j, i: (j, 0, 0)) for piece in pieces]


def project(normed, pieces, cosine, sine):
    groups = 4
    wide = 3 * LANES
    table = pl.BlockSpec((1, CHUNK, LANES), lambda j, i: (0, 0, 0))
    return pl.pallas_call(
        project_kernel,
        grid=(groups, 2),
        in_specs=[pl.BlockSpec((1, CHUNK, MODEL_WIDTH), lambda j, i: (i, 0, 0))]
        + piece_specs(pieces)
        + [table, table],
        out_specs=pl.BlockSpec((1, 1, CHUNK, wide), lambda j, i: (j, i, 0, 0)),
        out_shape=jax.ShapeDtypeStruct((groups, 2, CHUNK, wide), LOW),
        compiler_params=pltpu.CompilerParams(vmem_limit_bytes=VMEM_BYTES),
        cost_estimate=cost(
            2 * CHUNK * MODEL_WIDTH * groups * wide, MODEL_WIDTH * (CHUNK + groups * wide), 0
        ),
    )(normed, *pieces, cosine, sine)


def project_back_kernel(
    grad_ref, own_ref, kv_ref, first_ref, second_ref, kv_other_ref, out_ref, acc
):
    group, tokens = pl.program_id(0), pl.program_id(1)
    half = own_ref.shape[1]

    @pl.when(group == 0)
    def _():
        acc[tokens] = jnp.zeros(acc.shape[1:], WIDE)

    near_rows = jnp.concatenate([own_ref[0], kv_ref[0]], axis=1)
    other_rows = jnp.concatenate([first_ref[0], second_ref[0], kv_other_ref[0]], axis=1)
    acc[tokens, :, :half] += dot_nt(grad_ref[0], near_rows)
    acc[tokens, :, half:] += dot_nt(grad_ref[0], other_rows)

    @pl.when(group == pl.num_programs(0) - 1)
    def _():
        out_ref[tokens] = acc[tokens].astype(LOW)


def project_back(grads, pieces):
    groups = 4
    wide = 3 * LANES
    return pl.pallas_call(
        project_back_kernel,
        grid=(groups, 2),
        in_specs=[pl.BlockSpec((1, CHUNK, wide), lambda j, i: (i, 0, j))] + piece_specs(pieces),
        out_specs=pl.BlockSpec((2, CHUNK, MODEL_WIDTH), lambda j, i: (0, 0, 0)),
        out_shape=jax.ShapeDtypeStruct((2, CHUNK, MODEL_WIDTH), LOW),
        scratch_shapes=[pltpu.VMEM((2, CHUNK, MODEL_WIDTH), WIDE)],
        compiler_params=pltpu.CompilerParams(vmem_limit_bytes=VMEM_BYTES),
        cost_estimate=cost(
            2 * CHUNK * MODEL_WIDTH * groups * wide, MODEL_WIDTH * (CHUNK + groups * wide), 0
        ),
    )(grads, *pieces)


def split_heads(tiles, lanes_from):
    heads = []
    for head in range(4):
        tile = tiles[:, (head // 2) * LANES : (head // 2 + 1) * LANES].astype(WIDE)
        if (head % 2) * HEAD_SIZE != lanes_from:
            tile = pltpu.roll(tile, HEAD_SIZE, 1)
        low = first_lanes(tile.shape)
        heads.append(jnp.where(low if lanes_from == 0 else ~low, tile, 0.0).astype(LOW))
    return heads


def join_heads(heads, lanes_from):
    tiles = []
    for pair in range(2):
        even, odd = heads[2 * pair], heads[2 * pair + 1]
        if lanes_from == 0:
            odd = pltpu.roll(odd, HEAD_SIZE, 1)
        else:
            even = pltpu.roll(even, HEAD_SIZE, 1)
        tiles.append(jnp.where(first_lanes(even.shape), even, odd))
    return tiles


def visible_chunks(chunk, prefix):
    whole = jnp.maximum(chunk, prefix // CHUNK)
    some = jnp.maximum(chunk + 1, (prefix + CHUNK - 1) // CHUNK)
    return whole, some


def attend_kernel(place_ref, q_ref, kv_ref, *rest):
    o_ref, lse_ref, heads, top, total, acc = rest[-6:]
    place = place_ref[0]
    prefix = place_ref[1 + pl.program_id(0)]
    chunk = pl.program_id(1) ^ place
    for head, tile in enumerate(split_heads(q_ref[0, 0], 0)):
        heads[head] = tile
        top[head] = jnp.full((CHUNK, LANES), MASKED, WIDE)
        total[head] = jnp.zeros((CHUNK, LANES), WIDE)
        acc[head] = jnp.zeros((CHUNK, LANES), WIDE)

    def step(masked, other, carry):
        kv = kv_ref[other ^ place, 0]
        if masked:
            row = lax.broadcasted_iota(jnp.int32, (CHUNK, CHUNK), 0) + chunk * CHUNK
            key = lax.broadcasted_iota(jnp.int32, (CHUNK, CHUNK), 1) + other * CHUNK
            visible = key <= jnp.maximum(row, prefix - 1)
        for head in range(4):
            scores = dot_nt(heads[head], kv)
            if masked:
                scores = jnp.where(visible, scores, MASKED)
            old = top[head]
            new = jnp.maximum(old, jnp.max(scores, axis=1, keepdims=True))
            exponent = jnp.exp(scores - new[:, :1])
            shrink = jnp.exp(old - new)
            top[head] = new
            total[head] = total[head] * shrink + jnp.sum(exponent, axis=1, keepdims=True)
            acc[head] = acc[head] * shrink + jnp.dot(
                exponent.astype(LOW), kv, preferred_element_type=WIDE
            )
        return carry

    whole, some = visible_chunks(chunk, prefix)
    lax.fori_loop(0, whole, functools.partial(step, False), 0)
    lax.fori_loop(whole, some, functools.partial(step, True), 0)
    lane = lax.broadcasted_iota(jnp.int32, (CHUNK, LANES), 1)
    logs = jnp.zeros((CHUNK, LANES), WIDE)
    results = []
    for head in range(4):
        results.append(acc[head] / total[head])
        logs = jnp.where(lane == head, top[head] + jnp.log(total[head]), logs)
    lse_ref[0, 0] = jnp.transpose(logs)[:8]
    for pair, tile in enumerate(join_heads(results, HEAD_SIZE)):
        o_ref[0, 0, :, pair * LANES : (pair + 1) * LANES] = tile.astype(LOW)


def attend(spot, packed, holds=()):
    units = 2 * 4 * 10
    return pl.pallas_call(
        attend_kernel,
        grid_spec=pltpu.PrefetchScalarGridSpec(
            num_scalar_prefetch=1,
            grid=(2, 4),
            in_specs=[
                pl.BlockSpec((1, 1, CHUNK, 2 * LANES), lambda i, j, *_: (j, i, 0, 0)),
                pl.BlockSpec((4, 1, CHUNK, LANES), lambda i, j, *_: (0, i, 0, 2)),
            ]
            + [pl.BlockSpec(memory_space=pl.ANY)] * len(holds),
            out_specs=[
                pl.BlockSpec((1, 1, CHUNK, 2 * LANES), lambda i, j, *_: (j, i, 0, 0)),
                pl.BlockSpec((1, 1, 8, CHUNK), lambda i, j, *_: (j, i, 0, 0)),
            ],
            scratch_shapes=[
                pltpu.VMEM((4, CHUNK, LANES), LOW),
                pltpu.VMEM((4, CHUNK, LANES), WIDE),
                pltpu.VMEM((4, CHUNK, LANES), WIDE),
                pltpu.VMEM((4, CHUNK, LANES), WIDE),
            ],
        ),
        out_shape=[
            jax.ShapeDtypeStruct((4, 2, CHUNK, 2 * LANES), LOW),
            jax.ShapeDtypeStruct((4, 2, 8, CHUNK), WIDE),
        ],
        compiler_params=pltpu.CompilerParams(vmem_limit_bytes=VMEM_BYTES),
        cost_estimate=pl.CostEstimate(
            flops=int(units * 4 * CHUNK * CHUNK * 256 * 2 * 2 * COST_SHARE),
            bytes_accessed=1024 * 1024,
            transcendentals=0,
        ),
    )(spot, packed, packed, *holds)


def attend_back_kernel(
    sequence, place_ref, q_ref, kv_ref, o_ref, do_ref, lse_ref, cosine_ref, sine_ref, *rest
):
    out_ref, heads, grads, deltas, q_acc, kv_acc = rest[-6:]
    slot = pl.program_id(0)
    place = place_ref[0]
    prefix = place_ref[1 + sequence]
    chunk = slot ^ place

    @pl.when(slot == 0)
    def _():
        kv_acc[...] = jnp.zeros_like(kv_acc)

    ones = jnp.ones((8, LANES), WIDE)
    out_heads = split_heads(o_ref[0, 0], HEAD_SIZE)
    grad_heads = split_heads(do_ref[0, 0], HEAD_SIZE)
    for head, tile in enumerate(split_heads(q_ref[0, 0], 0)):
        heads[head] = tile
        grads[head] = grad_heads[head]
        product = out_heads[head].astype(WIDE) * grad_heads[head].astype(WIDE)
        deltas[head] = lax.dot_general(
            ones,
            product,
            (((1,), (1,)), ((), ())),
            precision=lax.Precision.HIGHEST,
            preferred_element_type=WIDE,
        )
        q_acc[head] = jnp.zeros((CHUNK, LANES), WIDE)

    def step(masked, other, carry):
        other_slot = other ^ place
        kv = kv_ref[other_slot, 0]
        if masked:
            key = lax.broadcasted_iota(jnp.int32, (CHUNK, CHUNK), 0) + other * CHUNK
            row = lax.broadcasted_iota(jnp.int32, (CHUNK, CHUNK), 1) + chunk * CHUNK
            visible = key <= jnp.maximum(row, prefix - 1)
        for head in range(4):
            scores = dot_nt(kv, heads[head])
            if masked:
                scores = jnp.where(visible, scores, MASKED)
            probability = jnp.exp(scores - lse_ref[0, 0, head : head + 1])
            grad_prob = dot_nt(kv, grads[head])
            grad_scores = (probability * (grad_prob - deltas[head][:1])).astype(LOW)
            kv_acc[other_slot] += jnp.dot(
                grad_scores, heads[head], preferred_element_type=WIDE
            ) + jnp.dot(probability.astype(LOW), grads[head], preferred_element_type=WIDE)
            q_acc[head] += dot_tn(grad_scores, kv)
        return carry

    whole, some = visible_chunks(chunk, prefix)
    lax.fori_loop(0, whole, functools.partial(step, False), 0)
    lax.fori_loop(whole, some, functools.partial(step, True), 0)
    cosine = cosine_ref[slot]
    sine = sine_ref[slot]
    for pair, tile in enumerate(join_heads([q_acc[head] for head in range(4)], 0)):
        tile = tile * ATTN_SCALE
        turned = tile * cosine + partner_lanes(tile * sine)
        out_ref[slot, :, pair * LANES : (pair + 1) * LANES] = turned.astype(LOW)

    @pl.when(slot == 3)
    def _():
        for other in range(4):
            tile = kv_acc[other]
            turned = tile * cosine_ref[other] + partner_lanes(tile * sine_ref[other])
            turned = jnp.where(first_lanes(tile.shape), turned, tile)
            out_ref[other, :, 2 * LANES :] = turned.astype(LOW)


def attend_grad(sequence, spot, packed, attended, grad_attended, logsum, cosine, sine, holds=()):
    units = 4 * 10
    tile = pl.BlockSpec((1, 1, CHUNK, 2 * LANES), lambda j, *_: (j, sequence, 0, 0))
    table = pl.BlockSpec((4, CHUNK, LANES), lambda j, *_: (0, 0, 0))
    return pl.pallas_call(
        functools.partial(attend_back_kernel, sequence),
        grid_spec=pltpu.PrefetchScalarGridSpec(
            num_scalar_prefetch=1,
            grid=(4,),
            in_specs=[
                tile,
                pl.BlockSpec((4, 1, CHUNK, LANES), lambda j, *_: (0, sequence, 0, 2)),
                tile,
                tile,
                pl.BlockSpec((1, 1, 8, CHUNK), lambda j, *_: (j, sequence, 0, 0)),
                table,
                table,
            ]
            + [pl.BlockSpec(memory_space=pl.ANY)] * len(holds),
            out_specs=pl.BlockSpec((4, CHUNK, 3 * LANES), lambda j, *_: (0, 0, 0)),
            scratch_shapes=[
                pltpu.VMEM((4, CHUNK, LANES), LOW),
                pltpu.VMEM((4, CHUNK, LANES), LOW),
                pltpu.VMEM((4, 8, CHUNK), WIDE),
                pltpu.VMEM((4, CHUNK, LANES), WIDE),
                pltpu.VMEM((4, CHUNK, LANES), WIDE),
            ],
        ),
        out_shape=jax.ShapeDtypeStruct((4, CHUNK, 3 * LANES), LOW),
        compiler_params=pltpu.CompilerParams(vmem_limit_bytes=VMEM_BYTES),
        cost_estimate=pl.CostEstimate(
            flops=int(units * 4 * CHUNK * CHUNK * 256 * 2 * 5 * COST_SHARE),
            bytes_accessed=1024 * 1024,
            transcendentals=0,
        ),
    )(spot, packed, packed, attended, grad_attended, logsum, cosine, sine, *holds)


def dp_spot(dp):
    return dp.reshape(1)


def step_kernel(spot_ref, factor_ref, grad_ref, weight_ref, moment_ref, square_ref, *outs):
    gradient = grad_ref[0].astype(WIDE) * factor_ref[0, 0]
    following, variance = adam(
        weight_ref[...], gradient, moment_ref[...], square_ref[...], DECAY, LEARN
    )
    outs[0][...] = gradient
    outs[1][...] = following
    outs[2][...] = variance


def step_weight(spot, factor, pieces, axis, weight, moment, square):
    count, rows, columns = pieces.shape
    block_rows = min(rows, (1 << 19) // columns)
    parts = rows // block_rows

    def piece_at(block, part, spot_ref):
        code = spot_ref[0]
        return (block ^ ((code % 2) * 2 + code // 2), part, 0)

    def weight_at(block, part, spot_ref):
        return (part, block) if axis == 1 else (block * parts + part, 0)

    spec = pl.BlockSpec((block_rows, columns), weight_at)
    return pl.pallas_call(
        step_kernel,
        grid_spec=pltpu.PrefetchScalarGridSpec(
            num_scalar_prefetch=1,
            grid=(count, parts),
            in_specs=[
                pl.BlockSpec(memory_space=pltpu.SMEM),
                pl.BlockSpec((1, block_rows, columns), piece_at),
                spec,
                spec,
                spec,
            ],
            out_specs=[spec] * 3,
        ),
        out_shape=[jax.ShapeDtypeStruct(weight.shape, WIDE)] * 3,
        compiler_params=pltpu.CompilerParams(vmem_limit_bytes=VMEM_BYTES),
        cost_estimate=pl.CostEstimate(
            flops=12 * weight.size, bytes_accessed=26 * weight.size, transcendentals=weight.size
        ),
    )(spot, factor, pieces, weight, moment, square)


def step_pair_kernel(spot_ref, factor_ref, grad_ref, *refs):
    core, start = spot_ref[0], spot_ref[1]
    factor = factor_ref[0, 0]
    for group in range(4):
        turned = group ^ start
        slot = turned // 2 + (turned % 2) * 2
        first = grad_ref[core * 4 + slot].astype(WIDE) * factor
        second = grad_ref[(1 - core) * 4 + slot].astype(WIDE) * factor
        low = first_lanes(first.shape)
        lanes = pl.ds(group * LANES, LANES)
        key_grad = jnp.where(low, first, pltpu.roll(second, HEAD_SIZE, 1))
        value_grad = jnp.where(low, pltpu.roll(first, HEAD_SIZE, 1), second)
        for gradient, at in ((key_grad, 0), (value_grad, 1)):
            weight_ref, moment_ref, square_ref = refs[3 * at : 3 * at + 3]
            following, variance = adam(
                weight_ref[:, lanes],
                gradient,
                moment_ref[:, lanes],
                square_ref[:, lanes],
                DECAY,
                LEARN,
            )
            outs = refs[6 + 3 * at : 9 + 3 * at]
            outs[0][:, lanes] = gradient
            outs[1][:, lanes] = following
            outs[2][:, lanes] = variance


def step_pair(spot, factor, pieces, key, value):
    rows, columns = key[0].shape
    block_rows = 128
    spec = pl.BlockSpec((block_rows, columns), lambda i, *_: (i, 0))
    outs = pl.pallas_call(
        step_pair_kernel,
        grid_spec=pltpu.PrefetchScalarGridSpec(
            num_scalar_prefetch=1,
            grid=(rows // block_rows,),
            in_specs=[
                pl.BlockSpec(memory_space=pltpu.SMEM),
                pl.BlockSpec((8, block_rows, LANES), lambda i, *_: (0, i, 0)),
            ]
            + [spec] * 6,
            out_specs=[spec] * 6,
        ),
        out_shape=[jax.ShapeDtypeStruct((rows, columns), WIDE)] * 6,
        compiler_params=pltpu.CompilerParams(vmem_limit_bytes=VMEM_BYTES),
        cost_estimate=pl.CostEstimate(
            flops=24 * rows * columns,
            bytes_accessed=52 * rows * columns,
            transcendentals=2 * rows * columns,
        ),
    )(spot, factor, pieces, *key, *value)
    return outs[:3], outs[3:]


def slot_tables(place):
    half = HEAD_SIZE // 2
    frequency = THETA ** (-(jnp.arange(half, dtype=WIDE) * 2.0 / HEAD_SIZE))
    chunk = jnp.arange(4, dtype=jnp.int32) ^ place
    position = (chunk[:, None] * CHUNK + jnp.arange(CHUNK)[None, :]).astype(WIDE)
    angles = position[:, :, None] * frequency[None, None, :]
    cosine, sine = jnp.cos(angles), jnp.sin(angles)
    return (
        jnp.concatenate([cosine] * 4, axis=2),
        jnp.concatenate([-sine, sine, -sine, sine], axis=2),
    )


def exchange(pieces):
    return [
        pieces[0],
        swap_x(pieces[1]),
        swap_near(pieces[2]),
        swap_corner(pieces[3]),
    ]


def rows_norm(values):
    factor = lax.rsqrt(
        jnp.sum(values * values, axis=1, keepdims=True) / MODEL_WIDTH + EPS_NORM
    )
    return values * factor, factor


def rows_norm_back(gradient, normed, factor, gain_row):
    weighted = gradient * gain_row
    inner = jnp.sum(weighted * normed, axis=1, keepdims=True) / MODEL_WIDTH
    return factor * (weighted - normed * inner), jnp.sum(gradient * normed, axis=0)


def swapped_shards(
    tokens,
    cotangent,
    prefix,
    query_weight,
    key_projection,
    value_projection,
    out_weight,
    gate_weight,
    up_weight,
    down_weight,
    norm_gains,
    query_moment,
    key_first_moment,
    value_first_moment,
    out_moment,
    gate_moment,
    up_moment,
    down_moment,
    gains_moment,
    query_square,
    key_second_moment,
    value_second_moment,
    out_square,
    gate_square,
    up_square,
    down_square,
    gains_square,
):
    row = lax.axis_index("row")
    col = lax.axis_index("col")
    dp = lax.axis_index("dp")
    core = dp % 2
    side = dp // 2
    near = col % 2
    far = col // 2
    place = near * 2 + row
    half_rows = tokens.shape[0] // 2
    half_width = tokens.shape[1]

    swapped = [1, 0, 3, 2]
    wide = 3 * LANES
    owner = [col ^ (2 * row), col ^ (2 - 2 * row), col ^ (1 + 2 * row), col ^ (3 - 2 * row)]

    def reorder(blocks):
        return jnp.stack([blocks[place_at] for place_at in swapped])

    def ordered_halves(matrix, axis):
        start = core * 2 * LANES
        return jnp.concatenate(
            [
                cut(matrix, start + side * LANES, LANES, axis),
                cut(matrix, start + (1 - side) * LANES, LANES, axis),
            ],
            axis=axis,
        ).astype(LOW)

    def halves_of(values):
        own = cut(values, row * half_rows, half_rows, 0)
        return own, cut(values, (1 - row) * half_rows, half_rows, 0)

    def leave(values, others):
        back = after(swap_x(after(values[:, half_width:], others[0])), others[1])
        return in_order(row, values[:, :half_width], back, 0)

    def add_low(kept, got):
        return (kept.astype(WIDE) + got.astype(WIDE)).astype(LOW)

    own_rows, other_rows = halves_of(tokens)
    got_rows = swap_x(other_rows)
    gains = jnp.concatenate([norm_gains, swap_x(norm_gains)], axis=1)
    prefixes = [prefix[far], swap_core(prefix)[far]]
    spot = jnp.stack([place, *prefixes])
    cosine, sine = slot_tables(place)

    def heads_of(matrix):
        return jnp.stack(
            [cut(matrix, (at * 2 + core) * HEAD_SIZE, HEAD_SIZE, 1) for at in owner]
        ).astype(LOW)

    kv_own = jnp.concatenate([heads_of(key_projection), heads_of(value_projection)], axis=2)
    kv_other = swap_x(reorder(kv_own))

    def far_pair(block, other):
        return jnp.stack([jnp.where(row == 0, block, other), jnp.where(row == 0, other, block)])

    units = gate_weight.shape[1] // 2

    def hidden_low(matrix, axis, which):
        start = core * units + (side if which == 0 else 1 - side) * (units // 2)
        return cut(matrix, start, units // 2, axis).astype(LOW)

    pair_own = [
        jnp.stack([hidden_low(gate_weight, 1, which), hidden_low(up_weight, 1, which)])
        for which in range(2)
    ]
    down_own = [hidden_low(down_weight, 0, which) for which in range(2)]
    q_low, o_low = ordered_halves(query_weight, 1), ordered_halves(out_weight, 0)

    q_far = swap_far(q_low)
    q_pair = after(far_pair(q_low, q_far), kv_other)
    q_near = swap_near(q_pair)
    q_pair_x = swap_x(jnp.stack([q_pair[1, :, :LANES], q_pair[0, :, :LANES]]))
    q_near_x = swap_near(after(q_pair_x, q_near))
    q_pair_y = swap_y(q_pair_x)
    pair_x = swap_x(after(pair_own[0], q_pair_x))
    q_near_y = swap_y(after(q_near_x, q_pair_y))
    o_far = swap_far(after(o_low, q_near_x))
    pair_far = swap_far(after(pair_own[0], o_far))
    o_pair = far_pair(o_low, o_far)
    o_near = swap_near(o_pair)

    in_pieces = (
        jnp.concatenate([q_pair, q_near]),
        kv_own,
        jnp.concatenate([q_pair_x, q_near_x]),
        jnp.concatenate([q_pair_y, q_near_y]),
        kv_other,
    )

    def exchange(pieces):
        return [
            pieces[0],
            swap_x(pieces[1]),
            swap_near(pieces[2]),
            swap_corner(pieces[3]),
        ]

    def tokens_of(pieces):
        return jnp.concatenate(exchange([pieces[slot] for slot in range(4)]), axis=1)

    def slots_of(values):
        size = values.shape[1] // 4
        return jnp.stack(exchange([values[:, at * size : (at + 1) * size] for at in range(4)]))

    x = jnp.concatenate([own_rows, after(got_rows, q_pair_x)], axis=1).astype(WIDE)
    normed_one, factor_one = rows_norm(x)
    h_own = (normed_one * gains[0]).astype(LOW)
    h_one = [h_own, swap_core(h_own)]
    h_pair = jnp.stack(h_one)
    projected = project(h_pair, in_pieces, cosine, sine)
    pair_x_y = swap_y(after(pair_x, projected))
    packed = jnp.stack(exchange([projected[slot] for slot in range(4)]))
    packed = after(packed, pair_far, pair_x_y, o_near)
    pair_far_x = swap_x(after(pair_far, packed))
    pair_far_y = swap_y(after(pair_far, packed))
    o_own = jnp.concatenate([o_pair, o_near])
    o_first = swap_x(after(reorder(o_own[:, :LANES]), packed))
    down_far = swap_far(after(down_own[0], packed))
    attended, logsum = attend(spot, packed)
    attended = after(attended, pair_far_x, pair_far_y, o_first, down_far)
    o_second = swap_y(after(o_first, attended))
    o_back = jnp.concatenate(exchange([attended[slot] for slot in range(4)]), axis=2)
    pair_far_xy = swap_y(after(pair_far_x, o_second))
    o_tokens = [o_back[0], o_back[1]]
    out_weights = jnp.concatenate(
        [o_own, jnp.concatenate([o_first, o_second], axis=1)], axis=2
    ).reshape(4 * 2 * LANES, MODEL_WIDTH)
    out_part = matrix_multiply(o_back.reshape(2 * CHUNK, 4 * 2 * LANES), out_weights)
    residual = x + RESID * fold(out_part[:CHUNK], out_part[CHUNK:], swap_core)
    pairs = (
        ((pair_own[0], pair_far), (pair_x, pair_far_x)),
        ((pair_own[1], pair_far_y), (pair_x_y, pair_far_xy)),
    )

    own_grad, other_grad = halves_of(cotangent)
    got_grad = swap_x(after(other_grad, o_back))
    def columns(values, order, size):
        return jnp.concatenate([values[:, at * size : (at + 1) * size] for at in order], axis=1)

    def rows(values, order, size):
        return jnp.concatenate([values[at * size : (at + 1) * size] for at in order])

    def beyond_of(parts):
        return add_low(parts[0], swap_core(parts[1]))

    def sum_four(parts):
        beyond = swap_near(parts[1])

        def finish(*others):
            own = parts[0][0].astype(WIDE) + swap_core(parts[0][1]).astype(WIDE)
            return own + after(beyond, *others).astype(WIDE)

        return finish

    normed_two, factor_two = rows_norm(residual)
    h_own = (normed_two * gains[1]).astype(LOW)
    h_near = swap_near(h_own)
    h_two = [jnp.concatenate([h_own, swap_core(h_own)]), None]
    down_pair = jnp.stack([down_own[0], down_far])
    down_pair_x = swap_x(after(down_pair, o_back))
    down_far_y = swap_y(after(down_far, pair_far_xy))
    down_pair_xy = swap_y(after(down_pair_x, down_far_y))
    down = (
        ((down_own[0], down_far), (down_pair_x[0], down_pair_x[1])),
        ((down_own[1], down_far_y), (down_pair_xy[0], down_pair_xy[1])),
    )

    hidden, gate_values, up_values = [[], []], [[], []], [[], []]
    for half in range(2):
        if half == 1:
            h_near, got_grad = after(h_near, hidden[0][0]), after(got_grad, hidden[0][0])
            grad_output = jnp.concatenate([own_grad, got_grad], axis=1).astype(WIDE)
            grad_own = (RESID * grad_output).astype(LOW)
            grad_near = swap_near(after(grad_own, h_near))
            h_two[1] = jnp.concatenate([h_near, swap_core(h_near)])
        for which in range(2):
            one, two, three = hidden_units(h_two[half], pairs[which])
            hidden[which].append(one)
            gate_values[which].append(two)
            up_values[which].append(three)

    grad_near = after(grad_near, hidden[0][1])
    grad_mlp = [
        jnp.concatenate([grad_own, swap_core(grad_own)]),
        jnp.concatenate([grad_near, swap_core(grad_near)]),
    ]
    down_sent, down_kept = [
        weight_grad(hidden[which], 0, [grad_mlp], units) for which in (1, 0)
    ]
    part_rows = units // 2
    down_y = swap_y(down_sent[:part_rows])
    down_x = swap_x(
        jnp.concatenate([down_kept[part_rows:, half_width:], down_sent[part_rows:, half_width:]])
    )
    down_first = down_kept[:part_rows]
    down_second = jnp.concatenate(
        [down_kept[part_rows:, :half_width], down_sent[part_rows:, :half_width]]
    )
    down_pair_xy = after(down_pair_xy, down_kept)
    down = (
        ((down_own[0], down_far), (down_pair_x[0], down_pair_x[1])),
        ((down_own[1], down_far_y), (down_pair_xy[0], down_pair_xy[1])),
    )


    grad_gate, grad_up = [[None, None], [None, None]], [[None, None], [None, None]]
    for half in (1, 0):
        grads_here = after(grad_mlp[half], down_sent, down_kept)
        for which in range(2):
            grad_gate[which][half], grad_up[which][half] = hidden_back(
                grads_here, down[which], gate_values[which][half], up_values[which][half]
            )
    up_sent = weight_grad(h_two, 1, grad_up, half_width)
    gate_sent = weight_grad(h_two, 0, grad_gate[1:], MODEL_WIDTH)
    h_two_parts = [None, None]

    def back_of(half, *others):
        grads = [[after(kind[which][half], *others) for which in range(2)]
                 for kind in (grad_gate, grad_up)]
        return normed_back(*grads, pairs)

    h_two_parts[1] = back_of(1, up_sent, gate_sent)
    h_two_beyond = beyond_of(h_two_parts[1])
    down_y, down_x = after(down_y, *h_two_parts[1]), after(down_x, *h_two_parts[1])
    down_first = [
        add_low(down_first[:, at * half_width : (at + 1) * half_width],
                down_y[:, at * half_width : (at + 1) * half_width])
        for at in range(2)
    ]
    down_second = [
        add_low(down_second[at * part_rows : (at + 1) * part_rows],
                down_x[at * part_rows : (at + 1) * part_rows])
        for at in range(2)
    ]
    h_two_parts[0] = back_of(0, h_two_beyond, *down_first, *down_second)
    h_two_sum = sum_four((h_two_parts[0], h_two_beyond))
    hidden_late = [[after(value, *h_two_parts[0]) for value in values] for values in hidden]
    down_parts = [
        down_units([hidden_late[0][half], hidden_late[1][half]], down) for half in (1, 0)
    ][::-1]
    up_kept = weight_grad([after(value, *h_two_parts[0]) for value in h_two], 0, grad_up, half_width)
    up_sum_x = swap_x(up_sent)
    gate_got_y = swap_y(after(gate_sent[:, :part_rows], down_y))
    down_first_x, down_second_y = swap_x(down_first[1]), swap_y(down_second[1])

    grad_mid_part, gain_two_part = rows_norm_back(
        h_two_sum(up_kept, *down_parts[0], *down_parts[1]), normed_two, factor_two, gains[1]
    )
    grad_mid = grad_output + grad_mid_part

    grad_attended = [(RESID * grad_mid).astype(LOW)]
    gate_kept = weight_grad(
        [after(value, grad_attended[0]) for value in h_two], 0, grad_gate[:1], MODEL_WIDTH
    )
    gate_got_x = swap_x(
        jnp.concatenate([gate_kept[half_width:, part_rows:], gate_sent[half_width:, part_rows:]])
    )
    layer_sum = sum_four((down_parts[0], beyond_of(down_parts[1])))
    grad_attended.append(swap_core(grad_attended[0]))
    head_grad = right_product(jnp.concatenate(grad_attended), out_weights).astype(LOW)
    head_grad = head_grad.reshape(2, CHUNK, 4 * 2 * LANES)
    head_grad = jnp.stack(
        exchange([head_grad[:, :, at * 2 * LANES : (at + 1) * 2 * LANES] for at in range(4)])
    )
    out_local = [
        weight_grad(o_tokens, 0, [[values[:, half * half_width : (half + 1) * half_width]
                                   for values in grad_attended]], 4 * 2 * LANES)
        for half in range(2)
    ]
    out_near = swap_near(jnp.concatenate([values[4 * LANES :] for values in out_local], axis=1))
    down_first_x, down_second_y, up_sum_x = (
        after(value, gate_kept) for value in (down_first_x, down_second_y, up_sum_x)
    )
    gate_got_y, gate_got_x = after(gate_got_y, *out_local), after(gate_got_x, *out_local)
    down_part = add_low(down_first[0], down_first_x)
    down_far_sum = swap_far(add_low(down_second[0], down_second_y))
    size = up_kept.shape[1] // 2
    up_kept = [
        add_low(up_kept[:, at * size : (at + 1) * size], up_sum_x[:, at * size : (at + 1) * size])
        for at in range(2)
    ]
    gate_first = add_low(gate_kept[:half_width, :part_rows], gate_got_y[:half_width])
    gate_second = add_low(gate_kept[:half_width, part_rows:], gate_got_x[:half_width])
    gate_first_x = swap_x(add_low(gate_kept[half_width:, :part_rows], gate_got_y[half_width:]))
    gate_second_y = swap_y(add_low(gate_sent[:half_width, part_rows:], gate_got_x[half_width:]))

    def sequence_grad(sequence, *others):
        return attend_grad(
            sequence,
            spot,
            packed,
            attended,
            after(head_grad, *others),
            logsum,
            cosine,
            sine,
        )

    packed_first = sequence_grad(0, down_part, *up_kept, gate_first, gate_second)
    gate_first_x, gate_second_y, down_far_sum, out_near = (
        after(value, packed_first)
        for value in (gate_first_x, gate_second_y, down_far_sum, out_near)
    )
    gate_first = add_low(gate_first, gate_first_x)
    gate_second = add_low(gate_second, gate_second_y)
    gate_far_sum = swap_far(gate_second)
    up_sum_y = swap_y(after(up_kept[1], gate_second_y))
    in_first = tokens_of(packed_first)
    packed_second = sequence_grad(1, gate_first, gate_second)
    gate_far_sum, in_first, up_sum_y = (
        after(value, packed_second) for value in (gate_far_sum, in_first, up_sum_y)
    )
    up_part = add_low(up_kept[0], up_sum_y)
    up_far_sum = swap_far(after(up_part[:, units // 2 :], gate_far_sum))
    layer_part = (residual + RESID * layer_sum(packed_second)).astype(LOW)
    in_back = jnp.stack([in_first, tokens_of(after(packed_second, gate_far_sum, up_part))])
    down_piece = add_low(down_part, down_far_sum)
    gate_piece = add_low(gate_first, gate_far_sum)
    up_piece = add_low(up_part[:, : units // 2], up_far_sum)
    in_grads = [in_back[0], in_back[1]]
    out_kept = add_low(
        jnp.concatenate([values[: 4 * LANES] for values in out_local], axis=1), out_near
    )
    out_kept = add_low(
        out_kept[:, :half_width],
        swap_x(after(rows(out_kept[:, half_width:], [1, 0], 2 * LANES), in_back)),
    )
    in_local = [weight_grad(h_one, half, [in_grads], half_width) for half in (1, 0)][::-1]
    h_one_parts = project_back(after(in_back, up_far_sum), in_pieces)
    grad_in_part, gain_one_part = rows_norm_back(
        h_one_parts[0].astype(WIDE) + swap_core(h_one_parts[1]).astype(WIDE), normed_one, factor_one, gains[0]
    )
    input_part = (grad_mid + grad_in_part).astype(LOW)

    def spread(piece):
        pair = jnp.stack([piece, after(swap_y(piece), h_one_parts)])
        return jnp.concatenate([pair, swap_core(pair)])


    pair = 2 * LANES
    first_cut, second_cut = half_width * 3 // 8, half_width * 5 // 8

    def keep_side(values, got):
        size = values.shape[1] // wide
        kept = jnp.concatenate(
            [
                jnp.concatenate(
                    [
                        values[:, at * wide : at * wide + LANES],
                        values[:, at * wide + pair : (at + 1) * wide],
                    ],
                    axis=1,
                )
                for at in range(size)
            ],
            axis=1,
        )
        return add_low(kept, got)

    def for_side(values):
        size = values.shape[1] // wide
        return jnp.concatenate(
            [values[:, at * wide + LANES : (at + 1) * wide] for at in range(size)], axis=1
        )

    def rows_of(start, stop):
        return [values[start:stop] for values in in_local]

    def near_halves(values):
        size = values.shape[1] // 2
        return values[:, :size], values[:, size:]

    part = rows_of(0, first_cut)
    part = add_low(part[0], swap_x(columns(part[1], swapped, wide)))
    part = keep_side(part, swap_y(for_side(part)))
    kept, sent = near_halves(part)
    ways = [add_low(kept, swap_near(sent))]

    part = jnp.concatenate(rows_of(first_cut, second_cut))
    part = keep_side(part, swap_y(for_side(part)))
    kept, sent = near_halves(part)
    part = add_low(kept, swap_near(sent))
    size = second_cut - first_cut
    ways.append(add_low(part[:size], swap_x(columns(part[size:], [1, 0], pair))))

    part = jnp.concatenate(rows_of(second_cut, half_width))
    kept, sent = near_halves(part)
    part = add_low(kept, swap_near(sent))
    size = half_width - second_cut
    part = add_low(part[:size], swap_x(columns(part[size:], [1, 0], wide)))
    ways.append(keep_side(part, swap_y(for_side(part))))

    in_part = jnp.concatenate(ways)
    in_part = add_low(
        jnp.where(row == 0, in_part[:, :pair], in_part[:, pair:]),
        swap_far(jnp.where(row == 0, in_part[:, pair:], in_part[:, :pair])),
    )
    query_piece = in_part[:, :LANES]
    kv_piece = in_part[:, LANES:]

    out_part = add_low(
        jnp.where(row == 0, out_kept[:pair], out_kept[pair:]),
        swap_far(jnp.where(row == 0, out_kept[pair:], out_kept[:pair])),
    )
    out_piece = add_low(out_part[:LANES], swap_y(out_part[LANES:]))

    gain_sums = jnp.stack([gain_one_part, gain_two_part]).reshape(2, 2, 8, half_width // 8)
    gain_sums = gain_sums[:, 0] + swap_x(gain_sums[:, 1])
    for move in (swap_y, swap_core, swap_near, swap_far):
        gain_sums = gain_sums + move(gain_sums)
    gains_total = gain_sums.reshape(2, half_width)

    kv_pieces = jnp.stack([kv_piece, swap_far(kv_piece)])
    kv_pieces = jnp.concatenate([kv_pieces, swap_near(kv_pieces)])
    kv_pieces = jnp.concatenate([kv_pieces, swap_core(kv_pieces)])

    def squares_of(values):
        values = values.astype(WIDE)
        return jnp.sum(values * values)

    square_local = jnp.where(side == 0, squares_of(kv_piece), 0.0)
    square_local = square_local + jnp.where((col == 0) & (dp == 0), squares_of(gains_total), 0.0)
    for piece in (query_piece, out_piece, gate_piece, up_piece, down_piece):
        square_local = square_local + squares_of(piece)
    square_local = jnp.full((8, LANES), square_local, WIDE)
    for move in (swap_y, swap_core):
        square_local = square_local + move(square_local)
    grad_norm = jnp.sqrt(lax.psum(square_local[0, 0], ("row", "col")))
    factor = jnp.minimum(1.0, CLIP / grad_norm)
    factor_cell = factor.reshape(1, 1)
    spot = dp_spot(dp)

    def step(piece, axis, weight, moment, square):
        return step_weight(spot, factor_cell, spread(piece), axis, weight, moment, square)

    query_out = step(query_piece, 1, query_weight, query_moment, query_square)
    out_out = step(out_piece, 0, out_weight, out_moment, out_square)
    gate_out = step(gate_piece, 1, gate_weight, gate_moment, gate_square)
    up_out = step(up_piece, 1, up_weight, up_moment, up_square)
    down_out = step(down_piece, 0, down_weight, down_moment, down_square)
    layer_out = leave(layer_part, (in_part, up_out[0]))
    input_grad = leave(input_part, (in_part, up_out[0]))
    kv_spot = jnp.stack([core, col])
    key_out, value_out = step_pair(
        kv_spot,
        factor_cell,
        kv_pieces,
        (key_projection, key_first_moment, key_second_moment),
        (value_projection, value_first_moment, value_second_moment),
    )
    results = (query_out, key_out, value_out, out_out, gate_out, up_out, down_out)
    clipped, nexts, variances = zip(*results)
    gains_grad = gains_total * factor
    gains_next, gains_variance = adam(
        norm_gains, gains_grad, gains_moment, gains_square, 0.0, GAINS_LEARN
    )
    return (
        layer_out,
        input_grad,
        *clipped,
        gains_grad,
        *nexts,
        gains_next,
        *variances,
        gains_variance,
        grad_norm,
    )


def solution(mesh):
    placed = (
        P(("dp", "col"), "row"),
        P(("dp", "col"), "row"),
        P("dp"),
        P("row", "col"),
        P("row", None),
        P("row", None),
        P("col", "row"),
        P("row", "col"),
        P("row", "col"),
        P("col", "row"),
        P(None, "row"),
        P("row", "col"),
        P("row", None),
        P("row", None),
        P("col", "row"),
        P("row", "col"),
        P("row", "col"),
        P("col", "row"),
        P(None, "row"),
        P("row", "col"),
        P("row", None),
        P("row", None),
        P("col", "row"),
        P("row", "col"),
        P("row", "col"),
        P("col", "row"),
        P(None, "row"),
    )
    return jax.shard_map(
        swapped_shards if swaps_fit(mesh) else shards,
        mesh=mesh,
        in_specs=placed,
        out_specs=(
            P(("dp", "col"), "row"),
            P(("dp", "col"), "row"),
            P("row", "col"),
            P("row", None),
            P("row", None),
            P("col", "row"),
            P("row", "col"),
            P("row", "col"),
            P("col", "row"),
            P(None, "row"),
            P("row", "col"),
            P("row", None),
            P("row", None),
            P("col", "row"),
            P("row", "col"),
            P("row", "col"),
            P("col", "row"),
            P(None, "row"),
            P("row", "col"),
            P("row", None),
            P("row", None),
            P("col", "row"),
            P("row", "col"),
            P("row", "col"),
            P("col", "row"),
            P(None, "row"),
            P(),
        ),
        check_vma=False,
    )
```
